32 devices in a mesh: groups: 2 (over x), fsdp: 16 (over z, y, core).
Axes of the slice: x: 2, y: 2, z: 4, core: 2. Of those that a mesh axis runs over, the one named last changes fastest.
Arguments:
- expert_grad: float32 [8, 3, 768, 2048], P('groups', None, 'fsdp'), parts along dimension 0, may hold values from -12 to 12
- expert_momentum: float32 [8, 3, 768, 2048], P('groups', None, 'fsdp'), parts along dimension 0, may hold values from -6 to 6
- expert_master: float32 [8, 3, 768, 2048], P('groups', None, 'fsdp'), parts along dimension 0, may hold values from -6 to 6
- kv_grad: float32 [4, 512, 2048], P('groups', 'fsdp'), parts along dimension 0, may hold values from -12 to 12
- kv_momentum: float32 [4, 512, 2048], P('groups', 'fsdp'), parts along dimension 0, may hold values from -6 to 6
- kv_master: float32 [4, 512, 2048], P('groups', 'fsdp'), parts along dimension 0, may hold values from -6 to 6
Outputs:
- expert_master_new: float32 [8, 3, 768, 2048], P('groups', None, 'fsdp'), parts along dimension 0
- expert_momentum_new: float32 [8, 3, 768, 2048], P('groups', None, 'fsdp'), parts along dimension 0
- expert_weights: bfloat16 [8, 3, 768, 2048], P('groups', None, 'fsdp'), parts along dimension 0
- expert_update: bfloat16 [8, 3, 768, 2048], P('groups', None, 'fsdp'), parts along dimension 0
- kv_master_new: float32 [4, 512, 2048], P('groups', 'fsdp'), parts along dimension 0
- kv_momentum_new: float32 [4, 512, 2048], P('groups', 'fsdp'), parts along dimension 0
- kv_weights: bfloat16 [4, 512, 2048], P('groups', 'fsdp'), parts along dimension 0
- kv_update: bfloat16 [4, 512, 2048], P('groups', 'fsdp'), parts along dimension 0
The draws below stay inside these ranges and needn't reach their ends.
There are 2 independent parts, one for each index of `groups`. The reference program is written for one: setup_inputs(seed, part) draws one part's arguments, and reference() takes and returns one part's arrays. A program takes and returns all parts, laid end to end along the dimension named above; each array names one. Nothing has to cross between parts.
All inputs are finite; a program needn't handle non-finite values.
Results may differ from the reference program's by a relative error of at most 0.014.
Values may be sent and summed in bfloat16 or wider, within the bound.
No kernel may reach another device: no remote copies, remote signals or barrier semaphores. Data moves between devices by JAX's collectives and lax.ppermute only.
A program may use at most 128 MiB of HBM per device.

```python
import math
import jax
import jax.numpy as jnp
from jax import lax

D = 2048
FF = 768
KVW = 512
ITERS = 2
EXPERTS = 4


def scaled_field(key, noise_field, ramp_rate):
    layout = noise_field.shape
    leading = layout[:-2]
    row_count = layout[-2]
    col_count = layout[-1]
    row_key = jax.random.fold_in(key, 2)
    col_key = jax.random.fold_in(key, 3)
    row_scale = jnp.exp(jax.random.uniform(row_key, leading + (row_count, 1), jnp.float32, -1.15, 1.15))
    col_scale = jnp.exp(jax.random.uniform(col_key, leading + (1, col_count), jnp.float32, -1.15, 1.15))
    position = jnp.arange(row_count, dtype=jnp.float32).reshape(row_count, 1) / row_count
    values = noise_field * row_scale * col_scale * jnp.exp(ramp_rate * position)
    return jnp.clip(values, -12.0, 12.0)


def draw_expert_grad(key, part):
    key = jax.random.fold_in(key, 11)
    layout = (EXPERTS, 3, FF, D)
    noise_key = jax.random.fold_in(key, 1)
    noise_field = jax.random.normal(noise_key, layout, jnp.float32)
    return scaled_field(key, noise_field, 0.8)


def draw_kv_grad(key, part):
    key = jax.random.fold_in(key, 23)
    layout = (2, KVW, D)
    noise_key = jax.random.fold_in(key, 1)
    noise_field = jax.random.normal(noise_key, layout, jnp.float32)
    return scaled_field(key, noise_field, 0.8)


def block_scale(rng, shape, shards, least, high):
    level, own = 1.0, jax.random.fold_in(rng, 6)
    for dim, shards_of in shards:
        steps = jnp.exp(jax.random.uniform(jax.random.fold_in(own, dim), (shards_of,), jnp.float32, least / len(shards), high / len(shards)))
        level = level * jnp.repeat(steps, shape[dim] // shards_of).reshape([-1 if axis == dim else 1 for axis in range(len(shape))])
    return level


def centred(own_key, dims, width, most, split=(), kind=jnp.bfloat16):
    loudness = block_scale(own_key, dims, split, -0.22, 0.18) if split else 1.0
    drawn = jax.random.normal(own_key, dims, jnp.float32) * width * loudness
    return jnp.minimum(jnp.maximum(drawn, -most), most).astype(kind)


def setup_inputs(seed: int = 0, part: int = 0) -> dict:
    arg_keys = jax.random.split(jax.random.key(seed), 7)
    own_keys = jax.random.split(jax.random.fold_in(arg_keys[6], part), 7)
    expert_grad = draw_expert_grad(jax.random.fold_in(jax.random.fold_in(arg_keys[6], part), 71), part)
    expert_momentum = centred(own_keys[1], (EXPERTS, 3, FF, D), 1.0, 6.0, ((2, 16),), jnp.float32)
    expert_master = centred(own_keys[2], (EXPERTS, 3, FF, D), 1.0, 6.0, ((2, 16),), jnp.float32)
    kv_grad = draw_kv_grad(jax.random.fold_in(jax.random.fold_in(arg_keys[6], part), 71), part)
    kv_momentum = centred(own_keys[4], (2, KVW, D), 1.0, 6.0, ((1, 16),), jnp.float32)
    kv_master = centred(own_keys[5], (2, KVW, D), 1.0, 6.0, ((1, 16),), jnp.float32)
    return dict(expert_grad=expert_grad, expert_momentum=expert_momentum, expert_master=expert_master, kv_grad=kv_grad, kv_momentum=kv_momentum, kv_master=kv_master)


NS_A = 3.4445
NS_B = -4.775
NS_C = 2.0315
MOMENTUM = 0.95
RATE = 0.02
DECAY = 0.1
NORM_EPS = 1e-07
CLIP_EPS = 1e-06
CLIP_RATIO = 0.5
UPDATE_GAIN = 0.2

def newton_schulz(initial):
    current = initial
    for iteration in range(ITERS):
        gram_matrix = lax.dot_general(current, current, (((1,), (1,)), ((), ())), preferred_element_type=jnp.float32).astype(jnp.bfloat16)
        squared = jnp.dot(gram_matrix, gram_matrix, preferred_element_type=jnp.float32)
        polynomial = (NS_B * gram_matrix.astype(jnp.float32) + NS_C * squared).astype(jnp.bfloat16)
        current = (NS_A * current.astype(jnp.float32) + jnp.dot(polynomial, current, preferred_element_type=jnp.float32)).astype(jnp.bfloat16)
    return current

def reference(expert_grad, expert_momentum, expert_master, kv_grad, kv_momentum, kv_master):
    entry_count = expert_grad.size + kv_grad.size
    total_squares = jnp.sum(expert_grad * expert_grad) + jnp.sum(kv_grad * kv_grad)
    clip_factor = jnp.minimum(1.0, CLIP_RATIO * math.sqrt(entry_count) / (jnp.sqrt(total_squares) + CLIP_EPS))

    def one_kind(gradient, momentum, master):
        layout = gradient.shape
        clipped = clip_factor * gradient
        moment_new = MOMENTUM * momentum + clipped
        nesterov = (clipped + MOMENTUM * moment_new).reshape((-1,) + layout[-2:])
        norm_values = jnp.sqrt(lax.optimization_barrier(jnp.sum(nesterov * nesterov, axis=(1, 2), keepdims=True)))
        initial = (nesterov / (norm_values + NORM_EPS)).astype(jnp.bfloat16)
        orthogonal = lax.map(newton_schulz, initial)
        update = (UPDATE_GAIN * math.sqrt(layout[-1]) * orthogonal.astype(jnp.float32)).astype(jnp.bfloat16).reshape(layout)
        master_new = master * (1.0 - RATE * DECAY) - RATE * update.astype(jnp.float32)
        return (master_new, moment_new, master_new.astype(jnp.bfloat16), update)
    expert_out = one_kind(expert_grad, expert_momentum, expert_master)
    kv_out = one_kind(kv_grad, kv_momentum, kv_master)
    return (expert_out[0], expert_out[1], expert_out[2], expert_out[3], kv_out[0], kv_out[1], kv_out[2], kv_out[3])
```

```python
import functools
import math

import jax
import jax.numpy as jnp
import numpy as np
from jax import lax
from jax.experimental import pallas as pl
from jax.experimental.pallas import tpu as pltpu
from jax.sharding import PartitionSpec as P

NS_A = 3.4445
NS_B = -4.775
NS_C = 2.0315
MOMENTUM = 0.95
RATE = 0.02
DECAY = 0.1
NORM_EPS = 1e-07
CLIP_EPS = 1e-06
CLIP_RATIO = 0.5
UPDATE_GAIN = 0.2

F32 = jnp.float32
BF16 = jnp.bfloat16
VMEM_LIMIT = 48 * 1024 * 1024


def owner_tables(experts, kvs, devices):
    order = []
    for part in range(kvs):
        low, high = part * experts // kvs, (part + 1) * experts // kvs
        order += [("expert", index) for index in range(low, high)] + [("kv", part)]
    expert_slot, kv_slot = [0] * experts, [0] * kvs
    kind, expert_of, kv_of = [0] * devices, [0] * devices, [0] * devices
    for position, (name, index) in enumerate(order):
        slot = position * devices // len(order)
        kind[slot] = 1 if name == "expert" else 2
        (expert_slot if name == "expert" else kv_slot)[index] = slot
    last_expert = last_kv = 0
    for slot in range(devices):
        if slot in expert_slot:
            last_expert = expert_slot.index(slot)
        if slot in kv_slot:
            last_kv = kv_slot.index(slot)
        expert_of[slot], kv_of[slot] = last_expert, last_kv
    return expert_slot, kv_slot, kind, expert_of, kv_of


def squares_kernel(expert_ref, kv_ref, out_ref, total):
    step = pl.program_id(0)

    def fold(block):
        rows = block.reshape(-1, total.shape[0], block.shape[-1])
        return jnp.sum(rows * rows, axis=0)

    @pl.when(step == 0)
    def _():
        total[...] = jnp.zeros_like(total)
        for index in range(kv_ref.shape[0]):
            total[...] += fold(kv_ref[index])

    total[...] += fold(expert_ref[0].reshape(-1, expert_ref.shape[-1]))

    @pl.when(step == pl.num_programs(0) - 1)
    def _():
        out_ref[...] = jnp.full(out_ref.shape, jnp.sum(total[...]), F32)


def local_squares(expert_grad, kv_grad, devices):
    experts, three, rows, width = expert_grad.shape
    grouped = expert_grad.reshape(experts, three * rows, width)
    return pl.pallas_call(
        squares_kernel,
        grid=(experts,),
        in_specs=[
            pl.BlockSpec((1, three * rows, width), lambda i: (i, 0, 0)),
            pl.BlockSpec(kv_grad.shape, lambda i: (0, 0, 0)),
        ],
        out_specs=pl.BlockSpec((devices, 8, 128), lambda i: (0, 0, 0)),
        out_shape=jax.ShapeDtypeStruct((devices, 8, 128), F32),
        scratch_shapes=[pltpu.VMEM((math.gcd(8, 3 * rows, kv_grad.shape[1]), width), F32)],
        compiler_params=pltpu.CompilerParams(vmem_limit_bytes=VMEM_LIMIT),
        name="squares",
    )(grouped, kv_grad)


def form_kernel(entry_count, kind, expert_of, kv_of, squares, eg, em, kg, km, slots, clip):
    step = pl.program_id(0)
    total = jnp.sum(squares[...], axis=0)
    factor = jnp.minimum(
        1.0, CLIP_RATIO * math.sqrt(entry_count) / (jnp.sqrt(total) + CLIP_EPS)
    )
    clip[...] = factor
    scale = factor[0:1, 0:1]

    def nesterov(grad, moment):
        clipped = scale * grad
        return (clipped + MOMENTUM * (MOMENTUM * moment + clipped)).astype(BF16)

    @pl.when(kind[step] == 1)
    def _():
        slots[0] = nesterov(eg[0], em[0])

    @pl.when(kind[step] == 2)
    def _():
        kv_rows = kg.shape[1]
        slots[0, :kv_rows] = nesterov(kg[0], km[0])
        if kv_rows < slots.shape[1]:
            slots[0, kv_rows:] = jnp.zeros(
                (slots.shape[1] - kv_rows, slots.shape[2]), BF16
            )

    @pl.when(kind[step] == 0)
    def _():
        slots[...] = jnp.zeros_like(slots)


def form_slots(tables, squares, eg, em, kg, km, devices, entry_count):
    _, rows, width = eg.shape
    kv_rows = kg.shape[1]
    _, _, kind, expert_of, kv_of = tables
    expert_spec = pl.BlockSpec((1, rows, width), lambda i, k, e, v: (e[i], 0, 0))
    kv_spec = pl.BlockSpec((1, kv_rows, width), lambda i, k, e, v: (v[i], 0, 0))
    return pl.pallas_call(
        functools.partial(form_kernel, entry_count),
        grid_spec=pltpu.PrefetchScalarGridSpec(
            num_scalar_prefetch=3,
            grid=(devices,),
            in_specs=[
                pl.BlockSpec(squares.shape, lambda i, k, e, v: (0, 0, 0)),
                expert_spec,
                expert_spec,
                kv_spec,
                kv_spec,
            ],
            out_specs=[
                pl.BlockSpec((1, rows, width), lambda i, k, e, v: (i, 0, 0)),
                pl.BlockSpec((8, 128), lambda i, k, e, v: (0, 0)),
            ],
        ),
        out_shape=[
            jax.ShapeDtypeStruct((devices, rows, width), BF16),
            jax.ShapeDtypeStruct((8, 128), F32),
        ],
        compiler_params=pltpu.CompilerParams(vmem_limit_bytes=VMEM_LIMIT),
        name="form",
    )(
        jnp.asarray(kind, jnp.int32),
        jnp.asarray(expert_of, jnp.int32),
        jnp.asarray(kv_of, jnp.int32),
        squares,
        eg,
        em,
        kg,
        km,
    )


def dot(left, right):
    return jnp.dot(left, right, preferred_element_type=F32)


def orthogonal_kernel(gain, x_ref, out_ref):
    size, width = x_ref.shape
    x = x_ref[...]
    row = lax.broadcasted_iota(jnp.int32, (size, size), 0)
    col = lax.broadcasted_iota(jnp.int32, (size, size), 1)
    diagonal = row == col
    raw = lax.dot_general(x, x, (((1,), (1,)), ((), ())), preferred_element_type=F32)
    norm = jnp.sqrt(jnp.sum(jnp.where(diagonal, raw, 0.0), keepdims=True))
    inverse = 1.0 / (norm + NORM_EPS)
    gram = raw * inverse * inverse
    gram_low = gram.astype(BF16)
    poly = (NS_B * gram_low.astype(F32) + NS_C * dot(gram_low, gram_low)).astype(BF16)
    product = dot(poly, gram_low)
    gram = (
        (NS_A * NS_A) * gram + (2.0 * NS_A) * product + dot(product.astype(BF16), poly)
    )
    gram_low = gram.astype(BF16)
    second = (NS_B * gram_low.astype(F32) + NS_C * dot(gram_low, gram_low)).astype(BF16)
    mixed = NS_A * (poly.astype(F32) + second.astype(F32)) + dot(second, poly)
    main = NS_A * NS_A + jnp.sum(jnp.where(diagonal, mixed, 0.0), axis=1, keepdims=True)
    rest = jnp.where(diagonal, 0.0, mixed).astype(BF16)
    chunk = 512 if width % 512 == 0 else width
    for start in range(0, width, chunk):
        part = x_ref[:, start : start + chunk]
        value = (main * part.astype(F32) + dot(rest, part)) * inverse
        out_ref[:, start : start + chunk] = (
            gain * value.astype(BF16).astype(F32)
        ).astype(BF16)


def orthogonal_update(x):
    size, width = x.shape
    return pl.pallas_call(
        functools.partial(orthogonal_kernel, UPDATE_GAIN * math.sqrt(width)),
        in_specs=[pl.BlockSpec(memory_space=pltpu.VMEM)],
        out_specs=pl.BlockSpec(memory_space=pltpu.VMEM),
        out_shape=jax.ShapeDtypeStruct((size, width), BF16),
        compiler_params=pltpu.CompilerParams(vmem_limit_bytes=VMEM_LIMIT),
        name="orthogonal",
    )(x)


def finish_kernel(experts, slot_of, expert_of, kv_of, back, ew, kw, eo, eb, eu, ko, kb, ku):
    step = pl.program_id(0)

    def apply(update, master, new_ref, low_ref, update_ref):
        value = master * (1.0 - RATE * DECAY) - RATE * update.astype(F32)
        new_ref[0] = value
        low_ref[0] = value.astype(BF16)
        update_ref[0] = update

    @pl.when(step < experts)
    def _():
        apply(back[0], ew[0], eo, eb, eu)

    @pl.when(step >= experts)
    def _():
        apply(back[0, : kw.shape[1]], kw[0], ko, kb, ku)


def finish(tables, back, ew, kw):
    experts, rows, width = ew.shape
    kvs, kv_rows, _ = kw.shape
    expert_slot, kv_slot = tables[:2]
    expert_of = [min(step, experts - 1) for step in range(experts + kvs)]
    kv_of = [max(step - experts, 0) for step in range(experts + kvs)]
    expert_spec = pl.BlockSpec((1, rows, width), lambda i, s, e, v: (e[i], 0, 0))
    kv_spec = pl.BlockSpec((1, kv_rows, width), lambda i, s, e, v: (v[i], 0, 0))
    return pl.pallas_call(
        functools.partial(finish_kernel, experts),
        grid_spec=pltpu.PrefetchScalarGridSpec(
            num_scalar_prefetch=3,
            grid=(experts + kvs,),
            in_specs=[
                pl.BlockSpec((1, rows, width), lambda i, s, e, v: (s[i], 0, 0)),
                expert_spec,
                kv_spec,
            ],
            out_specs=[expert_spec] * 3 + [kv_spec] * 3,
        ),
        out_shape=[
            jax.ShapeDtypeStruct(ew.shape, F32),
            jax.ShapeDtypeStruct(ew.shape, BF16),
            jax.ShapeDtypeStruct(ew.shape, BF16),
            jax.ShapeDtypeStruct(kw.shape, F32),
            jax.ShapeDtypeStruct(kw.shape, BF16),
            jax.ShapeDtypeStruct(kw.shape, BF16),
        ],
        compiler_params=pltpu.CompilerParams(vmem_limit_bytes=VMEM_LIMIT),
        name="finish",
    )(
        jnp.asarray(expert_slot + kv_slot, jnp.int32),
        jnp.asarray(expert_of, jnp.int32),
        jnp.asarray(kv_of, jnp.int32),
        back,
        ew,
        kw,
    )


def exchange(slots):
    return lax.all_to_all(slots, "fsdp", split_axis=0, concat_axis=0, tiled=True)


def shards(expert_grad, expert_momentum, expert_master, kv_grad, kv_momentum, kv_master):
    devices = lax.axis_size("fsdp")
    shape = expert_grad.shape
    rows, width = shape[2], shape[3]
    flat = lambda array: array.reshape(-1, rows, width)
    eg, em, ew = flat(expert_grad), flat(expert_momentum), flat(expert_master)
    tables = owner_tables(eg.shape[0], kv_grad.shape[0], devices)
    entry_count = devices * (expert_grad.size + kv_grad.size)
    squares = exchange(local_squares(expert_grad, kv_grad, devices))
    slots, clip = form_slots(
        tables, squares, eg, em, kv_grad, kv_momentum, devices, entry_count
    )
    received = exchange(slots)
    factor = clip[0, 0]
    expert_moment_out = MOMENTUM * expert_momentum + factor * expert_grad
    kv_moment_out = MOMENTUM * kv_momentum + factor * kv_grad
    update = orthogonal_update(received.reshape(devices * rows, width))
    back = exchange(update.reshape(devices, rows, width))
    eo, eb, eu, ko, kb, ku = finish(tables, back, ew, kv_master)
    return (
        eo.reshape(shape),
        expert_moment_out,
        eb.reshape(shape),
        eu.reshape(shape),
        ko,
        kv_moment_out,
        kb,
        ku,
    )


def solution(mesh):
    expert = P("groups", None, "fsdp", None)
    kv = P("groups", "fsdp", None)
    return jax.shard_map(
        shards,
        mesh=mesh,
        in_specs=(expert, expert, expert, kv, kv, kv),
        out_specs=(expert, expert, expert, expert, kv, kv, kv, kv),
        check_vma=False,
    )
```

```python
import functools
import math

import jax
import jax.numpy as jnp
import numpy as np
from jax import lax
from jax.experimental import pallas as pl
from jax.experimental.pallas import tpu as pltpu
from jax.sharding import PartitionSpec as P

NS_A = 3.4445
NS_B = -4.775
NS_C = 2.0315
MOMENTUM = 0.95
RATE = 0.02
DECAY = 0.1
NORM_EPS = 1e-07
CLIP_EPS = 1e-06
CLIP_RATIO = 0.5
UPDATE_GAIN = 0.2

F32 = jnp.float32
BF16 = jnp.bfloat16
VMEM_LIMIT = 40 * 1024 * 1024
FORM_LIMIT = 24 * 1024 * 1024
FINISH_LIMIT = 16 * 1024 * 1024


def owner_tables(experts, kvs, devices):
    order = []
    for part in range(kvs):
        low, high = part * experts // kvs, (part + 1) * experts // kvs
        order += [(1, index) for index in range(low, high)] + [(2, part)]
    table = np.zeros((2, devices), np.int32)
    for position, entry in enumerate(order):
        table[:, position * devices // len(order)] = entry
    return table


def visit_tables(table, kind):
    devices = table.shape[1]
    visits = np.zeros((devices, devices), np.int32)
    for me in range(devices):
        owners = [me ^ step for step in range(devices)]
        held = next(table[1, owner] for owner in owners if table[0, owner] == kind)
        for step, owner in enumerate(owners):
            if table[0, owner] == kind:
                held = table[1, owner]
            visits[me, step] = held
    return visits


def squares_kernel(expert_ref, kv_ref, out_ref, total):
    step = pl.program_id(0)

    def fold(block):
        rows = block.reshape(-1, total.shape[0], block.shape[-1])
        return jnp.sum(rows * rows, axis=0)

    @pl.when(step == 0)
    def _():
        total[...] = jnp.zeros_like(total)
        for index in range(kv_ref.shape[0]):
            total[...] += fold(kv_ref[index])

    total[...] += fold(expert_ref[0].reshape(-1, expert_ref.shape[-1]))

    @pl.when(step == pl.num_programs(0) - 1)
    def _():
        out_ref[...] = jnp.full(out_ref.shape, jnp.sum(total[...]), F32)


def local_squares(expert_grad, kv_grad, devices):
    experts, three, rows, width = expert_grad.shape
    grouped = expert_grad.reshape(experts, three * rows, width)
    return pl.pallas_call(
        squares_kernel,
        grid=(experts,),
        in_specs=[
            pl.BlockSpec((1, three * rows, width), lambda i: (i, 0, 0)),
            pl.BlockSpec(kv_grad.shape, lambda i: (0, 0, 0)),
        ],
        out_specs=pl.BlockSpec((devices, 8, 128), lambda i: (0, 0, 0)),
        out_shape=jax.ShapeDtypeStruct((devices, 8, 128), F32),
        scratch_shapes=[pltpu.VMEM((math.gcd(8, 3 * rows, kv_grad.shape[1]), width), F32)],
        compiler_params=pltpu.CompilerParams(vmem_limit_bytes=VMEM_LIMIT),
        name="squares",
    )(grouped, kv_grad)


def form_kernel(entry_count, me, table, squares, eg, em, kg, km, *outs):
    clip, slots = outs[0], outs[1:]
    total = jnp.sum(squares[...], axis=0)
    factor = jnp.minimum(
        1.0, CLIP_RATIO * math.sqrt(entry_count) / (jnp.sqrt(total) + CLIP_EPS)
    )
    clip[...] = factor
    scale = factor[0:1, 0:1]
    kv_rows = kg.shape[1]

    def nesterov(grad, moment):
        clipped = scale * grad
        return (clipped + MOMENTUM * (MOMENTUM * moment + clipped)).astype(BF16)

    for step, slot in enumerate(slots):
        owner = me[0] ^ step
        kind, index = table[0, owner], table[1, owner]

        @pl.when(kind == 1)
        def _():
            slot[...] = nesterov(eg[index], em[index])

        @pl.when(kind == 2)
        def _():
            slot[:kv_rows] = nesterov(kg[index], km[index])
            if kv_rows < slot.shape[0]:
                slot[kv_rows:] = jnp.zeros((slot.shape[0] - kv_rows, slot.shape[1]), BF16)

        @pl.when(kind == 0)
        def _():
            slot[...] = jnp.zeros_like(slot)


def form_slots(me, table, squares, eg, em, kg, km, devices, entry_count):
    _, rows, width = eg.shape
    smem = pl.BlockSpec(memory_space=pltpu.SMEM)
    vmem = pl.BlockSpec(memory_space=pltpu.VMEM)
    return pl.pallas_call(
        functools.partial(form_kernel, entry_count),
        in_specs=[smem] * 2 + [vmem] * 5,
        out_specs=[vmem] * (1 + devices),
        out_shape=[jax.ShapeDtypeStruct((8, 128), F32)]
        + [jax.ShapeDtypeStruct((rows, width), BF16)] * devices,
        compiler_params=pltpu.CompilerParams(vmem_limit_bytes=FORM_LIMIT),
        name="form",
    )(me, table, squares, eg, em, kg, km)


def dot(left, right):
    return jnp.dot(left, right, preferred_element_type=F32)


def orthogonal_kernel(gain, *refs):
    blocks, outs, x_ref = refs[: len(refs) // 2], refs[len(refs) // 2 : -1], refs[-1]
    size, width = x_ref.shape
    rows = size // len(blocks)
    for index, block in enumerate(blocks):
        x_ref[index * rows : (index + 1) * rows] = block[...]
    x = x_ref[...]
    row = lax.broadcasted_iota(jnp.int32, (size, size), 0)
    col = lax.broadcasted_iota(jnp.int32, (size, size), 1)
    diagonal = row == col
    raw = lax.dot_general(x, x, (((1,), (1,)), ((), ())), preferred_element_type=F32)
    norm = jnp.sqrt(jnp.sum(jnp.where(diagonal, raw, 0.0), keepdims=True))
    inverse = 1.0 / (norm + NORM_EPS)
    gram = raw * inverse * inverse
    gram_low = gram.astype(BF16)
    poly = (NS_B * gram_low.astype(F32) + NS_C * dot(gram_low, gram_low)).astype(BF16)
    product = dot(poly, gram_low)
    gram = (
        (NS_A * NS_A) * gram + (2.0 * NS_A) * product + dot(product.astype(BF16), poly)
    )
    gram_low = gram.astype(BF16)
    second = (NS_B * gram_low.astype(F32) + NS_C * dot(gram_low, gram_low)).astype(BF16)
    mixed = NS_A * (poly.astype(F32) + second.astype(F32)) + dot(second, poly)
    main = NS_A * NS_A + jnp.sum(jnp.where(diagonal, mixed, 0.0), axis=1, keepdims=True)
    rest = jnp.where(diagonal, 0.0, mixed).astype(BF16)
    chunk = 512 if width % 512 == 0 else width
    for start in range(0, width, chunk):
        part = x_ref[:, start : start + chunk]
        value = (main * part.astype(F32) + dot(rest, part)) * inverse
        value = (gain * value.astype(BF16).astype(F32)).astype(BF16)
        for index, out in enumerate(outs):
            out[:, start : start + chunk] = value[index * rows : (index + 1) * rows]


def orthogonal_update(blocks):
    rows, width = blocks[0].shape
    vmem = pl.BlockSpec(memory_space=pltpu.VMEM)
    return pl.pallas_call(
        functools.partial(orthogonal_kernel, UPDATE_GAIN * math.sqrt(width)),
        in_specs=[vmem] * len(blocks),
        out_specs=[vmem] * len(blocks),
        out_shape=[jax.ShapeDtypeStruct((rows, width), BF16)] * len(blocks),
        scratch_shapes=[pltpu.VMEM((rows * len(blocks), width), BF16)],
        compiler_params=pltpu.CompilerParams(vmem_limit_bytes=VMEM_LIMIT),
        name="orthogonal",
    )(*blocks)


def finish_kernel(devices, me, kinds, expert_visit, kv_visit, *refs):
    backs, (ew, kw, eo, eb, eu, ko, kb, ku) = refs[:devices], refs[devices:]
    now = pl.program_id(0)

    def apply(update, master, new_ref, low_ref, update_ref):
        value = master * (1.0 - RATE * DECAY) - RATE * update.astype(F32)
        new_ref[0] = value
        low_ref[0] = value.astype(BF16)
        update_ref[0] = update

    for step, back in enumerate(backs):
        kind = kinds[me[0] ^ step]

        @pl.when(jnp.logical_and(now == step, kind == 1))
        def _():
            apply(back[...], ew[0], eo, eb, eu)

        @pl.when(jnp.logical_and(now == step, kind == 2))
        def _():
            apply(back[: kw.shape[1]], kw[0], ko, kb, ku)


def finish(me, table, backs, ew, kw):
    _, rows, width = ew.shape
    _, kv_rows, _ = kw.shape
    devices = len(backs)
    expert_spec = pl.BlockSpec(
        (1, rows, width), lambda i, me, kd, ev, kv: (ev[me[0] * devices + i], 0, 0)
    )
    kv_spec = pl.BlockSpec(
        (1, kv_rows, width), lambda i, me, kd, ev, kv: (kv[me[0] * devices + i], 0, 0)
    )
    whole = pl.BlockSpec((rows, width), lambda i, me, kd, ev, kv: (0, 0))
    return pl.pallas_call(
        functools.partial(finish_kernel, devices),
        grid_spec=pltpu.PrefetchScalarGridSpec(
            num_scalar_prefetch=4,
            grid=(devices,),
            in_specs=[whole] * devices + [expert_spec, kv_spec],
            out_specs=[expert_spec] * 3 + [kv_spec] * 3,
        ),
        out_shape=[
            jax.ShapeDtypeStruct(ew.shape, F32),
            jax.ShapeDtypeStruct(ew.shape, BF16),
            jax.ShapeDtypeStruct(ew.shape, BF16),
            jax.ShapeDtypeStruct(kw.shape, F32),
            jax.ShapeDtypeStruct(kw.shape, BF16),
            jax.ShapeDtypeStruct(kw.shape, BF16),
        ],
        compiler_params=pltpu.CompilerParams(vmem_limit_bytes=FINISH_LIMIT),
        name="finish",
    )(
        me,
        jnp.asarray(table[0]),
        jnp.asarray(visit_tables(table, 1).reshape(-1)),
        jnp.asarray(visit_tables(table, 2).reshape(-1)),
        *backs,
        ew,
        kw,
    )


def to_partners(blocks, owners, to_owners):
    devices = len(blocks)
    order = [0] + list(range(devices - 1, 0, -1))
    moved = [None] * devices
    for step in order:
        pairs = [
            (source, source ^ step)
            for source in range(devices)
            if (source ^ step if to_owners else source) in owners
        ]
        moved[step] = lax.ppermute(blocks[step], "fsdp", pairs) if step else blocks[0]
    return moved


def shards(expert_grad, expert_momentum, expert_master, kv_grad, kv_momentum, kv_master):
    devices = lax.axis_size("fsdp")
    me = lax.axis_index("fsdp").reshape(1)
    shape = expert_grad.shape
    rows, width = shape[2], shape[3]
    flat = lambda array: array.reshape(-1, rows, width)
    eg, em, ew = flat(expert_grad), flat(expert_momentum), flat(expert_master)
    table = owner_tables(eg.shape[0], kv_grad.shape[0], devices)
    owners = [device for device in range(devices) if table[0, device]]
    entry_count = devices * (expert_grad.size + kv_grad.size)
    squares = lax.all_to_all(
        local_squares(expert_grad, kv_grad, devices), "fsdp", 0, 0, tiled=True
    )
    clip, *slots = form_slots(
        me, jnp.asarray(table), squares, eg, em, kv_grad, kv_momentum, devices, entry_count
    )
    received = to_partners(slots, owners, True)
    factor = clip[0, 0]
    expert_moment_out = MOMENTUM * expert_momentum + factor * expert_grad
    kv_moment_out = MOMENTUM * kv_momentum + factor * kv_grad
    backs = to_partners(orthogonal_update(received), owners, False)
    eo, eb, eu, ko, kb, ku = finish(me, table, backs, ew, kv_master)
    return (
        eo.reshape(shape),
        expert_moment_out,
        eb.reshape(shape),
        eu.reshape(shape),
        ko,
        kv_moment_out,
        kb,
        ku,
    )


def solution(mesh):
    expert = P("groups", None, "fsdp", None)
    kv = P("groups", "fsdp", None)
    return jax.shard_map(
        shards,
        mesh=mesh,
        in_specs=(expert, expert, expert, kv, kv, kv),
        out_specs=(expert, expert, expert, expert, kv, kv, kv, kv),
        check_vma=False,
    )
```

```python
import functools
import math

import jax
import jax.numpy as jnp
import numpy as np
from jax import lax
from jax.experimental import pallas as pl
from jax.experimental.pallas import tpu as pltpu
from jax.sharding import PartitionSpec as P

NS_A = 3.4445
NS_B = -4.775
NS_C = 2.0315
MOMENTUM = 0.95
RATE = 0.02
DECAY = 0.1
NORM_EPS = 1e-07
CLIP_EPS = 1e-06
CLIP_RATIO = 0.5
UPDATE_GAIN = 0.2

F32 = jnp.float32
BF16 = jnp.bfloat16
VMEM_LIMIT = 40 * 1024 * 1024
SQUARES_LIMIT = 60 * 1024 * 1024
FORM_LIMIT = 24 * 1024 * 1024
FINISH_LIMIT = 16 * 1024 * 1024


def owner_tables(experts, kvs, devices):
    order = []
    for part in range(kvs):
        low, high = part * experts // kvs, (part + 1) * experts // kvs
        order += [(1, index) for index in range(low, high)] + [(2, part)]
    table = np.zeros((2, devices), np.int32)
    for position, entry in enumerate(order):
        table[:, position * devices // len(order)] = entry
    return table


def visit_tables(table, kind):
    devices = table.shape[1]
    visits = np.zeros((devices, devices), np.int32)
    for me in range(devices):
        owners = [me ^ step for step in range(devices)]
        held = next(table[1, owner] for owner in owners if table[0, owner] == kind)
        for step, owner in enumerate(owners):
            if table[0, owner] == kind:
                held = table[1, owner]
            visits[me, step] = held
    return visits


def squares_kernel(expert_ref, kv_ref, out_ref, total):
    step = pl.program_id(0)

    def fold(block):
        rows = block.reshape(-1, total.shape[0], block.shape[-1])
        return jnp.sum(rows * rows, axis=0)

    @pl.when(step == 0)
    def _():
        total[...] = jnp.zeros_like(total)
        for index in range(kv_ref.shape[0]):
            total[...] += fold(kv_ref[index])

    total[...] += fold(expert_ref[0].reshape(-1, expert_ref.shape[-1]))

    @pl.when(step == pl.num_programs(0) - 1)
    def _():
        out_ref[...] = jnp.full(out_ref.shape, jnp.sum(total[...]), F32)


def local_squares(expert_grad, kv_grad, devices):
    experts, three, rows, width = expert_grad.shape
    grouped = expert_grad.reshape(experts, three * rows, width)
    return pl.pallas_call(
        squares_kernel,
        grid=(experts,),
        in_specs=[
            pl.BlockSpec((1, three * rows, width), lambda i: (i, 0, 0)),
            pl.BlockSpec(kv_grad.shape, lambda i: (0, 0, 0)),
        ],
        out_specs=pl.BlockSpec((devices, 8, 128), lambda i: (0, 0, 0)),
        out_shape=jax.ShapeDtypeStruct((devices, 8, 128), F32),
        scratch_shapes=[pltpu.VMEM((math.gcd(8, 3 * rows, kv_grad.shape[1]), width), F32)],
        compiler_params=pltpu.CompilerParams(vmem_limit_bytes=SQUARES_LIMIT),
        name="squares",
    )(grouped, kv_grad)


def form_kernel(entry_count, me, table, squares, eg, em, kg, km, *outs):
    clip, slots = outs[0], outs[1:]
    total = jnp.sum(squares[...], axis=0)
    factor = jnp.minimum(
        1.0, CLIP_RATIO * math.sqrt(entry_count) / (jnp.sqrt(total) + CLIP_EPS)
    )
    clip[...] = factor
    scale = factor[0:1, 0:1]
    kv_rows = kg.shape[1]

    def nesterov(grad, moment):
        clipped = scale * grad
        return (clipped + MOMENTUM * (MOMENTUM * moment + clipped)).astype(BF16)

    for step, slot in enumerate(slots):
        owner = me[0] ^ step
        kind, index = table[0, owner], table[1, owner]

        @pl.when(kind == 1)
        def _():
            slot[...] = nesterov(eg[index], em[index])

        @pl.when(kind == 2)
        def _():
            slot[:kv_rows] = nesterov(kg[index], km[index])
            if kv_rows < slot.shape[0]:
                slot[kv_rows:] = jnp.zeros((slot.shape[0] - kv_rows, slot.shape[1]), BF16)

        @pl.when(kind == 0)
        def _():
            slot[...] = jnp.zeros_like(slot)


def form_slots(me, table, squares, eg, em, kg, km, devices, entry_count):
    _, rows, width = eg.shape
    smem = pl.BlockSpec(memory_space=pltpu.SMEM)
    vmem = pl.BlockSpec(memory_space=pltpu.VMEM)
    return pl.pallas_call(
        functools.partial(form_kernel, entry_count),
        in_specs=[smem] * 2 + [vmem] * 5,
        out_specs=[vmem] * (1 + devices),
        out_shape=[jax.ShapeDtypeStruct((8, 128), F32)]
        + [jax.ShapeDtypeStruct((rows, width), BF16)] * devices,
        compiler_params=pltpu.CompilerParams(vmem_limit_bytes=FORM_LIMIT),
        name="form",
    )(me, table, squares, eg, em, kg, km)


def dot(left, right):
    return jnp.dot(left, right, preferred_element_type=F32)


def orthogonal_kernel(gain, *refs):
    blocks, outs, x_ref = refs[: len(refs) // 2], refs[len(refs) // 2 : -1], refs[-1]
    size, width = x_ref.shape
    rows = size // len(blocks)
    for index, block in enumerate(blocks):
        x_ref[index * rows : (index + 1) * rows] = block[...]
    x = x_ref[...]
    row = lax.broadcasted_iota(jnp.int32, (size, size), 0)
    col = lax.broadcasted_iota(jnp.int32, (size, size), 1)
    diagonal = row == col
    raw = lax.dot_general(x, x, (((1,), (1,)), ((), ())), preferred_element_type=F32)
    norm = jnp.sqrt(jnp.sum(jnp.where(diagonal, raw, 0.0), keepdims=True))
    inverse = 1.0 / (norm + NORM_EPS)
    gram = raw * inverse * inverse
    gram_low = gram.astype(BF16)
    poly = (NS_B * gram_low.astype(F32) + NS_C * dot(gram_low, gram_low)).astype(BF16)
    product = dot(poly, gram_low)
    gram = (
        (NS_A * NS_A) * gram + (2.0 * NS_A) * product + dot(product.astype(BF16), poly)
    )
    gram_low = gram.astype(BF16)
    second = (NS_B * gram_low.astype(F32) + NS_C * dot(gram_low, gram_low)).astype(BF16)
    mixed = NS_A * (poly.astype(F32) + second.astype(F32)) + dot(second, poly)
    main = NS_A * NS_A + jnp.sum(jnp.where(diagonal, mixed, 0.0), axis=1, keepdims=True)
    rest = jnp.where(diagonal, 0.0, mixed).astype(BF16)
    chunk = 512 if width % 512 == 0 else width
    for start in range(0, width, chunk):
        part = x_ref[:, start : start + chunk]
        value = (main * part.astype(F32) + dot(rest, part)) * inverse
        value = (gain * value.astype(BF16).astype(F32)).astype(BF16)
        for index, out in enumerate(outs):
            out[:, start : start + chunk] = value[index * rows : (index + 1) * rows]


def orthogonal_update(blocks):
    rows, width = blocks[0].shape
    vmem = pl.BlockSpec(memory_space=pltpu.VMEM)
    return pl.pallas_call(
        functools.partial(orthogonal_kernel, UPDATE_GAIN * math.sqrt(width)),
        in_specs=[vmem] * len(blocks),
        out_specs=[vmem] * len(blocks),
        out_shape=[jax.ShapeDtypeStruct((rows, width), BF16)] * len(blocks),
        scratch_shapes=[pltpu.VMEM((rows * len(blocks), width), BF16)],
        compiler_params=pltpu.CompilerParams(vmem_limit_bytes=VMEM_LIMIT),
        name="orthogonal",
    )(*blocks)


def finish_kernel(devices, me, kinds, expert_visit, kv_visit, *refs):
    backs, (ew, kw, eo, eb, eu, ko, kb, ku) = refs[:devices], refs[devices:]
    now = pl.program_id(0)

    def apply(update, master, new_ref, low_ref, update_ref):
        value = master * (1.0 - RATE * DECAY) - RATE * update.astype(F32)
        new_ref[0] = value
        low_ref[0] = value.astype(BF16)
        update_ref[0] = update

    for step, back in enumerate(backs):
        kind = kinds[me[0] ^ step]

        @pl.when(jnp.logical_and(now == step, kind == 1))
        def _():
            apply(back[...], ew[0], eo, eb, eu)

        @pl.when(jnp.logical_and(now == step, kind == 2))
        def _():
            apply(back[: kw.shape[1]], kw[0], ko, kb, ku)


def finish(me, table, backs, ew, kw):
    _, rows, width = ew.shape
    _, kv_rows, _ = kw.shape
    devices = len(backs)
    expert_spec = pl.BlockSpec(
        (1, rows, width), lambda i, me, kd, ev, kv: (ev[me[0] * devices + i], 0, 0)
    )
    kv_spec = pl.BlockSpec(
        (1, kv_rows, width), lambda i, me, kd, ev, kv: (kv[me[0] * devices + i], 0, 0)
    )
    whole = pl.BlockSpec((rows, width), lambda i, me, kd, ev, kv: (0, 0))
    return pl.pallas_call(
        functools.partial(finish_kernel, devices),
        grid_spec=pltpu.PrefetchScalarGridSpec(
            num_scalar_prefetch=4,
            grid=(devices,),
            in_specs=[whole] * devices + [expert_spec, kv_spec],
            out_specs=[expert_spec] * 3 + [kv_spec] * 3,
        ),
        out_shape=[
            jax.ShapeDtypeStruct(ew.shape, F32),
            jax.ShapeDtypeStruct(ew.shape, BF16),
            jax.ShapeDtypeStruct(ew.shape, BF16),
            jax.ShapeDtypeStruct(kw.shape, F32),
            jax.ShapeDtypeStruct(kw.shape, BF16),
            jax.ShapeDtypeStruct(kw.shape, BF16),
        ],
        compiler_params=pltpu.CompilerParams(vmem_limit_bytes=FINISH_LIMIT),
        name="finish",
    )(
        me,
        jnp.asarray(table[0]),
        jnp.asarray(visit_tables(table, 1).reshape(-1)),
        jnp.asarray(visit_tables(table, 2).reshape(-1)),
        *backs,
        ew,
        kw,
    )


def to_partners(blocks, owners, to_owners):
    devices = len(blocks)
    half = devices // 2
    moved = [None] * devices
    moved[0] = blocks[0]

    def chain(steps, depth):
        for place, step in enumerate(steps):
            block = blocks[step]
            if place >= depth:
                earlier = steps[place - depth]
                block, moved[earlier] = lax.optimization_barrier((block, moved[earlier]))
            pairs = [
                (source, source ^ step)
                for source in range(devices)
                if (source ^ step if to_owners else source) in owners
            ]
            moved[step] = lax.ppermute(block, "fsdp", pairs)

    chain(list(range(half, devices)), 3)
    chain(list(range(half - 1, 0, -1)), 2)
    return moved


def shards(expert_grad, expert_momentum, expert_master, kv_grad, kv_momentum, kv_master):
    devices = lax.axis_size("fsdp")
    me = lax.axis_index("fsdp").reshape(1)
    shape = expert_grad.shape
    rows, width = shape[2], shape[3]
    flat = lambda array: array.reshape(-1, rows, width)
    eg, em, ew = flat(expert_grad), flat(expert_momentum), flat(expert_master)
    table = owner_tables(eg.shape[0], kv_grad.shape[0], devices)
    owners = [device for device in range(devices) if table[0, device]]
    entry_count = devices * (expert_grad.size + kv_grad.size)
    squares = lax.all_to_all(
        local_squares(expert_grad, kv_grad, devices), "fsdp", 0, 0, tiled=True
    )
    clip, *slots = form_slots(
        me, jnp.asarray(table), squares, eg, em, kv_grad, kv_momentum, devices, entry_count
    )
    received = to_partners(slots, owners, True)
    factor = clip[0, 0]
    expert_moment_out = MOMENTUM * expert_momentum + factor * expert_grad
    kv_moment_out = MOMENTUM * kv_momentum + factor * kv_grad
    backs = to_partners(orthogonal_update(received), owners, False)
    eo, eb, eu, ko, kb, ku = finish(me, table, backs, ew, kv_master)
    return (
        eo.reshape(shape),
        expert_moment_out,
        eb.reshape(shape),
        eu.reshape(shape),
        ko,
        kv_moment_out,
        kb,
        ku,
    )


def solution(mesh):
    expert = P("groups", None, "fsdp", None)
    kv = P("groups", "fsdp", None)
    return jax.shard_map(
        shards,
        mesh=mesh,
        in_specs=(expert, expert, expert, kv, kv, kv),
        out_specs=(expert, expert, expert, expert, kv, kv, kv, kv),
        check_vma=False,
    )
```

```python
import functools
import math

import jax
import jax.numpy as jnp
import numpy as np
from jax import lax
from jax.experimental import pallas as pl
from jax.experimental.pallas import tpu as pltpu
from jax.sharding import PartitionSpec as P

NS_A = 3.4445
NS_B = -4.775
NS_C = 2.0315
MOMENTUM = 0.95
RATE = 0.02
DECAY = 0.1
NORM_EPS = 1e-07
CLIP_EPS = 1e-06
CLIP_RATIO = 0.5
UPDATE_GAIN = 0.2

F32 = jnp.float32
BF16 = jnp.bfloat16
VMEM_LIMIT = 40 * 1024 * 1024
KV_LIMIT = 24 * 1024 * 1024
SQUARES_LIMIT = 60 * 1024 * 1024
STREAM_LIMIT = 16 * 1024 * 1024


def owner_table(experts, devices):
    table = np.zeros((2, devices), np.int32)
    chips = devices // 2
    first = min(experts, chips)
    for index in range(first):
        table[:, 2 * (index * chips // first)] = (1, index)
    by_parity = sorted(range(chips), key=lambda chip: bin(chip).count("1") % 2)
    for index in range(first, experts):
        table[:, 2 * by_parity[index - first] + 1] = (1, index)
    return table


def visit_tables(table, steps):
    devices = table.shape[1]
    kinds = np.zeros((devices, len(steps)), np.int32)
    held = np.zeros((devices, len(steps)), np.int32)
    for me in range(devices):
        owners = [me ^ step for step in steps]
        experts = [table[1, owner] for owner in owners if table[0, owner] == 1]
        last = experts[0] if experts else 0
        for place, owner in enumerate(owners):
            kinds[me, place] = table[0, owner] == 1
            last = table[1, owner] if table[0, owner] == 1 else last
            held[me, place] = last
    return kinds, held


def visits(table, steps):
    return tuple(jnp.asarray(part.reshape(-1)) for part in visit_tables(table, steps))


def squares_kernel(expert_ref, kv_ref, out_ref, total):
    step = pl.program_id(0)

    def fold(block):
        rows = block.reshape(-1, total.shape[0], block.shape[-1])
        return jnp.sum(rows * rows, axis=0)

    @pl.when(step == 0)
    def _():
        total[...] = jnp.zeros_like(total)
        for index in range(kv_ref.shape[0]):
            total[...] += fold(kv_ref[index])

    total[...] += fold(expert_ref[0].reshape(-1, expert_ref.shape[-1]))

    @pl.when(step == pl.num_programs(0) - 1)
    def _():
        out_ref[...] = jnp.full(out_ref.shape, jnp.sum(total[...]), F32)


def local_squares(expert_grad, kv_grad, devices):
    experts, three, rows, width = expert_grad.shape
    grouped = expert_grad.reshape(experts, three * rows, width)
    return pl.pallas_call(
        squares_kernel,
        grid=(experts,),
        in_specs=[
            pl.BlockSpec((1, three * rows, width), lambda i: (i, 0, 0)),
            pl.BlockSpec(kv_grad.shape, lambda i: (0, 0, 0)),
        ],
        out_specs=pl.BlockSpec((devices, 8, 128), lambda i: (0, 0, 0)),
        out_shape=jax.ShapeDtypeStruct((devices, 8, 128), F32),
        scratch_shapes=[pltpu.VMEM((math.gcd(8, 3 * rows, kv_grad.shape[1]), width), F32)],
        compiler_params=pltpu.CompilerParams(vmem_limit_bytes=SQUARES_LIMIT),
        name="squares",
    )(grouped, kv_grad)


def stage_kernel(me, held, eg, em, out):
    out[0] = eg[...].astype(BF16)
    out[1] = em[...].astype(BF16)


def stage_sibling(me, table, eg, em):
    _, rows, width = eg.shape
    chips = table.shape[1] // 2
    _, held = visits(table, [2 * step + 1 for step in range(chips)])
    spec = pl.BlockSpec((1, rows, width), lambda i, me, held: (held[me[0] * chips + i], 0, 0))
    return pl.pallas_call(
        stage_kernel,
        grid_spec=pltpu.PrefetchScalarGridSpec(
            num_scalar_prefetch=2,
            grid=(chips,),
            in_specs=[spec, spec],
            out_specs=pl.BlockSpec((2, 1, rows, width), lambda i, me, held: (0, i, 0, 0)),
        ),
        out_shape=jax.ShapeDtypeStruct((2, chips, rows, width), BF16),
        compiler_params=pltpu.CompilerParams(vmem_limit_bytes=STREAM_LIMIT),
        name="stage",
    )(me, held, eg, em)


def nesterov(scale, grad, moment):
    clipped = scale * grad.astype(F32)
    return (clipped + MOMENTUM * (MOMENTUM * moment.astype(F32) + clipped)).astype(BF16)


def clip_kernel(count, squares, kg, km, out_clip, out):
    total = jnp.sum(squares[...], axis=0)
    factor = jnp.minimum(1.0, count / (jnp.sqrt(total) + CLIP_EPS))
    out_clip[...] = factor
    out[...] = nesterov(factor[0:1, 0:1], kg[...], km[...])


def clip_and_kv(squares, kg, km, count):
    return pl.pallas_call(
        functools.partial(clip_kernel, count),
        out_shape=[
            jax.ShapeDtypeStruct((8, 128), F32),
            jax.ShapeDtypeStruct(kg.shape, BF16),
        ],
        compiler_params=pltpu.CompilerParams(vmem_limit_bytes=STREAM_LIMIT),
        name="clip",
    )(squares, kg, km)


def form_kernel(me, kinds, held, clip, eg, em, sib, *outs):
    now = pl.program_id(0)
    scale = clip[0:1, 0:1]
    for step, out in enumerate(outs):

        @pl.when(jnp.logical_and(now == step, kinds[me[0] * len(outs) + step] == 1))
        def _():
            out[0] = nesterov(scale, eg[0], em[0])
            out[1] = nesterov(scale, sib[0, 0], sib[1, 0])


def form_blocks(me, table, chip_steps, clip, eg, em, sib):
    _, rows, width = eg.shape
    size = len(chip_steps)
    start = chip_steps[0]
    kinds, held = visits(table, [2 * step for step in chip_steps])
    spec = pl.BlockSpec((1, rows, width), lambda i, me, k, h: (h[me[0] * size + i], 0, 0))
    block = (2, rows, width)
    return pl.pallas_call(
        form_kernel,
        grid_spec=pltpu.PrefetchScalarGridSpec(
            num_scalar_prefetch=3,
            grid=(size,),
            in_specs=[
                pl.BlockSpec(clip.shape, lambda i, *_: (0, 0)),
                spec,
                spec,
                pl.BlockSpec((2, 1, rows, width), lambda i, *_: (0, start + i, 0, 0)),
            ],
            out_specs=[pl.BlockSpec(block, lambda i, *_: (0, 0, 0))] * size,
        ),
        out_shape=[jax.ShapeDtypeStruct(block, BF16)] * size,
        compiler_params=pltpu.CompilerParams(vmem_limit_bytes=STREAM_LIMIT),
        name="form",
    )(me, kinds, held, clip, eg, em, sib)


def dot(left, right):
    return jnp.dot(left, right, preferred_element_type=F32)


def apply_rows(gain, x, rest, lead, low, high, store):
    width = x.shape[1]
    chunk = 512 if width % 512 == 0 else width
    for start in range(0, width, chunk):
        part = x[low:high, start : start + chunk].astype(F32)
        value = lead[low:high, 0:1] * part + dot(rest[low:high], x[:, start : start + chunk])
        value = (gain * value.astype(BF16).astype(F32)).astype(BF16)
        store(start, chunk, value)


def store_blocks(outs, rows):
    def store(start, chunk, value):
        for index, out in enumerate(outs):
            for core in range(2):
                low = (2 * index + core) * rows
                out[core, :, start : start + chunk] = value[low : low + rows]

    return store


def outer(left, right):
    return lax.dot_general(left, right, (((1,), (1,)), ((), ())), preferred_element_type=F32)


def transform(raw):
    size = raw.shape[0]
    row = lax.broadcasted_iota(jnp.int32, (size, size), 0)
    col = lax.broadcasted_iota(jnp.int32, (size, size), 1)
    diagonal = row == col
    norm = jnp.sqrt(jnp.sum(jnp.where(diagonal, raw, 0.0), keepdims=True))
    inverse = 1.0 / (norm + NORM_EPS)
    gram = raw * inverse * inverse
    low = gram.astype(BF16)
    first = (NS_B * low.astype(F32) + NS_C * dot(low, low)).astype(BF16)
    product = dot(first, low)
    gram = (NS_A * NS_A) * gram + (2.0 * NS_A) * product + dot(product.astype(BF16), first)
    low = gram.astype(BF16)
    second = (NS_B * low.astype(F32) + NS_C * dot(low, low)).astype(BF16)
    mixed = NS_A * (first.astype(F32) + second.astype(F32)) + dot(second, first)
    main = NS_A * NS_A + jnp.sum(jnp.where(diagonal, mixed, 0.0), axis=1, keepdims=True)
    return main * inverse, (jnp.where(diagonal, 0.0, mixed) * inverse).astype(BF16)


def place_blocks(blocks, x, start):
    rows = blocks[0].shape[1]
    for index, block in enumerate(blocks):
        for core in range(2):
            low = start + (2 * index + core) * rows
            x[low : low + rows] = block[core]


def near_kernel(me, kinds, *refs):
    blocks, (x, gram) = refs[:-2], refs[-2:]

    @pl.when(kinds[me[0]] == 1)
    def _():
        place_blocks(blocks, x, 0)
        gram[...] = outer(x[...], x[...])


def transform_kernel(gain, me, kinds, near, gram, *refs):
    chips = kinds.shape[0] // 2
    blocks, (x, rest, lead), outs = (
        refs[: chips // 2], refs[chips // 2 : chips // 2 + 3], refs[chips // 2 + 3 :]
    )
    half = near.shape[0]

    @pl.when(kinds[me[0]] == 1)
    def _():
        x[:half] = near[...]
        place_blocks(blocks, x, half)
        far = x[half:]
        cross = outer(near[...], far)
        raw = jnp.concatenate(
            [
                jnp.concatenate([gram[...], cross], axis=1),
                jnp.concatenate([cross.T, outer(far, far)], axis=1),
            ],
            axis=0,
        )
        main, other = transform(raw)
        lead[...] = jnp.broadcast_to(main, lead.shape)
        rest[...] = other
        apply_rows(gain, x, rest, lead, half, 2 * half, store_blocks(outs, blocks[0].shape[1]))


def apply_kernel(gain, me, kinds, x, rest, lead, *outs):
    @pl.when(kinds[me[0]] == 1)
    def _():
        store = store_blocks(outs, outs[0].shape[1])
        apply_rows(gain, x, rest, lead, 0, x.shape[0] // 2, store)


def near_gram(me, kinds, blocks):
    _, rows, width = blocks[0].shape
    half = 2 * len(blocks) * rows
    vmem = pl.BlockSpec(memory_space=pltpu.VMEM)
    smem = pl.BlockSpec(memory_space=pltpu.SMEM)
    return pl.pallas_call(
        near_kernel,
        in_specs=[smem, smem] + [vmem] * len(blocks),
        out_specs=[vmem, vmem],
        out_shape=[
            jax.ShapeDtypeStruct((half, width), BF16),
            jax.ShapeDtypeStruct((half, half), F32),
        ],
        compiler_params=pltpu.CompilerParams(vmem_limit_bytes=STREAM_LIMIT),
        cost_estimate=pl.CostEstimate(
            flops=2 * half * half * width, bytes_accessed=4 * half * width, transcendentals=0
        ),
        name="near",
    )(me, kinds, *blocks)


def orthogonal_update(me, kinds, near, gram, blocks):
    _, rows, width = blocks[0].shape
    half = near.shape[0]
    size = 2 * half
    gain = UPDATE_GAIN * math.sqrt(width)
    vmem = pl.BlockSpec(memory_space=pltpu.VMEM)
    smem = pl.BlockSpec(memory_space=pltpu.SMEM)
    outs = [jax.ShapeDtypeStruct((2, rows, width), BF16)] * len(blocks)
    params = pltpu.CompilerParams(vmem_limit_bytes=VMEM_LIMIT)
    x, rest, lead, *far = pl.pallas_call(
        functools.partial(transform_kernel, gain),
        in_specs=[smem, smem] + [vmem] * (2 + len(blocks)),
        out_specs=[vmem] * (3 + len(blocks)),
        out_shape=[
            jax.ShapeDtypeStruct((size, width), BF16),
            jax.ShapeDtypeStruct((size, size), BF16),
            jax.ShapeDtypeStruct((size, 128), F32),
            *outs,
        ],
        compiler_params=params,
        name="transform",
    )(me, kinds, near, gram, *blocks)
    near = pl.pallas_call(
        functools.partial(apply_kernel, gain),
        in_specs=[smem, smem] + [vmem] * 3,
        out_specs=[vmem] * len(blocks),
        out_shape=outs,
        compiler_params=params,
        name="apply",
    )(me, kinds, x, rest, lead)
    return list(near), far


def kv_kernel(gain, me, gathered, kw, ko, kb, ku, x):
    kvs, rows, _ = kw.shape
    devices = gathered.shape[0]
    for index in range(kvs):
        for device in range(devices):
            x[device * rows : (device + 1) * rows] = gathered[device, index]
        main, rest = transform(outer(x[...], x[...]))
        size = x.shape[0]
        row = lax.broadcasted_iota(jnp.int32, (rows, size), 0) + me[0] * rows
        col = lax.broadcasted_iota(jnp.int32, (rows, size), 1)
        pick = (row == col).astype(F32)
        lead = jnp.sum(pick * main.reshape(1, size), axis=1, keepdims=True)
        mine = dot(pick.astype(BF16), rest).astype(BF16)
        value = lead * gathered[me[0], index].astype(F32) + dot(mine, x[...])
        update = (gain * value.astype(BF16).astype(F32)).astype(BF16)
        master = kw[index] * (1.0 - RATE * DECAY) - RATE * update.astype(F32)
        ko[index] = master
        kb[index] = master.astype(BF16)
        ku[index] = update


def kv_update(me, gathered, kw):
    kvs, rows, width = kw.shape
    size = gathered.shape[0] * rows
    vmem = pl.BlockSpec(memory_space=pltpu.VMEM)
    return pl.pallas_call(
        functools.partial(kv_kernel, UPDATE_GAIN * math.sqrt(width)),
        in_specs=[pl.BlockSpec(memory_space=pltpu.SMEM), vmem, vmem],
        out_specs=[vmem] * 3,
        out_shape=[jax.ShapeDtypeStruct(kw.shape, kind) for kind in (F32, BF16, BF16)],
        scratch_shapes=[pltpu.VMEM((size, width), BF16)],
        compiler_params=pltpu.CompilerParams(vmem_limit_bytes=KV_LIMIT),
        cost_estimate=pl.CostEstimate(
            flops=kvs * (2 * size * size * width + 10 * size**3),
            bytes_accessed=kvs * size * width * 2,
            transcendentals=0,
        ),
        name="kv",
    )(me, gathered, kw)


def gather_kernel(*refs):
    out = refs[-1]
    for index, block in enumerate(refs[:-1]):
        out[index] = block[0]


def gather_sibling(blocks):
    _, rows, width = blocks[0].shape
    shape = (len(blocks), rows, width)
    return pl.pallas_call(
        gather_kernel,
        grid=(1,),
        in_specs=[pl.BlockSpec((1, rows, width), lambda i: (1, 0, 0))] * len(blocks),
        out_specs=pl.BlockSpec(shape, lambda i: (0, 0, 0)),
        out_shape=jax.ShapeDtypeStruct(shape, BF16),
        compiler_params=pltpu.CompilerParams(vmem_limit_bytes=STREAM_LIMIT),
        name="gather",
    )(*blocks)


def finish_kernel(plan, me, kinds, held, *refs):
    own, has_sibling, has_earlier, steps, idle = plan
    owns, refs = refs[:own], list(refs[own:])
    sibling = refs.pop(0) if has_sibling else None
    ew = refs.pop(0)
    earlier, (new_ref, low_ref, update_ref) = refs[:-3], refs[-3:]
    now = pl.program_id(0)

    if has_earlier and idle:
        first = me[0] * steps
        busy = functools.reduce(jnp.maximum, [kinds[first + step] for step in range(steps)])

        @pl.when(jnp.logical_and(now == 0, busy == 0))
        def _():
            for before, after in zip(earlier, refs[-3:]):
                pltpu.sync_copy(before.at[pl.ds(held[first], 1)], after)

    def apply(update):
        value = ew[0] * (1.0 - RATE * DECAY) - RATE * update.astype(F32)
        new_ref[0] = value
        low_ref[0] = value.astype(BF16)
        update_ref[0] = update

    valid = kinds[me[0] * steps + now] == 1
    for step, block in enumerate(owns):

        @pl.when(jnp.logical_and(now == step, valid))
        def _():
            apply(block[0])

    if has_sibling:

        @pl.when(jnp.logical_and(now >= own, valid))
        def _():
            apply(sibling[0])


def finish(me, table, ew, owns, own_steps, sibling, sibling_steps, earlier):
    _, rows, width = ew.shape
    steps = [2 * step for step in own_steps] + [2 * step + 1 for step in sibling_steps]
    kinds, held = visits(table, steps)
    idle = not visit_tables(table, steps)[0].any(axis=1).all()
    size, own = len(steps), len(owns)
    block = (1, rows, width)
    spec = pl.BlockSpec(block, lambda i, me, k, h: (h[me[0] * size + i], 0, 0))
    operands = [me, kinds, held, *owns]
    in_specs = [pl.BlockSpec(block, lambda i, *_: (0, 0, 0))] * own
    if sibling is not None:
        last = sibling.shape[0] - 1
        in_specs.append(pl.BlockSpec(block, lambda i, *_: (jnp.clip(i - own, 0, last), 0, 0)))
        operands.append(sibling)
    in_specs.append(spec)
    operands.append(ew)
    aliases = {}
    if earlier is not None:
        aliases = {len(operands) + index: index for index in range(3)}
        in_specs += [pl.BlockSpec(memory_space=pl.ANY)] * 3
        operands += list(earlier)
    return pl.pallas_call(
        functools.partial(
            finish_kernel, (own, sibling is not None, earlier is not None, size, idle)
        ),
        grid_spec=pltpu.PrefetchScalarGridSpec(
            num_scalar_prefetch=3,
            grid=(size,),
            in_specs=in_specs,
            out_specs=[spec] * 3,
        ),
        out_shape=[jax.ShapeDtypeStruct(ew.shape, kind) for kind in (F32, BF16, BF16)],
        input_output_aliases=aliases,
        compiler_params=pltpu.CompilerParams(vmem_limit_bytes=STREAM_LIMIT),
        name="finish",
    )(*operands)


def permute(array, pairs):
    return lax.ppermute(array, "fsdp", pairs)


def together(*arrays):
    return lax.optimization_barrier(arrays)


def block_pairs(table, step, to_owners):
    devices = table.shape[1]
    pairs = [(d ^ (2 * step), d) for d in range(devices) if table[0, d] == 1]
    return pairs if to_owners else [(there, here) for here, there in pairs]


def shards(expert_grad, expert_momentum, expert_master, kv_grad, kv_momentum, kv_master):
    devices = lax.axis_size("fsdp")
    chips, half = devices // 2, devices // 4
    me = lax.axis_index("fsdp").reshape(1)
    shape = expert_grad.shape
    rows, width = shape[2], shape[3]
    flat = lambda array: array.reshape(-1, rows, width)
    eg, em, ew = flat(expert_grad), flat(expert_momentum), flat(expert_master)
    table = owner_table(eg.shape[0], devices)
    entry_count = devices * (expert_grad.size + kv_grad.size)
    cores = [(device, device ^ 1) for device in range(devices)]
    near_steps, far_steps = list(range(half)), list(range(half, chips))

    staged = stage_sibling(me, table, eg, em)
    partial, staged = together(local_squares(expert_grad, kv_grad, devices), staged)
    squares = lax.all_to_all(partial, "fsdp", 0, 0, tiled=True)
    squares, sibling = together(squares, permute(staged, cores))
    clip, kv_rows = clip_and_kv(
        squares, kv_grad, kv_momentum, CLIP_RATIO * math.sqrt(entry_count)
    )

    gathered = lax.all_gather(kv_rows, "fsdp")
    far = list(form_blocks(me, table, far_steps, clip, eg, em, sibling))
    clip, far[0] = together(clip, far[0])
    near = list(form_blocks(me, table, near_steps, clip, eg, em, sibling))
    far = [permute(block, block_pairs(table, step, True)) for step, block in zip(far_steps, far)]
    for step in near_steps[1:]:
        near[step] = permute(near[step], block_pairs(table, step, True))
    kinds = jnp.asarray(table[0])
    near_rows, near_product = near_gram(me, kinds, near)

    near_rows, clip, gathered = together(near_rows, clip, gathered)
    factor = clip[0, 0]
    expert_moment_out = MOMENTUM * expert_momentum + factor * expert_grad
    kv_moment_out = MOMENTUM * kv_momentum + factor * kv_grad
    ko, kb, ku = kv_update(me, gathered, kv_master)
    near_rows, ko, kb, ku, expert_moment_out, kv_moment_out = together(
        near_rows, ko, kb, ku, expert_moment_out, kv_moment_out
    )
    near, far = orthogonal_update(me, kinds, near_rows, near_product, far)

    far = [permute(block, block_pairs(table, step, False)) for step, block in zip(far_steps, far)]
    for step in near_steps[1:]:
        near[step] = permute(near[step], block_pairs(table, step, False))
    near_sibling = permute(gather_sibling(near), cores)
    done = finish(me, table, ew, near, near_steps, None, [], None)
    far[0], *done = together(far[0], *done)
    far_sibling = permute(gather_sibling(far), cores)
    done = finish(me, table, ew, far, far_steps, near_sibling, near_steps, done)
    eo, eb, eu = finish(me, table, ew, [], [], far_sibling, far_steps, done)
    return (
        eo.reshape(shape),
        expert_moment_out,
        eb.reshape(shape),
        eu.reshape(shape),
        ko,
        kv_moment_out,
        kb,
        ku,
    )


def solution(mesh):
    expert = P("groups", None, "fsdp", None)
    kv = P("groups", "fsdp", None)
    return jax.shard_map(
        shards,
        mesh=mesh,
        in_specs=(expert, expert, expert, kv, kv, kv),
        out_specs=(expert, expert, expert, expert, kv, kv, kv, kv),
        check_vma=False,
    )
```

```python
import functools
import math

import jax
import jax.numpy as jnp
import numpy as np
from jax import lax
from jax.experimental import pallas as pl
from jax.experimental.pallas import tpu as pltpu
from jax.sharding import PartitionSpec as P

NS_A = 3.4445
NS_B = -4.775
NS_C = 2.0315
MOMENTUM = 0.95
RATE = 0.02
DECAY = 0.1
NORM_EPS = 1e-07
CLIP_EPS = 1e-06
CLIP_RATIO = 0.5
UPDATE_GAIN = 0.2

F32 = jnp.float32
BF16 = jnp.bfloat16
VMEM_LIMIT = 40 * 1024 * 1024
LOAD_LIMIT = 38 * 1024 * 1024
STREAM_LIMIT = 16 * 1024 * 1024


def owner_table(experts, kvs, devices):
    table = np.zeros((2, devices), np.int32)
    chips = devices // 2
    first = min(experts, chips)
    for index in range(first):
        table[:, 2 * (index * chips // first)] = (1, index)
    by_parity = sorted(range(chips), key=lambda chip: bin(chip).count("1") % 2)
    for index in range(first, experts):
        table[:, 2 * by_parity[index - first] + 1] = (1, index)
    for index in range(kvs):
        low = index * devices // kvs
        free = [d for d in range(low, low + devices // kvs) if d % 2 and not table[0, d]]
        table[:, free[0]] = (2, index)
    return table


def visit_tables(table, steps):
    devices = table.shape[1]
    kinds = np.zeros((devices, len(steps)), np.int32)
    held = np.zeros((devices, len(steps)), np.int32)
    for me in range(devices):
        owners = [me ^ step for step in steps]
        experts = [table[1, owner] for owner in owners if table[0, owner] == 1]
        last = experts[0] if experts else 0
        for place, owner in enumerate(owners):
            kinds[me, place] = table[0, owner]
            last = table[1, owner] if table[0, owner] == 1 else last
            held[me, place] = last
    return kinds, held


def visits(table, steps):
    return tuple(jnp.asarray(part.reshape(-1)) for part in visit_tables(table, steps))


def load_kernel(me, held, eg, em, kg, km, partial, gv, mv, staged, keep, away, total, sems):
    chunks = sems.shape[1]
    size = gv.shape[0] // chunks
    chips = staged.shape[1]
    copies = [
        [
            pltpu.make_async_copy(
                source.at[pl.ds(chunk * size, size)],
                target.at[pl.ds(chunk * size, size)],
                sems.at[place, chunk],
            )
            for chunk in range(chunks)
        ]
        for place, (source, target) in enumerate(((eg, gv), (em, mv)))
    ]
    for copy in copies[0] + copies[1]:
        copy.start()

    def fold(block):
        rows = block.reshape(-1, total.shape[0], block.shape[-1])
        return jnp.sum(rows * rows, axis=0)

    total[...] = fold(kg[...])
    mine = (me[0] >= partial.shape[0] // 2).astype(jnp.int32)
    for out, index in ((keep, mine), (away, 1 - mine)):
        out[0] = kg[index].astype(BF16)
        out[1] = km[index].astype(BF16)
    for chunk in range(chunks):
        copies[0][chunk].wait()
        total[...] += fold(gv[chunk * size : (chunk + 1) * size])
    partial[...] = jnp.full(partial.shape, jnp.sum(total[...]), F32)
    for step in range(chips):
        staged[0, step] = gv[held[me[0] * chips + step]].astype(BF16)
    for copy in copies[1]:
        copy.wait()
    for step in range(chips):
        staged[1, step] = mv[held[me[0] * chips + step]].astype(BF16)


def load(me, table, eg, em, kg, km):
    experts, rows, width = eg.shape
    _, kv_rows, _ = kg.shape
    devices = table.shape[1]
    chips = devices // 2
    _, held = visits(table, [2 * step + 1 for step in range(chips)])
    vmem = pl.BlockSpec(memory_space=pltpu.VMEM)
    smem = pl.BlockSpec(memory_space=pltpu.SMEM)
    hbm = pl.BlockSpec(memory_space=pltpu.HBM)
    chunks = experts // 3
    return pl.pallas_call(
        load_kernel,
        in_specs=[smem, smem, hbm, hbm, vmem, vmem],
        out_specs=[vmem] * 6,
        out_shape=[
            jax.ShapeDtypeStruct((devices, 8, 128), F32),
            jax.ShapeDtypeStruct(eg.shape, F32),
            jax.ShapeDtypeStruct(eg.shape, F32),
            jax.ShapeDtypeStruct((2, chips, rows, width), BF16),
            jax.ShapeDtypeStruct((2, kv_rows, width), BF16),
            jax.ShapeDtypeStruct((2, kv_rows, width), BF16),
        ],
        scratch_shapes=[
            pltpu.VMEM((math.gcd(8, 3 * rows, kv_rows), width), F32),
            pltpu.SemaphoreType.DMA((2, chunks)),
        ],
        compiler_params=pltpu.CompilerParams(vmem_limit_bytes=LOAD_LIMIT),
        name="load",
    )(me, held, eg, em, kg, km)


def nesterov(scale, grad, moment):
    clipped = scale * grad.astype(F32)
    return (clipped + MOMENTUM * (MOMENTUM * moment.astype(F32) + clipped)).astype(BF16)


def form_far_kernel(count, start, me, kinds, index, squares, gv, mv, sib, clip, *outs):
    total = jnp.sum(squares[...], axis=0)
    factor = jnp.minimum(1.0, count / (jnp.sqrt(total) + CLIP_EPS))
    clip[...] = factor
    scale = factor[0:1, 0:1]
    for step, out in enumerate(outs):
        place = me[0] * len(outs) + step

        @pl.when(kinds[place] == 1)
        def _():
            out[0] = nesterov(scale, gv[index[place]], mv[index[place]])
            out[1] = nesterov(scale, sib[0, start + step], sib[1, start + step])


def form_near_kernel(
    me, kinds, index, clip, gv, mv, sib, kg, km, mirror, kv_sib, *outs
):
    scale = clip[0:1, 0:1]
    rows, kv_rows = gv.shape[1], kg.shape[1]
    mine = (me[0] >= kinds.shape[0] // len(outs) // 2).astype(jnp.int32)
    for step, out in enumerate(outs):
        place = me[0] * len(outs) + step

        @pl.when(kinds[place] == 1)
        def _():
            out[0, :rows] = nesterov(scale, gv[index[place]], mv[index[place]])
            out[1, :rows] = nesterov(scale, sib[0, step], sib[1, step])

        @pl.when(kinds[place] == 2)
        def _():
            out[0, :kv_rows] = nesterov(scale, kg[mine], km[mine])
            out[0, kv_rows : 2 * kv_rows] = nesterov(scale, mirror[0], mirror[1])
            out[1, :kv_rows] = nesterov(scale, kv_sib[0, 0], kv_sib[0, 1])
            out[1, kv_rows : 2 * kv_rows] = nesterov(scale, kv_sib[1, 0], kv_sib[1, 1])


def form_call(kernel, name, table, chip_steps, me, operands, outs):
    kinds, index = visits(table, [2 * step for step in chip_steps])
    vmem = pl.BlockSpec(memory_space=pltpu.VMEM)
    smem = pl.BlockSpec(memory_space=pltpu.SMEM)
    return pl.pallas_call(
        kernel,
        in_specs=[smem] * 3 + [vmem] * len(operands),
        out_specs=[vmem] * len(outs),
        out_shape=outs,
        compiler_params=pltpu.CompilerParams(vmem_limit_bytes=STREAM_LIMIT),
        name=name,
    )(me, kinds, index, *operands)


def form_far(me, table, steps, squares, gv, mv, sib, count):
    block = jax.ShapeDtypeStruct((2,) + gv.shape[1:], BF16)
    clip = jax.ShapeDtypeStruct((8, 128), F32)
    kernel = functools.partial(form_far_kernel, count, steps[0])
    return form_call(
        kernel, "far", table, steps, me, (squares, gv, mv, sib), [clip] + [block] * len(steps)
    )


def form_near(me, table, steps, clip, gv, mv, sib, kg, km, mirror, kv_sib):
    _, rows, width = gv.shape
    block = jax.ShapeDtypeStruct((2, max(rows, 2 * kg.shape[1]), width), BF16)
    operands = (clip, gv, mv, sib, kg, km, mirror, kv_sib)
    return form_call(
        form_near_kernel, "form", table, steps, me, operands, [block] * len(steps)
    )


def dot(left, right):
    return jnp.dot(left, right, preferred_element_type=F32)


def apply_rows(gain, x, rest, lead, low, high, store):
    width = x.shape[1]
    chunk = 512 if width % 512 == 0 else width
    for start in range(0, width, chunk):
        part = x[low:high, start : start + chunk].astype(F32)
        value = lead[low:high, 0:1] * part + dot(rest[low:high], x[:, start : start + chunk])
        value = (gain * value.astype(BF16).astype(F32)).astype(BF16)
        store(start, chunk, value)


def store_blocks(outs, rows):
    def store(start, chunk, value):
        for index, out in enumerate(outs):
            for core in range(2):
                low = (2 * index + core) * rows
                out[core, :rows, start : start + chunk] = value[low : low + rows]

    return store


def outer(left, right):
    return lax.dot_general(left, right, (((1,), (1,)), ((), ())), preferred_element_type=F32)


def transform(raw):
    size = raw.shape[0]
    row = lax.broadcasted_iota(jnp.int32, (size, size), 0)
    col = lax.broadcasted_iota(jnp.int32, (size, size), 1)
    diagonal = row == col
    norm = jnp.sqrt(jnp.sum(jnp.where(diagonal, raw, 0.0), keepdims=True))
    inverse = 1.0 / (norm + NORM_EPS)
    gram = raw * inverse * inverse
    low = gram.astype(BF16)
    first = (NS_B * low.astype(F32) + NS_C * dot(low, low)).astype(BF16)
    product = dot(first, low)
    gram = (NS_A * NS_A) * gram + (2.0 * NS_A) * product + dot(product.astype(BF16), first)
    low = gram.astype(BF16)
    second = (NS_B * low.astype(F32) + NS_C * dot(low, low)).astype(BF16)
    mixed = NS_A * (first.astype(F32) + second.astype(F32)) + dot(second, first)
    main = NS_A * NS_A + jnp.sum(jnp.where(diagonal, mixed, 0.0), axis=1, keepdims=True)
    return main * inverse, (jnp.where(diagonal, 0.0, mixed) * inverse).astype(BF16)


def place_blocks(blocks, rows, x, start):
    for index, block in enumerate(blocks):
        for core in range(2):
            low = start + (2 * index + core) * rows
            x[low : low + rows] = block[core, :rows]


def near_kernel(me, kinds, *refs):
    blocks, (x, gram) = refs[:-2], refs[-2:]

    @pl.when(kinds[me[0]] == 1)
    def _():
        place_blocks(blocks, x.shape[0] // len(blocks) // 2, x, 0)
        gram[...] = outer(x[...], x[...])


def transform_kernel(gain, kv_rows, me, kinds, near, gram, *refs):
    chips = kinds.shape[0] // 2
    kv_blocks, blocks = refs[: chips // 2], refs[chips // 2 : chips]
    (x, rest, lead), outs = refs[chips : chips + 3], refs[chips + 3 :]
    half, rows = near.shape[0], blocks[0].shape[1]
    kind = kinds[me[0]]

    @pl.when(kind == 1)
    def _():
        x[:half] = near[...]
        place_blocks(blocks, rows, x, half)
        far = x[half:]
        cross = outer(near[...], far)
        raw = jnp.concatenate(
            [
                jnp.concatenate([gram[...], cross], axis=1),
                jnp.concatenate([cross.T, outer(far, far)], axis=1),
            ],
            axis=0,
        )
        main, other = transform(raw)
        lead[...] = jnp.broadcast_to(main, lead.shape)
        rest[...] = other
        apply_rows(gain, x, rest, lead, half, 2 * half, store_blocks(outs, rows))

    @pl.when(kind == 2)
    def _():
        size = 4 * kv_rows * len(kv_blocks)
        place_blocks(kv_blocks, 2 * kv_rows, x, 0)
        main, other = transform(outer(x[:size], x[:size]))
        lead[:size] = jnp.broadcast_to(main, (size, lead.shape[1]))
        rest[:size, :size] = other


def apply_kernel(gain, kv_rows, me, kinds, x, rest, lead, *outs):
    kind = kinds[me[0]]

    @pl.when(kind == 1)
    def _():
        rows = x.shape[0] // len(outs) // 4
        apply_rows(gain, x, rest, lead, 0, x.shape[0] // 2, store_blocks(outs, rows))

    @pl.when(kind == 2)
    def _():
        size = 4 * kv_rows * len(outs)
        kv = [ref.at[:size] for ref in (x, rest, lead)]
        kv[1] = rest.at[:size, :size]
        apply_rows(gain, *kv, 0, size, store_blocks(outs, 2 * kv_rows))


def near_gram(me, kinds, blocks, rows):
    width = blocks[0].shape[2]
    half = 2 * len(blocks) * rows
    vmem = pl.BlockSpec(memory_space=pltpu.VMEM)
    smem = pl.BlockSpec(memory_space=pltpu.SMEM)
    return pl.pallas_call(
        near_kernel,
        in_specs=[smem, smem] + [vmem] * len(blocks),
        out_specs=[vmem, vmem],
        out_shape=[
            jax.ShapeDtypeStruct((half, width), BF16),
            jax.ShapeDtypeStruct((half, half), F32),
        ],
        compiler_params=pltpu.CompilerParams(vmem_limit_bytes=STREAM_LIMIT),
        cost_estimate=pl.CostEstimate(
            flops=2 * half * half * width, bytes_accessed=4 * half * width, transcendentals=0
        ),
        name="near",
    )(me, kinds, *blocks)


def orthogonal_update(me, kinds, near, gram, kv_blocks, blocks, kv_rows):
    _, rows, width = blocks[0].shape
    half = near.shape[0]
    size = 2 * half
    gain = UPDATE_GAIN * math.sqrt(width)
    vmem = pl.BlockSpec(memory_space=pltpu.VMEM)
    smem = pl.BlockSpec(memory_space=pltpu.SMEM)
    like = lambda arrays: [jax.ShapeDtypeStruct(array.shape, BF16) for array in arrays]
    params = pltpu.CompilerParams(vmem_limit_bytes=VMEM_LIMIT)
    x, rest, lead, *far = pl.pallas_call(
        functools.partial(transform_kernel, gain, kv_rows),
        in_specs=[smem, smem] + [vmem] * (2 + 2 * len(blocks)),
        out_specs=[vmem] * (3 + len(blocks)),
        out_shape=[
            jax.ShapeDtypeStruct((size, width), BF16),
            jax.ShapeDtypeStruct((size, size), BF16),
            jax.ShapeDtypeStruct((size, 128), F32),
            *like(blocks),
        ],
        compiler_params=params,
        name="transform",
    )(me, kinds, near, gram, *kv_blocks, *blocks)
    near = pl.pallas_call(
        functools.partial(apply_kernel, gain, kv_rows),
        in_specs=[smem, smem] + [vmem] * 3,
        out_specs=[vmem] * len(blocks),
        out_shape=like(kv_blocks),
        compiler_params=params,
        name="apply",
    )(me, kinds, x, rest, lead)
    return list(near), far


def gather_kernel(rows, kv_rows, me, kinds, *refs):
    if kv_rows:
        blocks, (out, own, theirs) = refs[:-3], refs[-3:]
    else:
        blocks, out = refs[:-1], refs[-1]
    for index, block in enumerate(blocks):
        out[index] = block[1, :rows]
        if kv_rows:

            @pl.when(kinds[me[0] * len(blocks) + index] == 2)
            def _():
                for target, core in ((own, 0), (theirs, 1)):
                    target[0] = block[core, :kv_rows]
                    target[1] = block[core, kv_rows : 2 * kv_rows]


def gather_sibling(me, table, steps, blocks, rows, kv_rows):
    width = blocks[0].shape[2]
    kinds, _ = visits(table, [2 * step for step in steps])
    vmem = pl.BlockSpec(memory_space=pltpu.VMEM)
    smem = pl.BlockSpec(memory_space=pltpu.SMEM)
    kv = [jax.ShapeDtypeStruct((2, kv_rows, width), BF16)] * 2 if kv_rows else []
    return pl.pallas_call(
        functools.partial(gather_kernel, rows, kv_rows),
        in_specs=[smem, smem] + [vmem] * len(blocks),
        out_specs=[vmem] * (1 + len(kv)),
        out_shape=[jax.ShapeDtypeStruct((len(blocks), rows, width), BF16)] + kv,
        compiler_params=pltpu.CompilerParams(vmem_limit_bytes=STREAM_LIMIT),
        name="gather",
    )(me, kinds, *blocks)


def kv_kernel(devices, me, near, back, kw, ko, kb, ku):
    mine = (me[0] >= devices // 2).astype(jnp.int32)
    for index, update in ((mine, near[0]), (1 - mine, back[...])):
        value = kw[index] * (1.0 - RATE * DECAY) - RATE * update.astype(F32)
        ko[index] = value
        kb[index] = value.astype(BF16)
        ku[index] = update


def finish_kv(me, devices, near, back, kw):
    vmem = pl.BlockSpec(memory_space=pltpu.VMEM)
    return pl.pallas_call(
        functools.partial(kv_kernel, devices),
        in_specs=[pl.BlockSpec(memory_space=pltpu.SMEM)] + [vmem] * 3,
        out_specs=[vmem] * 3,
        out_shape=[jax.ShapeDtypeStruct(kw.shape, kind) for kind in (F32, BF16, BF16)],
        compiler_params=pltpu.CompilerParams(vmem_limit_bytes=STREAM_LIMIT),
        name="kv",
    )(me, near, back, kw)


def finish_kernel(plan, me, kinds, held, *refs):
    own, has_sibling, has_earlier, steps, idle = plan
    owns, refs = refs[:own], list(refs[own:])
    sibling = refs.pop(0) if has_sibling else None
    ew = refs.pop(0)
    earlier, (new_ref, low_ref, update_ref) = refs[:-3], refs[-3:]
    now = pl.program_id(0)

    if has_earlier and idle:
        first = me[0] * steps
        busy = sum((kinds[first + step] == 1).astype(jnp.int32) for step in range(steps))

        @pl.when(jnp.logical_and(now == 0, busy == 0))
        def _():
            for before, after in zip(earlier, refs[-3:]):
                pltpu.sync_copy(before.at[pl.ds(held[first], 1)], after)

    def apply(update):
        value = ew[0] * (1.0 - RATE * DECAY) - RATE * update.astype(F32)
        new_ref[0] = value
        low_ref[0] = value.astype(BF16)
        update_ref[0] = update

    valid = kinds[me[0] * steps + now] == 1
    for step, block in enumerate(owns):

        @pl.when(jnp.logical_and(now == step, valid))
        def _():
            apply(block[0, : ew.shape[1]])

    if has_sibling:

        @pl.when(jnp.logical_and(now >= own, valid))
        def _():
            apply(sibling[0])


def finish(me, table, ew, owns, own_steps, sibling, sibling_steps, earlier):
    _, rows, width = ew.shape
    steps = [2 * step for step in own_steps] + [2 * step + 1 for step in sibling_steps]
    kinds, held = visits(table, steps)
    idle = not (visit_tables(table, steps)[0] == 1).any(axis=1).all()
    size, own = len(steps), len(owns)
    block = (1, rows, width)
    spec = pl.BlockSpec(block, lambda i, me, k, h: (h[me[0] * size + i], 0, 0))
    operands = [me, kinds, held, *owns]
    in_specs = [
        pl.BlockSpec((1,) + array.shape[1:], lambda i, *_: (0, 0, 0)) for array in owns
    ]
    if sibling is not None:
        last = sibling.shape[0] - 1
        in_specs.append(pl.BlockSpec(block, lambda i, *_: (jnp.clip(i - own, 0, last), 0, 0)))
        operands.append(sibling)
    in_specs.append(spec)
    operands.append(ew)
    aliases = {}
    if earlier is not None:
        aliases = {len(operands) + index: index for index in range(3)}
        in_specs += [pl.BlockSpec(memory_space=pl.ANY)] * 3
        operands += list(earlier)
    return pl.pallas_call(
        functools.partial(
            finish_kernel, (own, sibling is not None, earlier is not None, size, idle)
        ),
        grid_spec=pltpu.PrefetchScalarGridSpec(
            num_scalar_prefetch=3,
            grid=(size,),
            in_specs=in_specs,
            out_specs=[spec] * 3,
        ),
        out_shape=[jax.ShapeDtypeStruct(ew.shape, kind) for kind in (F32, BF16, BF16)],
        input_output_aliases=aliases,
        compiler_params=pltpu.CompilerParams(vmem_limit_bytes=STREAM_LIMIT),
        name="finish",
    )(*operands)


def permute(array, pairs):
    return lax.ppermute(array, "fsdp", pairs)


def together(*arrays):
    return lax.optimization_barrier(arrays)


def block_pairs(table, step, to_owners):
    devices = table.shape[1]
    kinds = (1, 2) if 2 * step < devices // 2 else (1,)
    pairs = [(d ^ (2 * step), d) for d in range(devices) if table[0, d] in kinds]
    return pairs if to_owners else [(there, here) for here, there in pairs]


def shards(expert_grad, expert_momentum, expert_master, kv_grad, kv_momentum, kv_master):
    devices = lax.axis_size("fsdp")
    chips, half = devices // 2, devices // 4
    me = lax.axis_index("fsdp").reshape(1)
    shape = expert_grad.shape
    rows, width = shape[2], shape[3]
    kv_rows = kv_grad.shape[1]
    flat = lambda array: array.reshape(-1, rows, width)
    eg, em, ew = flat(expert_grad), flat(expert_momentum), flat(expert_master)
    table = owner_table(eg.shape[0], kv_grad.shape[0], devices)
    count = CLIP_RATIO * math.sqrt(devices * (expert_grad.size + kv_grad.size))
    cores = [(device, device ^ 1) for device in range(devices)]
    mirrors = [(device, device ^ chips) for device in range(devices)]
    near_steps, far_steps = list(range(half)), list(range(half, chips))

    partial, gv, mv, staged, keep, away = load(me, table, eg, em, kv_grad, kv_momentum)
    mirror = permute(away, mirrors)
    squares = lax.all_to_all(partial, "fsdp", 0, 0, tiled=True)
    squares, sibling, mirror = together(squares, permute(staged, cores), mirror)

    clip, *far = form_far(me, table, far_steps, squares, gv, mv, sibling, count)
    clip, far[0] = together(clip, far[0])
    kv_sibling = permute(jnp.stack([keep, mirror]), [pair for pair in cores if pair[1] % 2])
    near = form_near(
        me, table, near_steps, clip, gv, mv, sibling, kv_grad, kv_momentum, mirror, kv_sibling
    )
    near = list(near)
    far = [permute(block, block_pairs(table, step, True)) for step, block in zip(far_steps, far)]
    for step in near_steps[1:]:
        near[step] = permute(near[step], block_pairs(table, step, True))
    kinds = jnp.asarray(table[0])
    near_rows, near_product = near_gram(me, kinds, near, rows)

    near_rows, clip = together(near_rows, clip)
    factor = clip[0, 0]
    expert_moment_out = MOMENTUM * expert_momentum + factor * expert_grad
    kv_moment_out = MOMENTUM * kv_momentum + factor * kv_grad
    near_rows, expert_moment_out, kv_moment_out = together(
        near_rows, expert_moment_out, kv_moment_out
    )
    near, far = orthogonal_update(me, kinds, near_rows, near_product, near, far, kv_rows)

    far = [permute(block, block_pairs(table, step, False)) for step, block in zip(far_steps, far)]
    for step in near_steps[1:]:
        near[step] = permute(near[step], block_pairs(table, step, False))
    near_sibling, kv_own, kv_theirs = gather_sibling(me, table, near_steps, near, rows, kv_rows)
    near_sibling = permute(near_sibling, cores)
    kv_theirs = permute(kv_theirs, [pair for pair in cores if pair[0] % 2])
    kv_own = jnp.where(me[0] % 2 == 1, kv_own, kv_theirs)
    kv_back = permute(kv_own[1], mirrors)
    done = finish(me, table, ew, near, near_steps, None, [], None)
    far[0], *done = together(far[0], *done)
    far_sibling = permute(gather_sibling(me, table, far_steps, far, rows, 0)[0], cores)
    done = finish(me, table, ew, far, far_steps, near_sibling, near_steps, done)
    kv_back, *done = together(kv_back, *done)
    ko, kb, ku = finish_kv(me, devices, kv_own, kv_back, kv_master)
    eo, eb, eu = finish(me, table, ew, [], [], far_sibling, far_steps, done)
    return (
        eo.reshape(shape),
        expert_moment_out,
        eb.reshape(shape),
        eu.reshape(shape),
        ko,
        kv_moment_out,
        kb,
        ku,
    )


def solution(mesh):
    expert = P("groups", None, "fsdp", None)
    kv = P("groups", "fsdp", None)
    return jax.shard_map(
        shards,
        mesh=mesh,
        in_specs=(expert, expert, expert, kv, kv, kv),
        out_specs=(expert, expert, expert, expert, kv, kv, kv, kv),
        check_vma=False,
    )
```

```python
import functools
import math

import jax
import jax.numpy as jnp
import numpy as np
from jax import lax
from jax.experimental import pallas as pl
from jax.experimental.pallas import tpu as pltpu
from jax.sharding import PartitionSpec as P

NS_A = 3.4445
NS_B = -4.775
NS_C = 2.0315
MOMENTUM = 0.95
RATE = 0.02
DECAY = 0.1
NORM_EPS = 1e-07
CLIP_EPS = 1e-06
CLIP_RATIO = 0.5
UPDATE_GAIN = 0.2

F32 = jnp.float32
BF16 = jnp.bfloat16
VMEM_LIMIT = 40 * 1024 * 1024
LOAD_LIMIT = 42 * 1024 * 1024
STREAM_LIMIT = 16 * 1024 * 1024


def owner_table(experts, kvs, devices):
    table = np.zeros((2, devices), np.int32)
    chips = devices // 2
    first = min(experts, chips)
    for index in range(first):
        table[:, 2 * (index * chips // first)] = (1, index)
    by_parity = sorted(range(chips), key=lambda chip: bin(chip).count("1") % 2)
    for index in range(first, experts):
        table[:, 2 * by_parity[index - first] + 1] = (1, index)
    for index in range(kvs):
        low = index * devices // kvs
        free = [d for d in range(low, low + devices // kvs) if d % 2 and not table[0, d]]
        table[:, free[0]] = (2, index)
    return table


def near_owners(devices, flip):
    chips = devices // 4
    return [
        [2 * (device // (2 * chips) * chips + chip) + (device % 2 ^ flip) for chip in range(chips)]
        for device in range(devices)
    ]


def far_owners(devices, flip):
    steps = range(devices // 4, devices // 2)
    return [[device ^ (2 * step) ^ flip for step in steps] for device in range(devices)]


def visit_tables(table, owners):
    kinds = np.zeros((len(owners), len(owners[0])), np.int32)
    held = np.zeros_like(kinds)
    for device, row in enumerate(owners):
        experts = [table[1, owner] for owner in row if table[0, owner] == 1]
        last = experts[0] if experts else 0
        for place, owner in enumerate(row):
            kinds[device, place] = table[0, owner]
            last = table[1, owner] if table[0, owner] == 1 else last
            held[device, place] = last
    return kinds, held


def visits(table, owners):
    return tuple(jnp.asarray(part.reshape(-1)) for part in visit_tables(table, owners))


def joined(*parts):
    return [sum(rows, []) for rows in zip(*parts)]


def load_kernel(eg, em, kg, km, partial, gv, mv, kgv, kmv, total, sems, kv_sems):
    chunks = sems.shape[1]
    size = gv.shape[0] // chunks
    copies = [
        [
            pltpu.make_async_copy(
                source.at[pl.ds(chunk * size, size)],
                target.at[pl.ds(chunk * size, size)],
                sems.at[place, chunk],
            )
            for chunk in range(chunks)
        ]
        for place, (source, target) in enumerate(((eg, gv), (em, mv)))
    ]
    kv_copies = [
        pltpu.make_async_copy(source, target, kv_sems.at[place])
        for place, (source, target) in enumerate(((kg, kgv), (km, kmv)))
    ]
    for copy in kv_copies + copies[0] + copies[1]:
        copy.start()

    def fold(block):
        rows = block.reshape(-1, total.shape[0], block.shape[-1])
        return jnp.sum(rows * rows, axis=0)

    kv_copies[0].wait()
    total[...] = fold(kgv[...])
    for chunk in range(chunks):
        copies[0][chunk].wait()
        total[...] += fold(gv[chunk * size : (chunk + 1) * size])
    partial[...] = jnp.full(partial.shape, jnp.sum(total[...]), F32)
    kv_copies[1].wait()
    for copy in copies[1]:
        copy.wait()


def load(eg, em, kg, km, devices):
    vmem = pl.BlockSpec(memory_space=pltpu.VMEM)
    hbm = pl.BlockSpec(memory_space=pltpu.HBM)
    chunks = eg.shape[0] // 3
    rows = math.gcd(8, 3 * eg.shape[1], kg.shape[1])
    return pl.pallas_call(
        load_kernel,
        in_specs=[hbm] * 4,
        out_specs=[vmem] * 5,
        out_shape=[jax.ShapeDtypeStruct((devices, 8, 128), F32)]
        + [jax.ShapeDtypeStruct(array.shape, F32) for array in (eg, em, kg, km)],
        scratch_shapes=[
            pltpu.VMEM((rows, eg.shape[2]), F32),
            pltpu.SemaphoreType.DMA((2, chunks)),
            pltpu.SemaphoreType.DMA((2,)),
        ],
        compiler_params=pltpu.CompilerParams(vmem_limit_bytes=LOAD_LIMIT),
        name="load",
    )(eg, em, kg, km)


def stage_kernel(devices, me, held, gv, mv, kg, km, staged, keep, away):
    mine = (me[0] >= devices // 2).astype(jnp.int32)
    for out, index in ((keep, mine), (away, 1 - mine)):
        out[0] = kg[index].astype(BF16)
        out[1] = km[index].astype(BF16)
    chips = staged.shape[1]
    for step in range(chips):
        expert = held[me[0] * chips + step]
        staged[0, step] = gv[expert].astype(BF16)
        staged[1, step] = mv[expert].astype(BF16)


def stage(me, table, gv, mv, kg, km):
    _, rows, width = gv.shape
    devices = table.shape[1]
    _, held = visits(table, joined(near_owners(devices, 1), far_owners(devices, 1)))
    vmem = pl.BlockSpec(memory_space=pltpu.VMEM)
    smem = pl.BlockSpec(memory_space=pltpu.SMEM)
    kv = jax.ShapeDtypeStruct((2,) + kg.shape[1:], BF16)
    return pl.pallas_call(
        functools.partial(stage_kernel, devices),
        in_specs=[smem] * 2 + [vmem] * 4,
        out_specs=[vmem] * 3,
        out_shape=[jax.ShapeDtypeStruct((2, devices // 2, rows, width), BF16), kv, kv],
        compiler_params=pltpu.CompilerParams(vmem_limit_bytes=STREAM_LIMIT),
        name="stage",
    )(me, held, gv, mv, kg, km)


def nesterov(scale, grad, moment):
    clipped = scale * grad.astype(F32)
    return (clipped + MOMENTUM * (MOMENTUM * moment.astype(F32) + clipped)).astype(BF16)


def form_far_kernel(count, start, me, kinds, index, squares, gv, mv, sib, clip, *outs):
    total = jnp.sum(squares[...], axis=0)
    factor = jnp.minimum(1.0, count / (jnp.sqrt(total) + CLIP_EPS))
    clip[...] = factor
    scale = factor[0:1, 0:1]
    for step, out in enumerate(outs):
        place = me[0] * len(outs) + step

        @pl.when(kinds[place] == 1)
        def _():
            out[0] = nesterov(scale, gv[index[place]], mv[index[place]])
            out[1] = nesterov(scale, sib[0, start + step], sib[1, start + step])


def form_near_kernel(devices, me, kinds, index, clip, gv, mv, sib, kg, km, mirror, kv_sib, out):
    scale = clip[0:1, 0:1]
    rows, kv_rows = gv.shape[1], kg.shape[1]
    mine = (me[0] >= devices // 2).astype(jnp.int32)
    for step in range(out.shape[0]):
        place = me[0] * out.shape[0] + step

        @pl.when(kinds[place] == 1)
        def _():
            out[step, 0, :rows] = nesterov(scale, gv[index[place]], mv[index[place]])
            out[step, 1, :rows] = nesterov(scale, sib[0, step], sib[1, step])

        @pl.when(kinds[place] == 2)
        def _():
            for core, low, grad, moment in (
                (0, 0, kg[mine], km[mine]),
                (0, kv_rows, mirror[0], mirror[1]),
                (1, 0, kv_sib[0, 0], kv_sib[0, 1]),
                (1, kv_rows, kv_sib[1, 0], kv_sib[1, 1]),
            ):
                out[step, core, low : low + kv_rows] = nesterov(scale, grad, moment)


def form_call(kernel, name, table, owners, me, operands, outs):
    kinds, index = visits(table, owners)
    vmem = pl.BlockSpec(memory_space=pltpu.VMEM)
    smem = pl.BlockSpec(memory_space=pltpu.SMEM)
    return pl.pallas_call(
        kernel,
        in_specs=[smem] * 3 + [vmem] * len(operands),
        out_specs=[vmem] * len(outs),
        out_shape=outs,
        compiler_params=pltpu.CompilerParams(vmem_limit_bytes=STREAM_LIMIT),
        name=name,
    )(me, kinds, index, *operands)


def form_far(me, table, squares, gv, mv, sib, count):
    devices = table.shape[1]
    steps = devices // 4
    outs = [jax.ShapeDtypeStruct((8, 128), F32)]
    outs += [jax.ShapeDtypeStruct((2,) + gv.shape[1:], BF16)] * steps
    kernel = functools.partial(form_far_kernel, count, steps)
    owners = far_owners(devices, 0)
    return form_call(kernel, "far", table, owners, me, (squares, gv, mv, sib), outs)


def form_near(me, table, clip, gv, mv, sib, kg, km, mirror, kv_sib):
    _, rows, width = gv.shape
    devices = table.shape[1]
    outs = [
        jax.ShapeDtypeStruct((devices // 4, 2, max(rows, 2 * kg.shape[1]), width), BF16)
    ]
    operands = (clip, gv, mv, sib, kg, km, mirror, kv_sib)
    kernel = functools.partial(form_near_kernel, devices)
    return form_call(kernel, "form", table, near_owners(devices, 0), me, operands, outs)[0]


def dot(left, right):
    return jnp.dot(left, right, preferred_element_type=F32)


def apply_rows(gain, x, rest, lead, low, high, store):
    width = x.shape[1]
    chunk = 512 if width % 512 == 0 else width
    for start in range(0, width, chunk):
        part = x[low:high, start : start + chunk].astype(F32)
        value = lead[low:high, 0:1] * part + dot(rest[low:high], x[:, start : start + chunk])
        value = (gain * value.astype(BF16).astype(F32)).astype(BF16)
        store(start, chunk, value)


def outer(left, right):
    return lax.dot_general(left, right, (((1,), (1,)), ((), ())), preferred_element_type=F32)


def diagonal_blocks(size):
    step = 128 if size % 128 == 0 else size
    row = lax.broadcasted_iota(jnp.int32, (step, step), 0)
    col = lax.broadcasted_iota(jnp.int32, (step, step), 1)
    return row == col, [slice(low, low + step) for low in range(0, size, step)]


def transform(gram, rest, lead):
    size = gram.shape[0]
    mask, parts = diagonal_blocks(size)
    trace = sum(
        jnp.sum(jnp.where(mask, gram[part, part], 0.0), keepdims=True) for part in parts
    )
    inverse = 1.0 / (jnp.sqrt(trace) + NORM_EPS)
    scaled = gram[...] * (inverse * inverse)
    low = scaled.astype(BF16)
    first = (NS_B * low.astype(F32) + NS_C * dot(low, low)).astype(BF16)
    product = dot(first, low)
    scaled = (NS_A * NS_A) * scaled + (2.0 * NS_A) * product + dot(product.astype(BF16), first)
    low = scaled.astype(BF16)
    second = (NS_B * low.astype(F32) + NS_C * dot(low, low)).astype(BF16)
    mixed = NS_A * (first.astype(F32) + second.astype(F32)) + dot(second, first)
    gram[...] = mixed * inverse
    for part in parts:
        block = gram[part, part]
        main = jnp.sum(jnp.where(mask, block, 0.0), axis=1, keepdims=True)
        lead[part] = jnp.broadcast_to((NS_A * NS_A) * inverse + main, lead[part].shape)
        gram[part, part] = jnp.where(mask, 0.0, block)
    rest[...] = gram[...].astype(BF16)


def place_blocks(blocks, rows, x, start):
    for index, block in enumerate(blocks):
        for core in range(2):
            low = start + (2 * index + core) * rows
            x[low : low + rows] = block[core, :rows]


def store_blocks(outs, rows):
    def store(start, chunk, value):
        for index, out in enumerate(outs):
            for core in range(2):
                low = (2 * index + core) * rows
                out[core, :rows, start : start + chunk] = value[low : low + rows]

    return store


def split_blocks(ref):
    return [ref.at[index] for index in range(ref.shape[0])]


def near_kernel(rows, me, kinds, near, x, gram):
    @pl.when(kinds[me[0]] == 1)
    def _():
        place_blocks(split_blocks(near), rows, x, 0)
        gram[...] = outer(x[...], x[...])


def transform_kernel(gain, rows, kv_rows, me, kinds, near, near_rows, near_gram, *refs):
    steps = near.shape[0]
    far, (x, rest, lead), outs, gram = (
        refs[:steps], refs[steps : steps + 3], refs[steps + 3 : -1], refs[-1]
    )
    half = near_rows.shape[0]
    kind = kinds[me[0]]

    @pl.when(kind == 1)
    def _():
        x[:half] = near_rows[...]
        place_blocks(far, rows, x, half)
        gram[:half, :half] = near_gram[...]
        cross = outer(near_rows[...], x[half:])
        gram[:half, half:] = cross
        gram[half:, :half] = cross.T
        gram[half:, half:] = outer(x[half:], x[half:])
        transform(gram, rest, lead)
        apply_rows(gain, x, rest, lead, half, 2 * half, store_blocks(outs, rows))

    @pl.when(kind == 2)
    def _():
        size = 4 * kv_rows * steps
        place_blocks(split_blocks(near), 2 * kv_rows, x, 0)
        kv_gram = gram.at[:size, :size]
        kv_gram[...] = outer(x[:size], x[:size])
        transform(kv_gram, rest.at[:size, :size], lead.at[:size])


def apply_kernel(gain, rows, kv_rows, me, kinds, x, rest, lead, out):
    kind = kinds[me[0]]
    blocks = split_blocks(out)

    @pl.when(kind == 1)
    def _():
        apply_rows(gain, x, rest, lead, 0, x.shape[0] // 2, store_blocks(blocks, rows))

    @pl.when(kind == 2)
    def _():
        size = 4 * kv_rows * len(blocks)
        part = x.at[:size], rest.at[:size, :size], lead.at[:size]
        apply_rows(gain, *part, 0, size, store_blocks(blocks, 2 * kv_rows))


def near_product(me, kinds, near, rows):
    width = near.shape[3]
    half = 2 * near.shape[0] * rows
    vmem = pl.BlockSpec(memory_space=pltpu.VMEM)
    smem = pl.BlockSpec(memory_space=pltpu.SMEM)
    return pl.pallas_call(
        functools.partial(near_kernel, rows),
        in_specs=[smem, smem, vmem],
        out_specs=[vmem, vmem],
        out_shape=[
            jax.ShapeDtypeStruct((half, width), BF16),
            jax.ShapeDtypeStruct((half, half), F32),
        ],
        compiler_params=pltpu.CompilerParams(vmem_limit_bytes=STREAM_LIMIT),
        name="near",
    )(me, kinds, near)


def orthogonal_update(me, kinds, near, near_rows, near_gram, far, kv_rows):
    half, width = near_rows.shape
    size = 2 * half
    rows = far[0].shape[1]
    gain = UPDATE_GAIN * math.sqrt(width)
    vmem = pl.BlockSpec(memory_space=pltpu.VMEM)
    smem = pl.BlockSpec(memory_space=pltpu.SMEM)
    params = pltpu.CompilerParams(vmem_limit_bytes=VMEM_LIMIT)
    x, rest, lead, *back = pl.pallas_call(
        functools.partial(transform_kernel, gain, rows, kv_rows),
        in_specs=[smem, smem] + [vmem] * (3 + len(far)),
        out_specs=[vmem] * (3 + len(far)),
        out_shape=[
            jax.ShapeDtypeStruct((size, width), BF16),
            jax.ShapeDtypeStruct((size, size), BF16),
            jax.ShapeDtypeStruct((size, 128), F32),
        ]
        + [jax.ShapeDtypeStruct(block.shape, BF16) for block in far],
        scratch_shapes=[pltpu.VMEM((size, size), F32)],
        compiler_params=params,
        name="transform",
    )(me, kinds, near, near_rows, near_gram, *far)
    near = pl.pallas_call(
        functools.partial(apply_kernel, gain, rows, kv_rows),
        in_specs=[smem, smem] + [vmem] * 3,
        out_specs=vmem,
        out_shape=jax.ShapeDtypeStruct(near.shape, BF16),
        compiler_params=params,
        name="apply",
    )(me, kinds, x, rest, lead)
    return near, back


def gather_near_kernel(rows, kv_rows, me, kinds, near, out, own, theirs):
    for index, block in enumerate(split_blocks(near)):
        out[index] = block[1, :rows]

        @pl.when(kinds[me[0] * near.shape[0] + index] == 2)
        def _():
            for target, core in ((own, 0), (theirs, 1)):
                target[0] = block[core, :kv_rows]
                target[1] = block[core, kv_rows : 2 * kv_rows]


def gather_near(me, table, near, rows, kv_rows):
    steps, _, _, width = near.shape
    kinds, _ = visits(table, near_owners(table.shape[1], 0))
    vmem = pl.BlockSpec(memory_space=pltpu.VMEM)
    smem = pl.BlockSpec(memory_space=pltpu.SMEM)
    return pl.pallas_call(
        functools.partial(gather_near_kernel, rows, kv_rows),
        in_specs=[smem, smem, vmem],
        out_specs=[vmem] * 3,
        out_shape=[jax.ShapeDtypeStruct((steps, rows, width), BF16)]
        + [jax.ShapeDtypeStruct((2, kv_rows, width), BF16)] * 2,
        compiler_params=pltpu.CompilerParams(vmem_limit_bytes=STREAM_LIMIT),
        name="gathernear",
    )(me, kinds, near)


def gather_kernel(*refs):
    for index, block in enumerate(refs[:-1]):
        refs[-1][index] = block[1]


def gather_far(blocks):
    _, rows, width = blocks[0].shape
    vmem = pl.BlockSpec(memory_space=pltpu.VMEM)
    return pl.pallas_call(
        gather_kernel,
        in_specs=[vmem] * len(blocks),
        out_specs=vmem,
        out_shape=jax.ShapeDtypeStruct((len(blocks), rows, width), BF16),
        compiler_params=pltpu.CompilerParams(vmem_limit_bytes=STREAM_LIMIT),
        name="gather",
    )(*blocks)


def kv_kernel(devices, me, near, back, kw, ko, kb, ku):
    mine = (me[0] >= devices // 2).astype(jnp.int32)
    for index, update in ((mine, near[0]), (1 - mine, back[...])):
        value = kw[index] * (1.0 - RATE * DECAY) - RATE * update.astype(F32)
        ko[index] = value
        kb[index] = value.astype(BF16)
        ku[index] = update


def finish_kv(me, devices, near, back, kw):
    vmem = pl.BlockSpec(memory_space=pltpu.VMEM)
    return pl.pallas_call(
        functools.partial(kv_kernel, devices),
        in_specs=[pl.BlockSpec(memory_space=pltpu.SMEM)] + [vmem] * 3,
        out_specs=[vmem] * 3,
        out_shape=[jax.ShapeDtypeStruct(kw.shape, kind) for kind in (F32, BF16, BF16)],
        compiler_params=pltpu.CompilerParams(vmem_limit_bytes=STREAM_LIMIT),
        name="kv",
    )(me, near, back, kw)


def finish_kernel(plan, me, kinds, held, *refs):
    starts, has_earlier, steps, idle = plan
    sources, ew, refs = refs[: len(starts)], refs[len(starts)], refs[len(starts) + 1 :]
    earlier, (new_ref, low_ref, update_ref) = refs[:-3], refs[-3:]
    now = pl.program_id(0)

    if has_earlier and idle:
        first = me[0] * steps
        busy = sum((kinds[first + step] == 1).astype(jnp.int32) for step in range(steps))

        @pl.when(jnp.logical_and(now == 0, busy == 0))
        def _():
            for before, after in zip(earlier, refs[-3:]):
                pltpu.sync_copy(before.at[pl.ds(held[first], 1)], after)

    valid = kinds[me[0] * steps + now] == 1
    for source, (low, high) in zip(sources, starts):
        here = jnp.logical_and(now >= low, now < high)

        @pl.when(jnp.logical_and(here, valid))
        def _():
            update = source[0, 0, : ew.shape[1]]
            value = ew[0] * (1.0 - RATE * DECAY) - RATE * update.astype(F32)
            new_ref[0] = value
            low_ref[0] = value.astype(BF16)
            update_ref[0] = update


def finish(me, table, ew, sources, owners, earlier):
    _, rows, width = ew.shape
    owners = joined(*owners)
    kinds, held = visits(table, owners)
    idle = not (visit_tables(table, owners)[0] == 1).any(axis=1).all()
    size = len(owners[0])
    spec = pl.BlockSpec((1, rows, width), lambda i, me, k, h: (h[me[0] * size + i], 0, 0))
    operands, in_specs, starts = [me, kinds, held], [], []
    low = 0
    for source in sources:
        steps, _, source_rows, _ = source.shape
        in_specs.append(
            pl.BlockSpec(
                (1, 1, source_rows, width),
                lambda i, *_, low=low, steps=steps: (jnp.clip(i - low, 0, steps - 1), 0, 0, 0),
            )
        )
        operands.append(source)
        starts.append((low, low + steps))
        low += steps
    in_specs.append(spec)
    operands.append(ew)
    aliases = {}
    if earlier is not None:
        aliases = {len(operands) + index: index for index in range(3)}
        in_specs += [pl.BlockSpec(memory_space=pl.ANY)] * 3
        operands += list(earlier)
    return pl.pallas_call(
        functools.partial(finish_kernel, (starts, earlier is not None, size, idle)),
        grid_spec=pltpu.PrefetchScalarGridSpec(
            num_scalar_prefetch=3,
            grid=(size,),
            in_specs=in_specs,
            out_specs=[spec] * 3,
        ),
        out_shape=[jax.ShapeDtypeStruct(ew.shape, kind) for kind in (F32, BF16, BF16)],
        input_output_aliases=aliases,
        compiler_params=pltpu.CompilerParams(vmem_limit_bytes=STREAM_LIMIT),
        name="finish",
    )(*operands)


def permute(array, pairs):
    return lax.ppermute(array, "fsdp", pairs)


def together(*arrays):
    return lax.optimization_barrier(arrays)


def far_pairs(table, step, to_owners):
    devices = table.shape[1]
    pairs = [(d ^ (2 * step), d) for d in range(devices) if table[0, d] == 1]
    return pairs if to_owners else [(there, here) for here, there in pairs]


def exchange_near(blocks, devices):
    groups = [near_owners(devices, 0)[first] for first in (0, 1, devices // 2, devices // 2 + 1)]
    return lax.all_to_all(blocks, "fsdp", 0, 0, axis_index_groups=groups, tiled=True)


def shards(expert_grad, expert_momentum, expert_master, kv_grad, kv_momentum, kv_master):
    devices = lax.axis_size("fsdp")
    chips = devices // 2
    far_steps = range(chips // 2, chips)
    me = lax.axis_index("fsdp").reshape(1)
    shape = expert_grad.shape
    rows, width = shape[2], shape[3]
    kv_rows = kv_grad.shape[1]
    flat = lambda array: array.reshape(-1, rows, width)
    eg, em, ew = flat(expert_grad), flat(expert_momentum), flat(expert_master)
    table = owner_table(eg.shape[0], kv_grad.shape[0], devices)
    kinds = jnp.asarray(table[0])
    count = CLIP_RATIO * math.sqrt(devices * (expert_grad.size + kv_grad.size))
    cores = [(device, device ^ 1) for device in range(devices)]
    mirrors = [(device, device ^ chips) for device in range(devices)]
    near_own, near_other = near_owners(devices, 0), near_owners(devices, 1)
    far_own, far_other = far_owners(devices, 0), far_owners(devices, 1)

    partial, gv, mv, kg, km = load(eg, em, kv_grad, kv_momentum, devices)
    squares = lax.all_to_all(partial, "fsdp", 0, 0, tiled=True)
    staged, keep, away = stage(me, table, gv, mv, kg, km)
    mirror, sibling = permute(away, mirrors), permute(staged, cores)
    squares, sibling, mirror = together(squares, sibling, mirror)

    clip, *far = form_far(me, table, squares, gv, mv, sibling, count)
    clip, far[0] = together(clip, far[0])
    kv_sibling = permute(jnp.stack([keep, mirror]), [pair for pair in cores if pair[1] % 2])
    near = form_near(me, table, clip, gv, mv, sibling, kg, km, mirror, kv_sibling)
    far = [permute(block, far_pairs(table, step, True)) for step, block in zip(far_steps, far)]
    near = exchange_near(near, devices)

    near_rows, near_gram = near_product(me, kinds, near, rows)

    near_rows, clip = together(near_rows, clip)
    factor = clip[0, 0]
    expert_moment_out = MOMENTUM * expert_momentum + factor * expert_grad
    kv_moment_out = MOMENTUM * kv_momentum + factor * kv_grad
    near_rows, expert_moment_out, kv_moment_out = together(
        near_rows, expert_moment_out, kv_moment_out
    )
    near, far = orthogonal_update(me, kinds, near, near_rows, near_gram, far, kv_rows)

    far = [permute(block, far_pairs(table, step, False)) for step, block in zip(far_steps, far)]
    near = exchange_near(near, devices)
    near_sibling, kv_own, kv_theirs = gather_near(me, table, near, rows, kv_rows)
    near_sibling = permute(near_sibling, cores)
    kv_theirs = permute(kv_theirs, [pair for pair in cores if pair[0] % 2])
    kv_own = jnp.where(me[0] % 2 == 1, kv_own, kv_theirs)
    kv_back = permute(kv_own[1], mirrors)
    done = finish(me, table, ew, [near], [near_own], None)
    far[0], *done = together(far[0], *done)
    far_sibling = permute(gather_far(far), cores)
    sources = [block[None] for block in far] + [near_sibling[:, None]]
    done = finish(me, table, ew, sources, [far_own, near_other], done)
    kv_back, *done = together(kv_back, *done)
    ko, kb, ku = finish_kv(me, devices, kv_own, kv_back, kv_master)
    eo, eb, eu = finish(me, table, ew, [far_sibling[:, None]], [far_other], done)
    return (
        eo.reshape(shape),
        expert_moment_out,
        eb.reshape(shape),
        eu.reshape(shape),
        ko,
        kv_moment_out,
        kb,
        ku,
    )


def solution(mesh):
    expert = P("groups", None, "fsdp", None)
    kv = P("groups", "fsdp", None)
    return jax.shard_map(
        shards,
        mesh=mesh,
        in_specs=(expert, expert, expert, kv, kv, kv),
        out_specs=(expert, expert, expert, expert, kv, kv, kv, kv),
        check_vma=False,
    )
```

```python
import functools
import math

import jax
import jax.numpy as jnp
import numpy as np
from jax import lax
from jax.experimental import pallas as pl
from jax.experimental.pallas import tpu as pltpu
from jax.sharding import PartitionSpec as P

NS_A = 3.4445
NS_B = -4.775
NS_C = 2.0315
MOMENTUM = 0.95
RATE = 0.02
DECAY = 0.1
NORM_EPS = 1e-07
CLIP_EPS = 1e-06
CLIP_RATIO = 0.5
UPDATE_GAIN = 0.2

F32 = jnp.float32
BF16 = jnp.bfloat16
VMEM_LIMIT = 40 * 1024 * 1024
LOAD_LIMIT = 42 * 1024 * 1024
STREAM_LIMIT = 16 * 1024 * 1024


def owner_table(experts, kvs, devices):
    table = np.zeros((2, devices), np.int32)
    chips = devices // 2
    first = min(experts, chips)
    for index in range(first):
        table[:, 2 * (index * chips // first)] = (1, index)
    by_parity = sorted(range(chips), key=lambda chip: bin(chip).count("1") % 2)
    for index in range(first, experts):
        table[:, 2 * by_parity[index - first] + 1] = (1, index)
    for index in range(kvs):
        low = index * devices // kvs
        free = [d for d in range(low, low + devices // kvs) if d % 2 and not table[0, d]]
        table[:, free[0]] = (2, index)
    return table


def near_owners(devices, flip):
    chips = devices // 4
    return [
        [2 * (device // (2 * chips) * chips + chip) + (device % 2 ^ flip) for chip in range(chips)]
        for device in range(devices)
    ]


def far_owners(devices, flip):
    steps = range(devices // 4, devices // 2)
    return [[device ^ (2 * step) ^ flip for step in steps] for device in range(devices)]


def visit_tables(table, owners):
    kinds = np.zeros((len(owners), len(owners[0])), np.int32)
    held = np.zeros_like(kinds)
    for device, row in enumerate(owners):
        experts = [table[1, owner] for owner in row if table[0, owner] == 1]
        last = experts[0] if experts else 0
        for place, owner in enumerate(row):
            kinds[device, place] = table[0, owner]
            last = table[1, owner] if table[0, owner] == 1 else last
            held[device, place] = last
    return kinds, held


def visits(table, owners):
    return tuple(jnp.asarray(part.reshape(-1)) for part in visit_tables(table, owners))


def joined(*parts):
    return [sum(rows, []) for rows in zip(*parts)]


def fold(block, rows):
    parts = block.reshape(-1, rows, block.shape[-1])
    return jnp.sum(parts * parts, axis=0)


def load_kernel(eg, em, total, gv, mv, sems):
    chunks = sems.shape[1]
    size = gv.shape[0] // chunks
    copies = [
        [
            pltpu.make_async_copy(
                source.at[pl.ds(chunk * size, size)],
                target.at[pl.ds(chunk * size, size)],
                sems.at[place, chunk],
            )
            for chunk in range(chunks)
        ]
        for place, (source, target) in enumerate(((eg, gv), (em, mv)))
    ]
    for copy in copies[0] + copies[1]:
        copy.start()
    total[...] = jnp.zeros_like(total)
    for chunk in range(chunks):
        copies[0][chunk].wait()
        total[...] += fold(gv[chunk * size : (chunk + 1) * size], total.shape[0])
    for copy in copies[1]:
        copy.wait()


def load(eg, em):
    vmem = pl.BlockSpec(memory_space=pltpu.VMEM)
    hbm = pl.BlockSpec(memory_space=pltpu.HBM)
    chunks = eg.shape[0] // 3
    total = jax.ShapeDtypeStruct((math.gcd(8, 3 * eg.shape[1]), eg.shape[2]), F32)
    return pl.pallas_call(
        load_kernel,
        in_specs=[hbm] * 2,
        out_specs=[vmem] * 3,
        out_shape=[total] + [jax.ShapeDtypeStruct(eg.shape, F32)] * 2,
        scratch_shapes=[pltpu.SemaphoreType.DMA((2, chunks))],
        compiler_params=pltpu.CompilerParams(vmem_limit_bytes=LOAD_LIMIT),
        name="load",
    )(eg, em)


def stage_kernel(devices, me, held, total, gv, mv, kg, km, partial, staged, keep, away):
    squares = jnp.sum(total[...]) + jnp.sum(fold(kg[...], math.gcd(8, kg.shape[1])))
    partial[...] = jnp.full(partial.shape, squares, F32)
    mine = (me[0] >= devices // 2).astype(jnp.int32)
    for out, index in ((keep, mine), (away, 1 - mine)):
        out[0] = kg[index].astype(BF16)
        out[1] = km[index].astype(BF16)
    chips = staged.shape[1]
    for step in range(chips):
        expert = held[me[0] * chips + step]
        staged[0, step] = gv[expert].astype(BF16)
        staged[1, step] = mv[expert].astype(BF16)


def stage(me, table, total, gv, mv, kg, km):
    _, rows, width = gv.shape
    devices = table.shape[1]
    _, held = visits(table, joined(near_owners(devices, 1), far_owners(devices, 1)))
    vmem = pl.BlockSpec(memory_space=pltpu.VMEM)
    smem = pl.BlockSpec(memory_space=pltpu.SMEM)
    kv = jax.ShapeDtypeStruct((2,) + kg.shape[1:], BF16)
    return pl.pallas_call(
        functools.partial(stage_kernel, devices),
        in_specs=[smem] * 2 + [vmem] * 5,
        out_specs=[vmem] * 4,
        out_shape=[
            jax.ShapeDtypeStruct((devices, 8, 128), F32),
            jax.ShapeDtypeStruct((2, devices // 2, rows, width), BF16),
            kv,
            kv,
        ],
        compiler_params=pltpu.CompilerParams(vmem_limit_bytes=STREAM_LIMIT),
        name="stage",
    )(me, held, total, gv, mv, kg, km)


def nesterov(scale, grad, moment):
    clipped = scale * grad.astype(F32)
    return (clipped + MOMENTUM * (MOMENTUM * moment.astype(F32) + clipped)).astype(BF16)


def form_far_kernel(count, start, me, kinds, index, squares, gv, mv, sib, clip, *outs):
    total = jnp.sum(squares[...], axis=0)
    factor = jnp.minimum(1.0, count / (jnp.sqrt(total) + CLIP_EPS))
    clip[...] = factor
    scale = factor[0:1, 0:1]
    for step, out in enumerate(outs):
        place = me[0] * len(outs) + step

        @pl.when(kinds[place] == 1)
        def _():
            out[0] = nesterov(scale, gv[index[place]], mv[index[place]])
            out[1] = nesterov(scale, sib[0, start + step], sib[1, start + step])


def form_near_kernel(devices, me, kinds, index, clip, gv, mv, sib, kg, km, mirror, kv_sib, out):
    scale = clip[0:1, 0:1]
    rows, kv_rows = gv.shape[1], kg.shape[1]
    mine = (me[0] >= devices // 2).astype(jnp.int32)
    for step in range(out.shape[0]):
        place = me[0] * out.shape[0] + step

        @pl.when(kinds[place] == 1)
        def _():
            out[step, 0, :rows] = nesterov(scale, gv[index[place]], mv[index[place]])
            out[step, 1, :rows] = nesterov(scale, sib[0, step], sib[1, step])

        @pl.when(kinds[place] == 2)
        def _():
            for core, low, grad, moment in (
                (0, 0, kg[mine], km[mine]),
                (0, kv_rows, mirror[0], mirror[1]),
                (1, 0, kv_sib[0, 0], kv_sib[0, 1]),
                (1, kv_rows, kv_sib[1, 0], kv_sib[1, 1]),
            ):
                out[step, core, low : low + kv_rows] = nesterov(scale, grad, moment)


def form_call(kernel, name, table, owners, me, operands, outs):
    kinds, index = visits(table, owners)
    vmem = pl.BlockSpec(memory_space=pltpu.VMEM)
    smem = pl.BlockSpec(memory_space=pltpu.SMEM)
    return pl.pallas_call(
        kernel,
        in_specs=[smem] * 3 + [vmem] * len(operands),
        out_specs=[vmem] * len(outs),
        out_shape=outs,
        compiler_params=pltpu.CompilerParams(vmem_limit_bytes=STREAM_LIMIT),
        name=name,
    )(me, kinds, index, *operands)


def form_far(me, table, squares, gv, mv, sib, count):
    devices = table.shape[1]
    steps = devices // 4
    outs = [jax.ShapeDtypeStruct((8, 128), F32)]
    outs += [jax.ShapeDtypeStruct((2,) + gv.shape[1:], BF16)] * steps
    kernel = functools.partial(form_far_kernel, count, steps)
    owners = far_owners(devices, 0)
    return form_call(kernel, "far", table, owners, me, (squares, gv, mv, sib), outs)


def form_near(me, table, clip, gv, mv, sib, kg, km, mirror, kv_sib):
    _, rows, width = gv.shape
    devices = table.shape[1]
    outs = [
        jax.ShapeDtypeStruct((devices // 4, 2, max(rows, 2 * kg.shape[1]), width), BF16)
    ]
    operands = (clip, gv, mv, sib, kg, km, mirror, kv_sib)
    kernel = functools.partial(form_near_kernel, devices)
    return form_call(kernel, "form", table, near_owners(devices, 0), me, operands, outs)[0]


def dot(left, right):
    return jnp.dot(left, right, preferred_element_type=F32)


def apply_rows(gain, x, rest, lead, low, high, store):
    width = x.shape[1]
    chunk = 512 if width % 512 == 0 else width
    for start in range(0, width, chunk):
        part = x[low:high, start : start + chunk].astype(F32)
        value = lead[low:high, 0:1] * part + dot(rest[low:high], x[:, start : start + chunk])
        value = (gain * value.astype(BF16).astype(F32)).astype(BF16)
        store(start, chunk, value)


def outer(left, right):
    return lax.dot_general(left, right, (((1,), (1,)), ((), ())), preferred_element_type=F32)


def diagonal_blocks(size):
    step = 128 if size % 128 == 0 else size
    row = lax.broadcasted_iota(jnp.int32, (step, step), 0)
    col = lax.broadcasted_iota(jnp.int32, (step, step), 1)
    return row == col, [slice(low, low + step) for low in range(0, size, step)]


def transform(gram, rest, lead):
    size = gram.shape[0]
    mask, parts = diagonal_blocks(size)
    trace = sum(
        jnp.sum(jnp.where(mask, gram[part, part], 0.0), keepdims=True) for part in parts
    )
    inverse = 1.0 / (jnp.sqrt(trace) + NORM_EPS)
    scaled = gram[...] * (inverse * inverse)
    low = scaled.astype(BF16)
    first = (NS_B * low.astype(F32) + NS_C * dot(low, low)).astype(BF16)
    product = dot(first, low)
    scaled = (NS_A * NS_A) * scaled + (2.0 * NS_A) * product + dot(product.astype(BF16), first)
    low = scaled.astype(BF16)
    second = (NS_B * low.astype(F32) + NS_C * dot(low, low)).astype(BF16)
    mixed = NS_A * (first.astype(F32) + second.astype(F32)) + dot(second, first)
    gram[...] = mixed * inverse
    for part in parts:
        block = gram[part, part]
        main = jnp.sum(jnp.where(mask, block, 0.0), axis=1, keepdims=True)
        lead[part] = jnp.broadcast_to((NS_A * NS_A) * inverse + main, lead[part].shape)
        gram[part, part] = jnp.where(mask, 0.0, block)
    rest[...] = gram[...].astype(BF16)


def place_blocks(blocks, rows, x, start):
    for index, block in enumerate(blocks):
        for core in range(2):
            low = start + (2 * index + core) * rows
            x[low : low + rows] = block[core, :rows]


def store_blocks(outs, rows):
    def store(start, chunk, value):
        for index, out in enumerate(outs):
            for core in range(2):
                low = (2 * index + core) * rows
                out[core, :rows, start : start + chunk] = value[low : low + rows]

    return store


def split_blocks(ref):
    return [ref.at[index] for index in range(ref.shape[0])]


def far_kernel(me, kinds, *refs):
    blocks, (x, gram) = refs[:-2], refs[-2:]

    @pl.when(kinds[me[0]] == 1)
    def _():
        place_blocks(blocks, blocks[0].shape[1], x, 0)
        gram[...] = outer(x[...], x[...])


def transform_kernel(gain, rows, kv_rows, me, kinds, near, far, far_gram, x, rest, lead, *refs):
    outs, gram = refs[:-1], refs[-1]
    half = far.shape[0]
    kind = kinds[me[0]]

    @pl.when(kind == 1)
    def _():
        place_blocks(split_blocks(near), rows, x, 0)
        x[half:] = far[...]
        gram[:half, :half] = outer(x[:half], x[:half])
        cross = outer(x[:half], far[...])
        gram[:half, half:] = cross
        gram[half:, :half] = cross.T
        gram[half:, half:] = far_gram[...]
        transform(gram, rest, lead)
        apply_rows(gain, x, rest, lead, half, 2 * half, store_blocks(outs, rows))

    @pl.when(kind == 2)
    def _():
        size = 4 * kv_rows * near.shape[0]
        place_blocks(split_blocks(near), 2 * kv_rows, x, 0)
        kv_gram = gram.at[:size, :size]
        kv_gram[...] = outer(x[:size], x[:size])
        transform(kv_gram, rest.at[:size, :size], lead.at[:size])


def apply_kernel(gain, rows, kv_rows, me, kinds, x, rest, lead, out):
    kind = kinds[me[0]]
    blocks = split_blocks(out)

    @pl.when(kind == 1)
    def _():
        apply_rows(gain, x, rest, lead, 0, x.shape[0] // 2, store_blocks(blocks, rows))

    @pl.when(kind == 2)
    def _():
        size = 4 * kv_rows * len(blocks)
        part = x.at[:size], rest.at[:size, :size], lead.at[:size]
        apply_rows(gain, *part, 0, size, store_blocks(blocks, 2 * kv_rows))


def far_product(me, kinds, blocks):
    _, rows, width = blocks[0].shape
    half = 2 * len(blocks) * rows
    vmem = pl.BlockSpec(memory_space=pltpu.VMEM)
    smem = pl.BlockSpec(memory_space=pltpu.SMEM)
    return pl.pallas_call(
        far_kernel,
        in_specs=[smem, smem] + [vmem] * len(blocks),
        out_specs=[vmem, vmem],
        out_shape=[
            jax.ShapeDtypeStruct((half, width), BF16),
            jax.ShapeDtypeStruct((half, half), F32),
        ],
        compiler_params=pltpu.CompilerParams(vmem_limit_bytes=STREAM_LIMIT),
        name="product",
    )(me, kinds, *blocks)


def orthogonal_update(me, kinds, near, far, far_gram, rows, kv_rows):
    half, width = far.shape
    size = 2 * half
    steps = near.shape[0]
    gain = UPDATE_GAIN * math.sqrt(width)
    vmem = pl.BlockSpec(memory_space=pltpu.VMEM)
    smem = pl.BlockSpec(memory_space=pltpu.SMEM)
    params = pltpu.CompilerParams(vmem_limit_bytes=VMEM_LIMIT)
    x, rest, lead, *back = pl.pallas_call(
        functools.partial(transform_kernel, gain, rows, kv_rows),
        in_specs=[smem, smem] + [vmem] * 3,
        out_specs=[vmem] * (3 + steps),
        out_shape=[
            jax.ShapeDtypeStruct((size, width), BF16),
            jax.ShapeDtypeStruct((size, size), BF16),
            jax.ShapeDtypeStruct((size, 128), F32),
        ]
        + [jax.ShapeDtypeStruct((2, rows, width), BF16)] * steps,
        scratch_shapes=[pltpu.VMEM((size, size), F32)],
        compiler_params=params,
        name="transform",
    )(me, kinds, near, far, far_gram)
    near = pl.pallas_call(
        functools.partial(apply_kernel, gain, rows, kv_rows),
        in_specs=[smem, smem] + [vmem] * 3,
        out_specs=vmem,
        out_shape=jax.ShapeDtypeStruct(near.shape, BF16),
        compiler_params=params,
        name="apply",
    )(me, kinds, x, rest, lead)
    return near, back


def gather_kernel(rows, kv_rows, me, kinds, near, *refs):
    far, (out, kv, kv_mirror) = refs[:-3], refs[-3:]
    steps = near.shape[0]
    for index, block in enumerate(split_blocks(near)):
        out[index] = block[1, :rows]

        @pl.when(kinds[me[0] * steps + index] == 2)
        def _():
            for core in range(2):
                kv[core] = block[core, :kv_rows]
                kv_mirror[core] = block[core, kv_rows : 2 * kv_rows]

    for index, block in enumerate(far):
        out[steps + index] = block[1]


def gather(me, table, near, far, kv_rows):
    width = near.shape[3]
    rows = far[0].shape[1]
    kinds, _ = visits(table, near_owners(table.shape[1], 0))
    vmem = pl.BlockSpec(memory_space=pltpu.VMEM)
    smem = pl.BlockSpec(memory_space=pltpu.SMEM)
    return pl.pallas_call(
        functools.partial(gather_kernel, rows, kv_rows),
        in_specs=[smem, smem] + [vmem] * (1 + len(far)),
        out_specs=[vmem] * 3,
        out_shape=[jax.ShapeDtypeStruct((2 * len(far), rows, width), BF16)]
        + [jax.ShapeDtypeStruct((2, kv_rows, width), BF16)] * 2,
        compiler_params=pltpu.CompilerParams(vmem_limit_bytes=STREAM_LIMIT),
        name="gather",
    )(me, kinds, near, *far)


def kv_kernel(devices, me, kv, back, kv_sibling, back_sibling, kw, ko, kb, ku):
    mine = (me[0] >= devices // 2).astype(jnp.int32)

    def apply(index, update):
        value = kw[index] * (1.0 - RATE * DECAY) - RATE * update.astype(F32)
        ko[index] = value
        kb[index] = value.astype(BF16)
        ku[index] = update

    @pl.when(me[0] % 2 == 1)
    def _():
        apply(mine, kv[0])
        apply(1 - mine, back[0])

    @pl.when(me[0] % 2 == 0)
    def _():
        apply(mine, kv_sibling[...])
        apply(1 - mine, back_sibling[...])


def finish_kv(me, devices, sources, kw):
    vmem = pl.BlockSpec(memory_space=pltpu.VMEM)
    return pl.pallas_call(
        functools.partial(kv_kernel, devices),
        in_specs=[pl.BlockSpec(memory_space=pltpu.SMEM)] + [vmem] * 5,
        out_specs=[vmem] * 3,
        out_shape=[jax.ShapeDtypeStruct(kw.shape, kind) for kind in (F32, BF16, BF16)],
        compiler_params=pltpu.CompilerParams(vmem_limit_bytes=STREAM_LIMIT),
        name="kv",
    )(me, *sources, kw)


def finish_kernel(plan, me, kinds, held, *refs):
    starts, has_earlier, steps, idle = plan
    sources, ew, refs = refs[: len(starts)], refs[len(starts)], refs[len(starts) + 1 :]
    earlier, (new_ref, low_ref, update_ref) = refs[:-3], refs[-3:]
    now = pl.program_id(0)

    if has_earlier and idle:
        first = me[0] * steps
        busy = sum((kinds[first + step] == 1).astype(jnp.int32) for step in range(steps))

        @pl.when(jnp.logical_and(now == 0, busy == 0))
        def _():
            for before, after in zip(earlier, refs[-3:]):
                pltpu.sync_copy(before.at[pl.ds(held[first], 1)], after)

    valid = kinds[me[0] * steps + now] == 1
    for source, (low, high) in zip(sources, starts):
        here = jnp.logical_and(now >= low, now < high)

        @pl.when(jnp.logical_and(here, valid))
        def _():
            update = source[0, 0, : ew.shape[1]]
            value = ew[0] * (1.0 - RATE * DECAY) - RATE * update.astype(F32)
            new_ref[0] = value
            low_ref[0] = value.astype(BF16)
            update_ref[0] = update


def finish(me, table, ew, sources, owners, earlier):
    _, rows, width = ew.shape
    owners = joined(*owners)
    kinds, held = visits(table, owners)
    idle = not (visit_tables(table, owners)[0] == 1).any(axis=1).all()
    size = len(owners[0])
    spec = pl.BlockSpec((1, rows, width), lambda i, me, k, h: (h[me[0] * size + i], 0, 0))
    operands, in_specs, starts = [me, kinds, held], [], []
    low = 0
    for source in sources:
        steps, _, source_rows, _ = source.shape
        in_specs.append(
            pl.BlockSpec(
                (1, 1, source_rows, width),
                lambda i, *_, low=low, steps=steps: (jnp.clip(i - low, 0, steps - 1), 0, 0, 0),
            )
        )
        operands.append(source)
        starts.append((low, low + steps))
        low += steps
    in_specs.append(spec)
    operands.append(ew)
    aliases = {}
    if earlier is not None:
        aliases = {len(operands) + index: index for index in range(3)}
        in_specs += [pl.BlockSpec(memory_space=pl.ANY)] * 3
        operands += list(earlier)
    return pl.pallas_call(
        functools.partial(finish_kernel, (starts, earlier is not None, size, idle)),
        grid_spec=pltpu.PrefetchScalarGridSpec(
            num_scalar_prefetch=3,
            grid=(size,),
            in_specs=in_specs,
            out_specs=[spec] * 3,
        ),
        out_shape=[jax.ShapeDtypeStruct(ew.shape, kind) for kind in (F32, BF16, BF16)],
        input_output_aliases=aliases,
        compiler_params=pltpu.CompilerParams(vmem_limit_bytes=STREAM_LIMIT),
        name="finish",
    )(*operands)


def permute(array, pairs):
    return lax.ppermute(array, "fsdp", pairs)


def together(*arrays):
    return lax.optimization_barrier(arrays)


def far_pairs(table, step, to_owners):
    devices = table.shape[1]
    pairs = [(d ^ (2 * step), d) for d in range(devices) if table[0, d] == 1]
    return pairs if to_owners else [(there, here) for here, there in pairs]


def exchange_near(blocks, devices):
    groups = [near_owners(devices, 0)[first] for first in (0, 1, devices // 2, devices // 2 + 1)]
    return lax.all_to_all(blocks, "fsdp", 0, 0, axis_index_groups=groups, tiled=True)


def shards(expert_grad, expert_momentum, expert_master, kv_grad, kv_momentum, kv_master):
    devices = lax.axis_size("fsdp")
    chips = devices // 2
    far_steps = range(chips // 2, chips)
    me = lax.axis_index("fsdp").reshape(1)
    shape = expert_grad.shape
    rows, width = shape[2], shape[3]
    kv_rows = kv_grad.shape[1]
    flat = lambda array: array.reshape(-1, rows, width)
    eg, em, ew = flat(expert_grad), flat(expert_momentum), flat(expert_master)
    table = owner_table(eg.shape[0], kv_grad.shape[0], devices)
    kinds = jnp.asarray(table[0])
    count = CLIP_RATIO * math.sqrt(devices * (expert_grad.size + kv_grad.size))
    cores = [(device, device ^ 1) for device in range(devices)]
    mirrors = [(device, device ^ chips) for device in range(devices)]
    near_own, near_other = near_owners(devices, 0), near_owners(devices, 1)
    far_own, far_other = far_owners(devices, 0), far_owners(devices, 1)

    total, gv, mv = load(eg, em)
    partial, staged, keep, away = stage(me, table, total, gv, mv, kv_grad, kv_momentum)
    squares = lax.all_to_all(partial, "fsdp", 0, 0, tiled=True)
    mirror, sibling = permute(away, mirrors), permute(staged, cores)
    squares, sibling, mirror = together(squares, sibling, mirror)

    clip, *far = form_far(me, table, squares, gv, mv, sibling, count)
    clip, far[0], keep = together(clip, far[0], keep)
    kv_sibling = permute(jnp.stack([keep, mirror]), [pair for pair in cores if pair[1] % 2])
    near = form_near(
        me, table, clip, gv, mv, sibling, kv_grad, kv_momentum, mirror, kv_sibling
    )
    far = [permute(block, far_pairs(table, step, True)) for step, block in zip(far_steps, far)]
    clip, near = together(clip, near)
    near = exchange_near(near, devices)

    factor = clip[0, 0]
    expert_moment_out = MOMENTUM * expert_momentum + factor * expert_grad
    kv_moment_out = MOMENTUM * kv_momentum + factor * kv_grad
    far[0], expert_moment_out, kv_moment_out = together(
        far[0], expert_moment_out, kv_moment_out
    )
    far, far_gram = far_product(me, kinds, far)
    near, far = orthogonal_update(me, kinds, near, far, far_gram, rows, kv_rows)

    far = [permute(block, far_pairs(table, step, False)) for step, block in zip(far_steps, far)]
    near = exchange_near(near, devices)
    others, kv, kv_mirror = gather(me, table, near, far, kv_rows)
    others = permute(others, cores)
    odd_mirrors = [pair for pair in mirrors if pair[0] % 2]
    down = [pair for pair in cores if pair[0] % 2]
    kv_back = permute(kv_mirror, odd_mirrors)
    sources = [near] + [block[None] for block in far]
    done = finish(me, table, ew, sources, [near_own, far_own], None)
    kv_back, *done = together(kv_back, *done)
    kv_sources = (kv, kv_back, permute(kv[1], down), permute(kv_back[1], down))
    eo, eb, eu = finish(me, table, ew, [others[:, None]], [near_other, far_other], done)
    ko, kb, ku = finish_kv(me, devices, kv_sources, kv_master)
    return (
        eo.reshape(shape),
        expert_moment_out,
        eb.reshape(shape),
        eu.reshape(shape),
        ko,
        kv_moment_out,
        kb,
        ku,
    )


def solution(mesh):
    expert = P("groups", None, "fsdp", None)
    kv = P("groups", "fsdp", None)
    return jax.shard_map(
        shards,
        mesh=mesh,
        in_specs=(expert, expert, expert, kv, kv, kv),
        out_specs=(expert, expert, expert, expert, kv, kv, kv, kv),
        check_vma=False,
    )
```

```python
import functools
import math

import jax
import jax.numpy as jnp
import numpy as np
from jax import lax
from jax.experimental import pallas as pl
from jax.experimental.pallas import tpu as pltpu
from jax.sharding import PartitionSpec as P

NS_A = 3.4445
NS_B = -4.775
NS_C = 2.0315
MOMENTUM = 0.95
RATE = 0.02
DECAY = 0.1
NORM_EPS = 1e-07
CLIP_EPS = 1e-06
CLIP_RATIO = 0.5
UPDATE_GAIN = 0.2

F32 = jnp.float32
BF16 = jnp.bfloat16
VMEM_LIMIT = 40 * 1024 * 1024
LOAD_LIMIT = 42 * 1024 * 1024
STREAM_LIMIT = 16 * 1024 * 1024


def owner_table(experts, kvs, devices):
    table = np.zeros((2, devices), np.int32)
    chips = devices // 2
    first = min(experts, chips)
    for index in range(first):
        table[:, 2 * (index * chips // first)] = (1, index)
    by_parity = sorted(range(chips), key=lambda chip: bin(chip % (chips // 2)).count("1") % 2)
    for index in range(first, experts):
        table[:, 2 * by_parity[index - first] + 1] = (1, index)
    slot = kv_slot(table)
    for index in range(kvs):
        table[:, index * chips + slot] = (2, index)
    return table


def kv_slot(table):
    chips = table.shape[1] // 2
    free = (table[0, :chips] != 1) & (table[0, chips:] != 1)
    return next(slot for slot in range(1, chips, 2) if free[slot])


def near_owners(devices):
    half = devices // 2
    return [[device // half * half + other for other in range(half)] for device in range(devices)]


def far_owners(devices, flip):
    steps = range(devices // 4, devices // 2)
    return [[device ^ (2 * step) ^ flip for step in steps] for device in range(devices)]


class Plan:
    def __init__(self, table):
        self.table = table
        self.parts = []

    def section(self, owners):
        place = sum(part.size for part in self.parts)
        part = np.zeros((len(owners), 2, len(owners[0])), np.int32)
        for device, row in enumerate(owners):
            experts = [self.table[1, owner] for owner in row if self.table[0, owner] == 1]
            last = experts[0] if experts else 0
            for step, owner in enumerate(row):
                last = self.table[1, owner] if self.table[0, owner] == 1 else last
                part[device, :, step] = self.table[0, owner], last
        self.parts.append(part)
        idle = not (part[:, 0] == 1).any(axis=1).all()
        return place, part.shape[2], idle

    def array(self):
        return jnp.asarray(np.concatenate([part.reshape(-1) for part in self.parts]))


def kind_at(section, me, plan, step):
    return plan[section[0] + me[0] * 2 * section[1] + step]


def expert_at(section, me, plan, step):
    return plan[section[0] + (me[0] * 2 + 1) * section[1] + step]


def fold(block, rows):
    parts = block.reshape(-1, rows, block.shape[-1])
    return jnp.sum(parts * parts, axis=0)


def load_kernel(eg, em, total, gv, mv, sems):
    chunks = sems.shape[1]
    size = gv.shape[0] // chunks
    copies = [
        [
            pltpu.make_async_copy(
                source.at[pl.ds(chunk * size, size)],
                target.at[pl.ds(chunk * size, size)],
                sems.at[place, chunk],
            )
            for chunk in range(chunks)
        ]
        for place, (source, target) in enumerate(((eg, gv), (em, mv)))
    ]
    for copy in copies[0] + copies[1]:
        copy.start()
    total[...] = jnp.zeros_like(total)
    for chunk in range(chunks):
        copies[0][chunk].wait()
        total[...] += fold(gv[chunk * size : (chunk + 1) * size], total.shape[0])
    for copy in copies[1]:
        copy.wait()


def load(eg, em):
    vmem = pl.BlockSpec(memory_space=pltpu.VMEM)
    hbm = pl.BlockSpec(memory_space=pltpu.HBM)
    chunks = eg.shape[0] // 3
    total = jax.ShapeDtypeStruct((math.gcd(8, 3 * eg.shape[1]), eg.shape[2]), F32)
    return pl.pallas_call(
        load_kernel,
        in_specs=[hbm] * 2,
        out_specs=[vmem] * 3,
        out_shape=[total] + [jax.ShapeDtypeStruct(eg.shape, F32)] * 2,
        scratch_shapes=[pltpu.SemaphoreType.DMA((2, chunks))],
        compiler_params=pltpu.CompilerParams(vmem_limit_bytes=LOAD_LIMIT),
        name="load",
    )(eg, em)


def stage_kernel(section, devices, me, plan, total, gv, mv, kg, km, partial, staged, away):
    squares = jnp.sum(total[...]) + jnp.sum(fold(kg[...], math.gcd(8, kg.shape[1])))
    partial[...] = jnp.full(partial.shape, squares, F32)
    other = (me[0] < devices // 2).astype(jnp.int32)
    away[0] = kg[other].astype(BF16)
    away[1] = km[other].astype(BF16)
    for step in range(staged.shape[1]):
        expert = expert_at(section, me, plan, step)
        staged[0, step] = gv[expert].astype(BF16)
        staged[1, step] = mv[expert].astype(BF16)


def stage(section, devices, me, plan, total, gv, mv, kg, km):
    _, rows, width = gv.shape
    vmem = pl.BlockSpec(memory_space=pltpu.VMEM)
    smem = pl.BlockSpec(memory_space=pltpu.SMEM)
    return pl.pallas_call(
        functools.partial(stage_kernel, section, devices),
        in_specs=[smem] * 2 + [vmem] * 5,
        out_specs=[vmem] * 3,
        out_shape=[
            jax.ShapeDtypeStruct((devices, 8, 128), F32),
            jax.ShapeDtypeStruct((2, section[1], rows, width), BF16),
            jax.ShapeDtypeStruct((2,) + kg.shape[1:], BF16),
        ],
        compiler_params=pltpu.CompilerParams(vmem_limit_bytes=STREAM_LIMIT),
        name="stage",
    )(me, plan, total, gv, mv, kg, km)


def nesterov(scale, grad, moment):
    clipped = scale * grad.astype(F32)
    return (clipped + MOMENTUM * (MOMENTUM * moment.astype(F32) + clipped)).astype(BF16)


def form_far_kernel(section, count, me, plan, squares, gv, mv, sib, clip, *outs):
    total = jnp.sum(squares[...], axis=0)
    factor = jnp.minimum(1.0, count / (jnp.sqrt(total) + CLIP_EPS))
    clip[...] = factor
    scale = factor[0:1, 0:1]
    for step, out in enumerate(outs):

        @pl.when(kind_at(section, me, plan, step) == 1)
        def _():
            expert = expert_at(section, me, plan, step)
            out[0] = nesterov(scale, gv[expert], mv[expert])
            out[1] = nesterov(scale, sib[0, step], sib[1, step])


def form_far(section, me, plan, squares, gv, mv, sib, count):
    vmem = pl.BlockSpec(memory_space=pltpu.VMEM)
    smem = pl.BlockSpec(memory_space=pltpu.SMEM)
    return pl.pallas_call(
        functools.partial(form_far_kernel, section, count),
        in_specs=[smem] * 2 + [vmem] * 4,
        out_specs=[vmem] * (1 + section[1]),
        out_shape=[jax.ShapeDtypeStruct((8, 128), F32)]
        + [jax.ShapeDtypeStruct((2,) + gv.shape[1:], BF16)] * section[1],
        compiler_params=pltpu.CompilerParams(vmem_limit_bytes=STREAM_LIMIT),
        name="far",
    )(me, plan, squares, gv, mv, sib)


def form_near_kernel(section, me, plan, clip, gv, mv, kg, km, mirror, out):
    scale = clip[0:1, 0:1]
    rows, kv_rows = gv.shape[1], kg.shape[1]
    mine = (me[0] >= section[1]).astype(jnp.int32)
    for step in range(section[1]):
        kind = kind_at(section, me, plan, step)

        @pl.when(kind == 1)
        def _():
            expert = expert_at(section, me, plan, step)
            out[step, :rows] = nesterov(scale, gv[expert], mv[expert])

        @pl.when(kind == 2)
        def _():
            out[step, :kv_rows] = nesterov(scale, kg[mine], km[mine])
            out[step, kv_rows : 2 * kv_rows] = nesterov(scale, mirror[0], mirror[1])


def form_near(section, me, plan, clip, gv, mv, kg, km, mirror):
    _, rows, width = gv.shape
    vmem = pl.BlockSpec(memory_space=pltpu.VMEM)
    smem = pl.BlockSpec(memory_space=pltpu.SMEM)
    return pl.pallas_call(
        functools.partial(form_near_kernel, section),
        in_specs=[smem] * 2 + [vmem] * 6,
        out_specs=vmem,
        out_shape=jax.ShapeDtypeStruct(
            (section[1], max(rows, 2 * kg.shape[1]), width), BF16
        ),
        compiler_params=pltpu.CompilerParams(vmem_limit_bytes=STREAM_LIMIT),
        name="form",
    )(me, plan, clip, gv, mv, kg, km, mirror)


def dot(left, right):
    return jnp.dot(left, right, preferred_element_type=F32)


def apply_rows(gain, x, rest, lead, low, high, store):
    width = x.shape[1]
    chunk = 512 if width % 512 == 0 else width
    for start in range(0, width, chunk):
        part = x[low:high, start : start + chunk].astype(F32)
        value = lead[low:high, 0:1] * part + dot(rest[low:high], x[:, start : start + chunk])
        value = (gain * value.astype(BF16).astype(F32)).astype(BF16)
        store(start, chunk, value)


def outer(left, right):
    return lax.dot_general(left, right, (((1,), (1,)), ((), ())), preferred_element_type=F32)


def diagonal_blocks(size):
    step = 128 if size % 128 == 0 else size
    row = lax.broadcasted_iota(jnp.int32, (step, step), 0)
    col = lax.broadcasted_iota(jnp.int32, (step, step), 1)
    return row == col, [slice(low, low + step) for low in range(0, size, step)]


def transform(gram, rest, lead):
    size = gram.shape[0]
    mask, parts = diagonal_blocks(size)
    trace = sum(
        jnp.sum(jnp.where(mask, gram[part, part], 0.0), keepdims=True) for part in parts
    )
    inverse = 1.0 / (jnp.sqrt(trace) + NORM_EPS)
    scaled = gram[...] * (inverse * inverse)
    low = scaled.astype(BF16)
    first = (NS_B * low.astype(F32) + NS_C * dot(low, low)).astype(BF16)
    product = dot(first, low)
    scaled = (NS_A * NS_A) * scaled + (2.0 * NS_A) * product + dot(product.astype(BF16), first)
    low = scaled.astype(BF16)
    second = (NS_B * low.astype(F32) + NS_C * dot(low, low)).astype(BF16)
    mixed = NS_A * (first.astype(F32) + second.astype(F32)) + dot(second, first)
    gram[...] = mixed * inverse
    for part in parts:
        block = gram[part, part]
        main = jnp.sum(jnp.where(mask, block, 0.0), axis=1, keepdims=True)
        lead[part] = jnp.broadcast_to((NS_A * NS_A) * inverse + main, lead[part].shape)
        gram[part, part] = jnp.where(mask, 0.0, block)
    rest[...] = gram[...].astype(BF16)


def place_far(blocks, x, start):
    rows = blocks[0].shape[1]
    for index, block in enumerate(blocks):
        for core in range(2):
            low = start + (2 * index + core) * rows
            x[low : low + rows] = block[core]


def place_near(blocks, rows, x):
    for index in range(blocks.shape[0]):
        x[index * rows : (index + 1) * rows] = blocks[index, :rows]


def store_far(outs):
    rows = outs[0].shape[1]

    def store(start, chunk, value):
        for index, out in enumerate(outs):
            for core in range(2):
                low = (2 * index + core) * rows
                out[core, :, start : start + chunk] = value[low : low + rows]

    return store


def store_near(out, rows):
    def store(start, chunk, value):
        for index in range(out.shape[0]):
            part = value[index * rows : (index + 1) * rows]
            out[index, :rows, start : start + chunk] = part

    return store


def near_kernel(owns, rows, me, plan, near, x, gram):
    @pl.when(kind_at(owns, me, plan, 0) == 1)
    def _():
        place_near(near, rows, x)
        gram[...] = outer(x[...], x[...])


def transform_kernel(owns, gain, kv_rows, me, plan, near, near_rows, near_gram, *refs):
    steps = (len(refs) - 4) // 2
    far, (x, rest, lead) = refs[:steps], refs[steps : steps + 3]
    outs, gram = refs[steps + 3 : -1], refs[-1]
    half = near_rows.shape[0]
    kind = kind_at(owns, me, plan, 0)

    @pl.when(kind == 1)
    def _():
        x[:half] = near_rows[...]
        place_far(far, x, half)
        gram[:half, :half] = near_gram[...]
        cross = outer(near_rows[...], x[half:])
        gram[:half, half:] = cross
        gram[half:, :half] = cross.T
        gram[half:, half:] = outer(x[half:], x[half:])
        transform(gram, rest, lead)
        apply_rows(gain, x, rest, lead, half, 2 * half, store_far(outs))

    @pl.when(kind == 2)
    def _():
        size = 2 * kv_rows * near.shape[0]
        place_near(near, 2 * kv_rows, x)
        kv_gram = gram.at[:size, :size]
        kv_gram[...] = outer(x[:size], x[:size])
        transform(kv_gram, rest.at[:size, :size], lead.at[:size])


def apply_kernel(owns, gain, rows, kv_rows, me, plan, x, rest, lead, out):
    kind = kind_at(owns, me, plan, 0)

    @pl.when(kind == 1)
    def _():
        apply_rows(gain, x, rest, lead, 0, x.shape[0] // 2, store_near(out, rows))

    @pl.when(kind == 2)
    def _():
        size = 2 * kv_rows * out.shape[0]
        part = x.at[:size], rest.at[:size, :size], lead.at[:size]
        apply_rows(gain, *part, 0, size, store_near(out, 2 * kv_rows))


def near_product(owns, me, plan, near, rows):
    half, width = near.shape[0] * rows, near.shape[2]
    vmem = pl.BlockSpec(memory_space=pltpu.VMEM)
    smem = pl.BlockSpec(memory_space=pltpu.SMEM)
    return pl.pallas_call(
        functools.partial(near_kernel, owns, rows),
        in_specs=[smem, smem, vmem],
        out_specs=[vmem, vmem],
        out_shape=[
            jax.ShapeDtypeStruct((half, width), BF16),
            jax.ShapeDtypeStruct((half, half), F32),
        ],
        compiler_params=pltpu.CompilerParams(vmem_limit_bytes=STREAM_LIMIT),
        name="near",
    )(me, plan, near)


def orthogonal_update(owns, me, plan, near, near_rows, near_gram, far, kv_rows):
    half, width = near_rows.shape
    size = 2 * half
    rows = far[0].shape[1]
    gain = UPDATE_GAIN * math.sqrt(width)
    vmem = pl.BlockSpec(memory_space=pltpu.VMEM)
    smem = pl.BlockSpec(memory_space=pltpu.SMEM)
    params = pltpu.CompilerParams(vmem_limit_bytes=VMEM_LIMIT)
    x, rest, lead, *back = pl.pallas_call(
        functools.partial(transform_kernel, owns, gain, kv_rows),
        in_specs=[smem, smem] + [vmem] * (3 + len(far)),
        out_specs=[vmem] * (3 + len(far)),
        out_shape=[
            jax.ShapeDtypeStruct((size, width), BF16),
            jax.ShapeDtypeStruct((size, size), BF16),
            jax.ShapeDtypeStruct((size, 128), F32),
        ]
        + [jax.ShapeDtypeStruct(block.shape, BF16) for block in far],
        scratch_shapes=[pltpu.VMEM((size, size), F32)],
        compiler_params=params,
        name="transform",
    )(me, plan, near, near_rows, near_gram, *far)
    near = pl.pallas_call(
        functools.partial(apply_kernel, owns, gain, rows, kv_rows),
        in_specs=[smem, smem] + [vmem] * 3,
        out_specs=vmem,
        out_shape=jax.ShapeDtypeStruct(near.shape, BF16),
        compiler_params=params,
        name="apply",
    )(me, plan, x, rest, lead)
    return near, back


def gather_kernel(*refs):
    for index, block in enumerate(refs[:-1]):
        refs[-1][index] = block[1]


def gather_far(blocks):
    _, rows, width = blocks[0].shape
    vmem = pl.BlockSpec(memory_space=pltpu.VMEM)
    return pl.pallas_call(
        gather_kernel,
        in_specs=[vmem] * len(blocks),
        out_specs=vmem,
        out_shape=jax.ShapeDtypeStruct((len(blocks), rows, width), BF16),
        compiler_params=pltpu.CompilerParams(vmem_limit_bytes=STREAM_LIMIT),
        name="gather",
    )(*blocks)


def kv_kernel(devices, me, kv, back, kw, ko, kb, ku):
    mine = (me[0] >= devices // 2).astype(jnp.int32)
    for index, update in ((mine, kv[0, : kw.shape[1]]), (1 - mine, back[...])):
        value = kw[index] * (1.0 - RATE * DECAY) - RATE * update.astype(F32)
        ko[index] = value
        kb[index] = value.astype(BF16)
        ku[index] = update


def finish_kv(me, devices, near, slot, back, kw):
    whole = lambda array: pl.BlockSpec(array.shape, lambda i: (0,) * array.ndim)
    return pl.pallas_call(
        functools.partial(kv_kernel, devices),
        grid=(1,),
        in_specs=[
            pl.BlockSpec(memory_space=pltpu.SMEM),
            pl.BlockSpec((1,) + near.shape[1:], lambda i: (slot, 0, 0)),
            whole(back),
            whole(kw),
        ],
        out_specs=[whole(kw)] * 3,
        out_shape=[jax.ShapeDtypeStruct(kw.shape, kind) for kind in (F32, BF16, BF16)],
        compiler_params=pltpu.CompilerParams(vmem_limit_bytes=STREAM_LIMIT),
        name="kv",
    )(me, near, back, kw)


def finish_kernel(section, starts, me, plan, *refs):
    _, steps, idle = section
    sources, ew, refs = refs[: len(starts)], refs[len(starts)], refs[len(starts) + 1 :]
    earlier, (new_ref, low_ref, update_ref) = refs[:-3], refs[-3:]
    now = pl.program_id(0)

    if earlier and idle:
        kinds = [kind_at(section, me, plan, step) for step in range(steps)]
        busy = sum((kind == 1).astype(jnp.int32) for kind in kinds)

        @pl.when(jnp.logical_and(now == 0, busy == 0))
        def _():
            block = pl.ds(expert_at(section, me, plan, 0), 1)
            for before, after in zip(earlier, refs[-3:]):
                pltpu.sync_copy(before.at[block], after)

    valid = kind_at(section, me, plan, now) == 1
    for source, (low, high) in zip(sources, starts):
        here = jnp.logical_and(now >= low, now < high)

        @pl.when(jnp.logical_and(here, valid))
        def _():
            update = source[0, 0, : ew.shape[1]]
            value = ew[0] * (1.0 - RATE * DECAY) - RATE * update.astype(F32)
            new_ref[0] = value
            low_ref[0] = value.astype(BF16)
            update_ref[0] = update


def finish(section, me, plan, ew, sources, earlier):
    _, rows, width = ew.shape
    spec = pl.BlockSpec(
        (1, rows, width), lambda i, me, plan: (expert_at(section, me, plan, i), 0, 0)
    )
    operands, in_specs, starts = [me, plan], [], []
    low = 0
    for source in sources:
        steps, _, source_rows, _ = source.shape
        in_specs.append(
            pl.BlockSpec(
                (1, 1, source_rows, width),
                lambda i, *_, low=low, steps=steps: (jnp.clip(i - low, 0, steps - 1), 0, 0, 0),
            )
        )
        operands.append(source)
        starts.append((low, low + steps))
        low += steps
    in_specs.append(spec)
    operands.append(ew)
    aliases = {}
    if earlier is not None:
        aliases = {len(operands) + index: index for index in range(3)}
        in_specs += [pl.BlockSpec(memory_space=pl.ANY)] * 3
        operands += list(earlier)
    return pl.pallas_call(
        functools.partial(finish_kernel, section, starts),
        grid_spec=pltpu.PrefetchScalarGridSpec(
            num_scalar_prefetch=2,
            grid=(section[1],),
            in_specs=in_specs,
            out_specs=[spec] * 3,
        ),
        out_shape=[jax.ShapeDtypeStruct(ew.shape, kind) for kind in (F32, BF16, BF16)],
        input_output_aliases=aliases,
        compiler_params=pltpu.CompilerParams(vmem_limit_bytes=STREAM_LIMIT),
        name="finish",
    )(*operands)


def permute(array, pairs):
    return lax.ppermute(array, "fsdp", pairs)


def together(*arrays):
    return lax.optimization_barrier(arrays)


def far_pairs(table, step, to_owners):
    devices = table.shape[1]
    pairs = [(d ^ (2 * step), d) for d in range(devices) if table[0, d] == 1]
    return pairs if to_owners else [(there, here) for here, there in pairs]


def exchange_near(blocks, devices):
    groups = np.arange(devices).reshape(2, -1).tolist()
    return lax.all_to_all(blocks, "fsdp", 0, 0, axis_index_groups=groups, tiled=True)


def shards(expert_grad, expert_momentum, expert_master, kv_grad, kv_momentum, kv_master):
    devices = lax.axis_size("fsdp")
    chips = devices // 2
    far_steps = range(chips // 2, chips)
    me = lax.axis_index("fsdp").reshape(1)
    shape = expert_grad.shape
    rows, width = shape[2], shape[3]
    kv_rows = kv_grad.shape[1]
    flat = lambda array: array.reshape(-1, rows, width)
    eg, em, ew = flat(expert_grad), flat(expert_momentum), flat(expert_master)
    table = owner_table(eg.shape[0], kv_grad.shape[0], devices)
    sections = Plan(table)
    owns = sections.section([[device] for device in range(devices)])
    near_own = sections.section(near_owners(devices))
    far_own = sections.section(far_owners(devices, 0))
    far_other = sections.section(far_owners(devices, 1))
    plan = sections.array()
    slot = kv_slot(table)
    count = CLIP_RATIO * math.sqrt(devices * (expert_grad.size + kv_grad.size))
    cores = [(device, device ^ 1) for device in range(devices)]
    mirrors = [(device, device ^ chips) for device in range(devices)]

    total, gv, mv = load(eg, em)
    partial, staged, away = stage(
        far_other, devices, me, plan, total, gv, mv, kv_grad, kv_momentum
    )
    squares = lax.all_to_all(partial, "fsdp", 0, 0, tiled=True)
    mirror, sibling = permute(away, mirrors), permute(staged, cores)
    squares, sibling, mirror = together(squares, sibling, mirror)

    clip, *far = form_far(far_own, me, plan, squares, gv, mv, sibling, count)
    clip, far[0] = together(clip, far[0])
    near = form_near(near_own, me, plan, clip, gv, mv, kv_grad, kv_momentum, mirror)
    far = [permute(block, far_pairs(table, step, True)) for step, block in zip(far_steps, far)]
    near = exchange_near(near, devices)
    near_rows, near_gram = near_product(owns, me, plan, near, rows)

    near_rows, clip = together(near_rows, clip)
    factor = clip[0, 0]
    expert_moment_out = MOMENTUM * expert_momentum + factor * expert_grad
    kv_moment_out = MOMENTUM * kv_momentum + factor * kv_grad
    near_rows, expert_moment_out, kv_moment_out = together(
        near_rows, expert_moment_out, kv_moment_out
    )
    near, far = orthogonal_update(owns, me, plan, near, near_rows, near_gram, far, kv_rows)

    far = [permute(block, far_pairs(table, step, False)) for step, block in zip(far_steps, far)]
    near = exchange_near(near, devices)
    kv_back = permute(near[slot, kv_rows : 2 * kv_rows], mirrors)
    done = finish(near_own, me, plan, ew, [near[:, None]], None)
    far[0], *done = together(far[0], *done)
    others = permute(gather_far(far), cores)
    done = finish(far_own, me, plan, ew, [block[None] for block in far], done)
    done = finish(far_other, me, plan, ew, [others[:, None]], done)
    kv_back, eo, eb, eu = together(kv_back, *done)
    ko, kb, ku = finish_kv(me, devices, near, slot, kv_back, kv_master)
    return (
        eo.reshape(shape),
        expert_moment_out,
        eb.reshape(shape),
        eu.reshape(shape),
        ko,
        kv_moment_out,
        kb,
        ku,
    )


def solution(mesh):
    expert = P("groups", None, "fsdp", None)
    kv = P("groups", "fsdp", None)
    return jax.shard_map(
        shards,
        mesh=mesh,
        in_specs=(expert, expert, expert, kv, kv, kv),
        out_specs=(expert, expert, expert, expert, kv, kv, kv, kv),
        check_vma=False,
    )
```

```python
import functools
import math

import jax
import jax.numpy as jnp
import numpy as np
from jax import lax
from jax.experimental import pallas as pl
from jax.experimental.pallas import tpu as pltpu
from jax.sharding import PartitionSpec as P

NS_A = 3.4445
NS_B = -4.775
NS_C = 2.0315
MOMENTUM = 0.95
RATE = 0.02
DECAY = 0.1
NORM_EPS = 1e-07
CLIP_EPS = 1e-06
CLIP_RATIO = 0.5
UPDATE_GAIN = 0.2

F32 = jnp.float32
BF16 = jnp.bfloat16
VMEM_LIMIT = 40 * 1024 * 1024
LOAD_LIMIT = 46 * 1024 * 1024
GRAD_LIMIT = 46 * 1024 * 1024
STREAM_LIMIT = 16 * 1024 * 1024


def owner_table(experts, kvs, devices):
    table = np.zeros((2, devices), np.int32)
    chips = devices // 2
    first = min(experts, chips)
    for index in range(first):
        table[:, 2 * (index * chips // first)] = (1, index)
    by_parity = sorted(range(chips), key=lambda chip: bin(chip % (chips // 2)).count("1") % 2)
    for index in range(first, experts):
        table[:, 2 * by_parity[index - first] + 1] = (1, index)
    slot = kv_slot(table)
    for index in range(kvs):
        table[:, index * chips + slot] = (2, index)
    return table


def kv_slot(table):
    chips = table.shape[1] // 2
    free = (table[0, :chips] != 1) & (table[0, chips:] != 1)
    return next(slot for slot in range(1, chips, 2) if free[slot])


def near_owners(devices):
    half = devices // 2
    return [[device // half * half + other for other in range(half)] for device in range(devices)]


def far_owners(devices, flip):
    steps = range(devices // 4, devices // 2)
    return [[device ^ (2 * step) ^ flip for step in steps] for device in range(devices)]


class Plan:
    def __init__(self, table):
        self.table = table
        self.parts = []

    def section(self, owners):
        place = sum(part.size for part in self.parts)
        part = np.zeros((len(owners), 2, len(owners[0])), np.int32)
        for device, row in enumerate(owners):
            experts = [self.table[1, owner] for owner in row if self.table[0, owner] == 1]
            last = experts[0] if experts else 0
            for step, owner in enumerate(row):
                last = self.table[1, owner] if self.table[0, owner] == 1 else last
                part[device, :, step] = self.table[0, owner], last
        self.parts.append(part)
        idle = not (part[:, 0] == 1).any(axis=1).all()
        return place, part.shape[2], idle

    def array(self):
        return jnp.asarray(np.concatenate([part.reshape(-1) for part in self.parts]))


def kind_at(section, me, plan, step):
    return plan[section[0] + me[0] * 2 * section[1] + step]


def expert_at(section, me, plan, step):
    return plan[section[0] + (me[0] * 2 + 1) * section[1] + step]


def fold(block, rows):
    parts = block.reshape(-1, rows, block.shape[-1])
    return jnp.sum(parts * parts, axis=0)


def chunk_copies(source, target, sems):
    chunks = sems.shape[0]
    size = target.shape[0] // chunks
    pieces = [pl.ds(chunk * size, size) for chunk in range(chunks)]
    return [
        pltpu.make_async_copy(source.at[piece], target.at[piece], sems.at[chunk])
        for chunk, piece in enumerate(pieces)
    ]


def load_grad_kernel(eg, kg, gv, partial, total, sems):
    copies = chunk_copies(eg, gv, sems)
    for copy in copies:
        copy.start()
    size = gv.shape[0] // len(copies)
    total[...] = fold(kg[...], total.shape[0])
    for chunk, copy in enumerate(copies):
        copy.wait()
        total[...] += fold(gv[chunk * size : (chunk + 1) * size], total.shape[0])
    partial[...] = jnp.full(partial.shape, jnp.sum(total[...]), F32)


def load_kernel(em, mv, sems):
    copies = chunk_copies(em, mv, sems)
    for copy in copies:
        copy.start()
    for copy in copies:
        copy.wait()


def load_grad(eg, kg, devices):
    vmem = pl.BlockSpec(memory_space=pltpu.VMEM)
    hbm = pl.BlockSpec(memory_space=pltpu.HBM)
    rows = math.gcd(8, 3 * eg.shape[1], kg.shape[1])
    return pl.pallas_call(
        load_grad_kernel,
        in_specs=[hbm, vmem],
        out_specs=[vmem] * 2,
        out_shape=[
            jax.ShapeDtypeStruct(eg.shape, F32),
            jax.ShapeDtypeStruct((devices, 8, 128), F32),
        ],
        scratch_shapes=[
            pltpu.VMEM((rows, eg.shape[2]), F32),
            pltpu.SemaphoreType.DMA((eg.shape[0] // 3,)),
        ],
        compiler_params=pltpu.CompilerParams(vmem_limit_bytes=GRAD_LIMIT),
        name="loadgrad",
    )(eg, kg)


def load(em):
    return pl.pallas_call(
        load_kernel,
        in_specs=[pl.BlockSpec(memory_space=pltpu.HBM)],
        out_specs=pl.BlockSpec(memory_space=pltpu.VMEM),
        out_shape=jax.ShapeDtypeStruct(em.shape, F32),
        scratch_shapes=[pltpu.SemaphoreType.DMA((em.shape[0] // 3,))],
        compiler_params=pltpu.CompilerParams(vmem_limit_bytes=LOAD_LIMIT),
        name="load",
    )(em)


def stage_kernel(section, devices, me, plan, gv, mv, kg, km, staged, away):
    other = (me[0] < devices // 2).astype(jnp.int32)
    away[0] = kg[other].astype(BF16)
    away[1] = km[other].astype(BF16)
    for step in range(staged.shape[1]):
        expert = expert_at(section, me, plan, step)
        staged[0, step] = gv[expert].astype(BF16)
        staged[1, step] = mv[expert].astype(BF16)


def stage(section, devices, me, plan, gv, mv, kg, km):
    _, rows, width = gv.shape
    vmem = pl.BlockSpec(memory_space=pltpu.VMEM)
    smem = pl.BlockSpec(memory_space=pltpu.SMEM)
    return pl.pallas_call(
        functools.partial(stage_kernel, section, devices),
        in_specs=[smem] * 2 + [vmem] * 4,
        out_specs=[vmem] * 2,
        out_shape=[
            jax.ShapeDtypeStruct((2, section[1], rows, width), BF16),
            jax.ShapeDtypeStruct((2,) + kg.shape[1:], BF16),
        ],
        compiler_params=pltpu.CompilerParams(vmem_limit_bytes=STREAM_LIMIT),
        name="stage",
    )(me, plan, gv, mv, kg, km)


def nesterov(scale, grad, moment):
    clipped = scale * grad.astype(F32)
    return (clipped + MOMENTUM * (MOMENTUM * moment.astype(F32) + clipped)).astype(BF16)


def form_far_kernel(section, count, me, plan, squares, gv, mv, sib, clip, *outs):
    total = jnp.sum(squares[...], axis=0)
    factor = jnp.minimum(1.0, count / (jnp.sqrt(total) + CLIP_EPS))
    clip[...] = factor
    scale = factor[0:1, 0:1]
    for step, out in enumerate(outs):

        @pl.when(kind_at(section, me, plan, step) == 1)
        def _():
            expert = expert_at(section, me, plan, step)
            out[0] = nesterov(scale, gv[expert], mv[expert])
            out[1] = nesterov(scale, sib[0, step], sib[1, step])


def form_far(section, me, plan, squares, gv, mv, sib, count):
    vmem = pl.BlockSpec(memory_space=pltpu.VMEM)
    smem = pl.BlockSpec(memory_space=pltpu.SMEM)
    return pl.pallas_call(
        functools.partial(form_far_kernel, section, count),
        in_specs=[smem] * 2 + [vmem] * 4,
        out_specs=[vmem] * (1 + section[1]),
        out_shape=[jax.ShapeDtypeStruct((8, 128), F32)]
        + [jax.ShapeDtypeStruct((2,) + gv.shape[1:], BF16)] * section[1],
        compiler_params=pltpu.CompilerParams(vmem_limit_bytes=STREAM_LIMIT),
        name="far",
    )(me, plan, squares, gv, mv, sib)


def form_near_kernel(section, me, plan, clip, gv, mv, kg, km, mirror, out):
    scale = clip[0:1, 0:1]
    rows, kv_rows = gv.shape[1], kg.shape[1]
    mine = (me[0] >= section[1]).astype(jnp.int32)
    for step in range(section[1]):
        kind = kind_at(section, me, plan, step)

        @pl.when(kind == 1)
        def _():
            expert = expert_at(section, me, plan, step)
            out[step, :rows] = nesterov(scale, gv[expert], mv[expert])

        @pl.when(kind == 2)
        def _():
            out[step, :kv_rows] = nesterov(scale, kg[mine], km[mine])
            out[step, kv_rows : 2 * kv_rows] = nesterov(scale, mirror[0], mirror[1])


def form_near(section, me, plan, clip, gv, mv, kg, km, mirror):
    _, rows, width = gv.shape
    vmem = pl.BlockSpec(memory_space=pltpu.VMEM)
    smem = pl.BlockSpec(memory_space=pltpu.SMEM)
    return pl.pallas_call(
        functools.partial(form_near_kernel, section),
        in_specs=[smem] * 2 + [vmem] * 6,
        out_specs=vmem,
        out_shape=jax.ShapeDtypeStruct(
            (section[1], max(rows, 2 * kg.shape[1]), width), BF16
        ),
        compiler_params=pltpu.CompilerParams(vmem_limit_bytes=STREAM_LIMIT),
        name="form",
    )(me, plan, clip, gv, mv, kg, km, mirror)


def dot(left, right):
    return jnp.dot(left, right, preferred_element_type=F32)


def apply_rows(gain, x, rest, lead, low, high, store):
    width = x.shape[1]
    chunk = 512 if width % 512 == 0 else width
    for start in range(0, width, chunk):
        part = x[low:high, start : start + chunk].astype(F32)
        value = lead[low:high, 0:1] * part + dot(rest[low:high], x[:, start : start + chunk])
        value = (gain * value.astype(BF16).astype(F32)).astype(BF16)
        store(start, chunk, value)


def outer(left, right):
    return lax.dot_general(left, right, (((1,), (1,)), ((), ())), preferred_element_type=F32)


def diagonal_blocks(size):
    step = 128 if size % 128 == 0 else size
    row = lax.broadcasted_iota(jnp.int32, (step, step), 0)
    col = lax.broadcasted_iota(jnp.int32, (step, step), 1)
    return row == col, [slice(low, low + step) for low in range(0, size, step)]


def transform(gram, rest, lead):
    size = gram.shape[0]
    mask, parts = diagonal_blocks(size)
    trace = sum(
        jnp.sum(jnp.where(mask, gram[part, part], 0.0), keepdims=True) for part in parts
    )
    inverse = 1.0 / (jnp.sqrt(trace) + NORM_EPS)
    scaled = gram[...] * (inverse * inverse)
    low = scaled.astype(BF16)
    first = (NS_B * low.astype(F32) + NS_C * dot(low, low)).astype(BF16)
    product = dot(first, low)
    scaled = (NS_A * NS_A) * scaled + (2.0 * NS_A) * product + dot(product.astype(BF16), first)
    low = scaled.astype(BF16)
    second = (NS_B * low.astype(F32) + NS_C * dot(low, low)).astype(BF16)
    mixed = NS_A * (first.astype(F32) + second.astype(F32)) + dot(second, first)
    gram[...] = mixed * inverse
    for part in parts:
        block = gram[part, part]
        main = jnp.sum(jnp.where(mask, block, 0.0), axis=1, keepdims=True)
        lead[part] = jnp.broadcast_to((NS_A * NS_A) * inverse + main, lead[part].shape)
        gram[part, part] = jnp.where(mask, 0.0, block)
    rest[...] = gram[...].astype(BF16)


def place_far(blocks, x, start):
    rows = blocks[0].shape[1]
    for index, block in enumerate(blocks):
        for core in range(2):
            low = start + (2 * index + core) * rows
            x[low : low + rows] = block[core]


def place_near(blocks, rows, x):
    for index in range(blocks.shape[0]):
        x[index * rows : (index + 1) * rows] = blocks[index, :rows]


def store_far(outs):
    rows = outs[0].shape[1]

    def store(start, chunk, value):
        for index, out in enumerate(outs):
            for core in range(2):
                low = (2 * index + core) * rows
                out[core, :, start : start + chunk] = value[low : low + rows]

    return store


def store_near(out, rows):
    def store(start, chunk, value):
        for index in range(out.shape[0]):
            part = value[index * rows : (index + 1) * rows]
            out[index, :rows, start : start + chunk] = part

    return store


def near_kernel(owns, rows, me, plan, near, x, gram):
    @pl.when(kind_at(owns, me, plan, 0) == 1)
    def _():
        place_near(near, rows, x)
        gram[...] = outer(x[...], x[...])


def transform_kernel(owns, gain, kv_rows, me, plan, near, near_rows, near_gram, *refs):
    steps = (len(refs) - 4) // 2
    far, (x, rest, lead) = refs[:steps], refs[steps : steps + 3]
    outs, gram = refs[steps + 3 : -1], refs[-1]
    half = near_rows.shape[0]
    kind = kind_at(owns, me, plan, 0)

    @pl.when(kind == 1)
    def _():
        x[:half] = near_rows[...]
        place_far(far, x, half)
        gram[:half, :half] = near_gram[...]
        cross = outer(near_rows[...], x[half:])
        gram[:half, half:] = cross
        gram[half:, :half] = cross.T
        gram[half:, half:] = outer(x[half:], x[half:])
        transform(gram, rest, lead)
        apply_rows(gain, x, rest, lead, half, 2 * half, store_far(outs))

    @pl.when(kind == 2)
    def _():
        size = 2 * kv_rows * near.shape[0]
        place_near(near, 2 * kv_rows, x)
        kv_gram = gram.at[:size, :size]
        kv_gram[...] = outer(x[:size], x[:size])
        transform(kv_gram, rest.at[:size, :size], lead.at[:size])


def apply_kernel(owns, gain, rows, kv_rows, me, plan, x, rest, lead, out):
    kind = kind_at(owns, me, plan, 0)

    @pl.when(kind == 1)
    def _():
        apply_rows(gain, x, rest, lead, 0, x.shape[0] // 2, store_near(out, rows))

    @pl.when(kind == 2)
    def _():
        size = 2 * kv_rows * out.shape[0]
        part = x.at[:size], rest.at[:size, :size], lead.at[:size]
        apply_rows(gain, *part, 0, size, store_near(out, 2 * kv_rows))


def near_product(owns, me, plan, near, rows):
    half, width = near.shape[0] * rows, near.shape[2]
    vmem = pl.BlockSpec(memory_space=pltpu.VMEM)
    smem = pl.BlockSpec(memory_space=pltpu.SMEM)
    return pl.pallas_call(
        functools.partial(near_kernel, owns, rows),
        in_specs=[smem, smem, vmem],
        out_specs=[vmem, vmem],
        out_shape=[
            jax.ShapeDtypeStruct((half, width), BF16),
            jax.ShapeDtypeStruct((half, half), F32),
        ],
        compiler_params=pltpu.CompilerParams(vmem_limit_bytes=STREAM_LIMIT),
        name="near",
    )(me, plan, near)


def orthogonal_update(owns, me, plan, near, near_rows, near_gram, far, kv_rows):
    half, width = near_rows.shape
    size = 2 * half
    rows = far[0].shape[1]
    gain = UPDATE_GAIN * math.sqrt(width)
    vmem = pl.BlockSpec(memory_space=pltpu.VMEM)
    smem = pl.BlockSpec(memory_space=pltpu.SMEM)
    params = pltpu.CompilerParams(vmem_limit_bytes=VMEM_LIMIT)
    x, rest, lead, *back = pl.pallas_call(
        functools.partial(transform_kernel, owns, gain, kv_rows),
        in_specs=[smem, smem] + [vmem] * (3 + len(far)),
        out_specs=[vmem] * (3 + len(far)),
        out_shape=[
            jax.ShapeDtypeStruct((size, width), BF16),
            jax.ShapeDtypeStruct((size, size), BF16),
            jax.ShapeDtypeStruct((size, 128), F32),
        ]
        + [jax.ShapeDtypeStruct(block.shape, BF16) for block in far],
        scratch_shapes=[pltpu.VMEM((size, size), F32)],
        compiler_params=params,
        name="transform",
    )(me, plan, near, near_rows, near_gram, *far)
    near = pl.pallas_call(
        functools.partial(apply_kernel, owns, gain, rows, kv_rows),
        in_specs=[smem, smem] + [vmem] * 3,
        out_specs=vmem,
        out_shape=jax.ShapeDtypeStruct(near.shape, BF16),
        compiler_params=params,
        name="apply",
    )(me, plan, x, rest, lead)
    return near, back


def gather_kernel(*refs):
    for index, block in enumerate(refs[:-1]):
        refs[-1][index] = block[1]


def gather_far(blocks):
    _, rows, width = blocks[0].shape
    vmem = pl.BlockSpec(memory_space=pltpu.VMEM)
    return pl.pallas_call(
        gather_kernel,
        in_specs=[vmem] * len(blocks),
        out_specs=vmem,
        out_shape=jax.ShapeDtypeStruct((len(blocks), rows, width), BF16),
        compiler_params=pltpu.CompilerParams(vmem_limit_bytes=STREAM_LIMIT),
        name="gather",
    )(*blocks)


def kv_kernel(devices, me, kv, back, kw, ko, kb, ku):
    mine = (me[0] >= devices // 2).astype(jnp.int32)
    for index, update in ((mine, kv[0, : kw.shape[1]]), (1 - mine, back[...])):
        value = kw[index] * (1.0 - RATE * DECAY) - RATE * update.astype(F32)
        ko[index] = value
        kb[index] = value.astype(BF16)
        ku[index] = update


def finish_kv(me, devices, near, slot, back, kw):
    whole = lambda array: pl.BlockSpec(array.shape, lambda i: (0,) * array.ndim)
    return pl.pallas_call(
        functools.partial(kv_kernel, devices),
        grid=(1,),
        in_specs=[
            pl.BlockSpec(memory_space=pltpu.SMEM),
            pl.BlockSpec((1,) + near.shape[1:], lambda i: (slot, 0, 0)),
            whole(back),
            whole(kw),
        ],
        out_specs=[whole(kw)] * 3,
        out_shape=[jax.ShapeDtypeStruct(kw.shape, kind) for kind in (F32, BF16, BF16)],
        compiler_params=pltpu.CompilerParams(vmem_limit_bytes=STREAM_LIMIT),
        name="kv",
    )(me, near, back, kw)


def finish_kernel(section, starts, me, plan, *refs):
    _, steps, idle = section
    sources, ew, refs = refs[: len(starts)], refs[len(starts)], refs[len(starts) + 1 :]
    earlier, (new_ref, low_ref, update_ref) = refs[:-3], refs[-3:]
    now = pl.program_id(0)

    if earlier and idle:
        kinds = [kind_at(section, me, plan, step) for step in range(steps)]
        busy = sum((kind == 1).astype(jnp.int32) for kind in kinds)

        @pl.when(jnp.logical_and(now == 0, busy == 0))
        def _():
            block = pl.ds(expert_at(section, me, plan, 0), 1)
            for before, after in zip(earlier, refs[-3:]):
                pltpu.sync_copy(before.at[block], after)

    valid = kind_at(section, me, plan, now) == 1
    for source, (low, high) in zip(sources, starts):
        here = jnp.logical_and(now >= low, now < high)

        @pl.when(jnp.logical_and(here, valid))
        def _():
            update = source[0, 0, : ew.shape[1]]
            value = ew[0] * (1.0 - RATE * DECAY) - RATE * update.astype(F32)
            new_ref[0] = value
            low_ref[0] = value.astype(BF16)
            update_ref[0] = update


def finish(section, me, plan, ew, sources, earlier):
    _, rows, width = ew.shape
    spec = pl.BlockSpec(
        (1, rows, width), lambda i, me, plan: (expert_at(section, me, plan, i), 0, 0)
    )
    operands, in_specs, starts = [me, plan], [], []
    low = 0
    for source in sources:
        steps, _, source_rows, _ = source.shape
        in_specs.append(
            pl.BlockSpec(
                (1, 1, source_rows, width),
                lambda i, *_, low=low, steps=steps: (jnp.clip(i - low, 0, steps - 1), 0, 0, 0),
            )
        )
        operands.append(source)
        starts.append((low, low + steps))
        low += steps
    in_specs.append(spec)
    operands.append(ew)
    aliases = {}
    if earlier is not None:
        aliases = {len(operands) + index: index for index in range(3)}
        in_specs += [pl.BlockSpec(memory_space=pl.ANY)] * 3
        operands += list(earlier)
    return pl.pallas_call(
        functools.partial(finish_kernel, section, starts),
        grid_spec=pltpu.PrefetchScalarGridSpec(
            num_scalar_prefetch=2,
            grid=(section[1],),
            in_specs=in_specs,
            out_specs=[spec] * 3,
        ),
        out_shape=[jax.ShapeDtypeStruct(ew.shape, kind) for kind in (F32, BF16, BF16)],
        input_output_aliases=aliases,
        compiler_params=pltpu.CompilerParams(vmem_limit_bytes=STREAM_LIMIT),
        name="finish",
    )(*operands)


def permute(array, pairs):
    return lax.ppermute(array, "fsdp", pairs)


def together(*arrays):
    return lax.optimization_barrier(arrays)


def far_pairs(table, step, to_owners):
    devices = table.shape[1]
    pairs = [(d ^ (2 * step), d) for d in range(devices) if table[0, d] == 1]
    return pairs if to_owners else [(there, here) for here, there in pairs]


def exchange_near(blocks, devices):
    groups = np.arange(devices).reshape(2, -1).tolist()
    return lax.all_to_all(blocks, "fsdp", 0, 0, axis_index_groups=groups, tiled=True)


def shards(expert_grad, expert_momentum, expert_master, kv_grad, kv_momentum, kv_master):
    devices = lax.axis_size("fsdp")
    chips = devices // 2
    far_steps = range(chips // 2, chips)
    me = lax.axis_index("fsdp").reshape(1)
    shape = expert_grad.shape
    rows, width = shape[2], shape[3]
    kv_rows = kv_grad.shape[1]
    flat = lambda array: array.reshape(-1, rows, width)
    eg, em, ew = flat(expert_grad), flat(expert_momentum), flat(expert_master)
    table = owner_table(eg.shape[0], kv_grad.shape[0], devices)
    sections = Plan(table)
    owns = sections.section([[device] for device in range(devices)])
    near_own = sections.section(near_owners(devices))
    far_own = sections.section(far_owners(devices, 0))
    far_other = sections.section(far_owners(devices, 1))
    plan = sections.array()
    slot = kv_slot(table)
    count = CLIP_RATIO * math.sqrt(devices * (expert_grad.size + kv_grad.size))
    cores = [(device, device ^ 1) for device in range(devices)]
    mirrors = [(device, device ^ chips) for device in range(devices)]

    gv, partial = load_grad(eg, kv_grad, devices)
    partial, later = together(partial, em)
    squares = lax.all_to_all(partial, "fsdp", 0, 0, tiled=True)
    mv = load(later)
    staged, away = stage(far_other, devices, me, plan, gv, mv, kv_grad, kv_momentum)
    mirror, sibling = permute(away, mirrors), permute(staged, cores)
    squares, sibling, mirror = together(squares, sibling, mirror)

    clip, *far = form_far(far_own, me, plan, squares, gv, mv, sibling, count)
    clip, far[0] = together(clip, far[0])
    near = form_near(near_own, me, plan, clip, gv, mv, kv_grad, kv_momentum, mirror)
    far = [permute(block, far_pairs(table, step, True)) for step, block in zip(far_steps, far)]
    clip, near = together(clip, near)
    near = exchange_near(near, devices)

    factor = clip[0, 0]
    expert_moment_out = MOMENTUM * expert_momentum + factor * expert_grad
    kv_moment_out = MOMENTUM * kv_momentum + factor * kv_grad
    near_rows, near_gram = near_product(owns, me, plan, near, rows)
    near_rows, expert_moment_out, kv_moment_out = together(
        near_rows, expert_moment_out, kv_moment_out
    )
    near, far = orthogonal_update(owns, me, plan, near, near_rows, near_gram, far, kv_rows)

    far = [permute(block, far_pairs(table, step, False)) for step, block in zip(far_steps, far)]
    near = exchange_near(near, devices)
    kv_back = permute(near[slot, kv_rows : 2 * kv_rows], mirrors)
    done = finish(near_own, me, plan, ew, [near[:, None]], None)
    far[0], kv_back, *done = together(far[0], kv_back, *done)
    others = permute(gather_far(far), cores)
    done = finish(far_own, me, plan, ew, [block[None] for block in far], done)
    done = finish(far_other, me, plan, ew, [others[:, None]], done)
    eo, eb, eu = done
    ko, kb, ku = finish_kv(me, devices, near, slot, kv_back, kv_master)
    return (
        eo.reshape(shape),
        expert_moment_out,
        eb.reshape(shape),
        eu.reshape(shape),
        ko,
        kv_moment_out,
        kb,
        ku,
    )


def solution(mesh):
    expert = P("groups", None, "fsdp", None)
    kv = P("groups", "fsdp", None)
    return jax.shard_map(
        shards,
        mesh=mesh,
        in_specs=(expert, expert, expert, kv, kv, kv),
        out_specs=(expert, expert, expert, expert, kv, kv, kv, kv),
        check_vma=False,
    )
```

```python
import functools
import math

import jax
import jax.numpy as jnp
import numpy as np
from jax import lax
from jax.experimental import pallas as pl
from jax.experimental.pallas import tpu as pltpu
from jax.sharding import PartitionSpec as P

NS_A = 3.4445
NS_B = -4.775
NS_C = 2.0315
MOMENTUM = 0.95
RATE = 0.02
DECAY = 0.1
NORM_EPS = 1e-07
CLIP_EPS = 1e-06
CLIP_RATIO = 0.5
UPDATE_GAIN = 0.2

F32 = jnp.float32
BF16 = jnp.bfloat16
VMEM_LIMIT = 40 * 1024 * 1024
LOAD_LIMIT = 42 * 1024 * 1024
STREAM_LIMIT = 16 * 1024 * 1024


def owner_table(experts, kvs, devices):
    table = np.zeros((2, devices), np.int32)
    chips = devices // 2
    first = min(experts, chips)
    for index in range(first):
        table[:, 2 * (index * chips // first)] = (1, index)
    by_parity = sorted(range(chips), key=lambda chip: bin(chip).count("1") % 2)
    for index in range(first, experts):
        table[:, 2 * by_parity[index - first] + 1] = (1, index)
    for index in range(kvs):
        low = index * devices // kvs
        free = [d for d in range(low, low + devices // kvs) if d % 2 and not table[0, d]]
        table[:, free[0]] = (2, index)
    return table


def visit_tables(table, steps):
    devices = table.shape[1]
    kinds = np.zeros((devices, len(steps)), np.int32)
    held = np.zeros((devices, len(steps)), np.int32)
    for me in range(devices):
        owners = [me ^ step for step in steps]
        experts = [table[1, owner] for owner in owners if table[0, owner] == 1]
        last = experts[0] if experts else 0
        for place, owner in enumerate(owners):
            kinds[me, place] = table[0, owner]
            last = table[1, owner] if table[0, owner] == 1 else last
            held[me, place] = last
    return kinds, held


def visits(table, steps):
    return tuple(jnp.asarray(part.reshape(-1)) for part in visit_tables(table, steps))


def fold(block, rows):
    parts = block.reshape(-1, rows, block.shape[-1])
    return jnp.sum(parts * parts, axis=0)


def load_kernel(eg, em, total, gv, mv, sems):
    chunks = sems.shape[1]
    size = gv.shape[0] // chunks
    copies = [
        [
            pltpu.make_async_copy(
                source.at[pl.ds(chunk * size, size)],
                target.at[pl.ds(chunk * size, size)],
                sems.at[place, chunk],
            )
            for chunk in range(chunks)
        ]
        for place, (source, target) in enumerate(((eg, gv), (em, mv)))
    ]
    for copy in copies[0] + copies[1]:
        copy.start()
    total[...] = jnp.zeros_like(total)
    for chunk in range(chunks):
        copies[0][chunk].wait()
        total[...] += fold(gv[chunk * size : (chunk + 1) * size], total.shape[0])
    for copy in copies[1]:
        copy.wait()


def load(eg, em):
    vmem = pl.BlockSpec(memory_space=pltpu.VMEM)
    hbm = pl.BlockSpec(memory_space=pltpu.HBM)
    chunks = eg.shape[0] // 3
    total = jax.ShapeDtypeStruct((math.gcd(8, 3 * eg.shape[1]), eg.shape[2]), F32)
    return pl.pallas_call(
        load_kernel,
        in_specs=[hbm] * 2,
        out_specs=[vmem] * 3,
        out_shape=[total] + [jax.ShapeDtypeStruct(eg.shape, F32)] * 2,
        scratch_shapes=[pltpu.SemaphoreType.DMA((2, chunks))],
        compiler_params=pltpu.CompilerParams(vmem_limit_bytes=LOAD_LIMIT),
        name="load",
    )(eg, em)


def stage_kernel(devices, me, held, total, gv, mv, kg, km, partial, staged, keep, away):
    squares = jnp.sum(total[...]) + jnp.sum(fold(kg[...], math.gcd(8, kg.shape[1])))
    partial[...] = jnp.full(partial.shape, squares, F32)
    mine = (me[0] >= devices // 2).astype(jnp.int32)
    for out, index in ((keep, mine), (away, 1 - mine)):
        out[0] = kg[index].astype(BF16)
        out[1] = km[index].astype(BF16)
    chips = staged.shape[1]
    for step in range(chips):
        expert = held[me[0] * chips + step]
        staged[0, step] = gv[expert].astype(BF16)
        staged[1, step] = mv[expert].astype(BF16)


def stage(me, table, total, gv, mv, kg, km):
    _, rows, width = gv.shape
    devices = table.shape[1]
    chips = devices // 2
    _, held = visits(table, [2 * step + 1 for step in range(chips)])
    vmem = pl.BlockSpec(memory_space=pltpu.VMEM)
    smem = pl.BlockSpec(memory_space=pltpu.SMEM)
    kv = jax.ShapeDtypeStruct((2,) + kg.shape[1:], BF16)
    return pl.pallas_call(
        functools.partial(stage_kernel, devices),
        in_specs=[smem] * 2 + [vmem] * 5,
        out_specs=[vmem] * 4,
        out_shape=[
            jax.ShapeDtypeStruct((devices, 8, 128), F32),
            jax.ShapeDtypeStruct((2, chips, rows, width), BF16),
            kv,
            kv,
        ],
        compiler_params=pltpu.CompilerParams(vmem_limit_bytes=STREAM_LIMIT),
        name="stage",
    )(me, held, total, gv, mv, kg, km)


def nesterov(scale, grad, moment):
    clipped = scale * grad.astype(F32)
    return (clipped + MOMENTUM * (MOMENTUM * moment.astype(F32) + clipped)).astype(BF16)


def form_far_kernel(count, start, me, kinds, index, squares, gv, mv, sib, clip, *outs):
    total = jnp.sum(squares[...], axis=0)
    factor = jnp.minimum(1.0, count / (jnp.sqrt(total) + CLIP_EPS))
    clip[...] = factor
    scale = factor[0:1, 0:1]
    for step, out in enumerate(outs):
        place = me[0] * len(outs) + step

        @pl.when(kinds[place] == 1)
        def _():
            out[0] = nesterov(scale, gv[index[place]], mv[index[place]])
            out[1] = nesterov(scale, sib[0, start + step], sib[1, start + step])


def form_near_kernel(
    me, kinds, index, clip, gv, mv, sib, kg, km, mirror, kv_sib, *outs
):
    scale = clip[0:1, 0:1]
    rows, kv_rows = gv.shape[1], kg.shape[1]
    mine = (me[0] >= kinds.shape[0] // len(outs) // 2).astype(jnp.int32)
    for step, out in enumerate(outs):
        place = me[0] * len(outs) + step

        @pl.when(kinds[place] == 1)
        def _():
            out[0, :rows] = nesterov(scale, gv[index[place]], mv[index[place]])
            out[1, :rows] = nesterov(scale, sib[0, step], sib[1, step])

        @pl.when(kinds[place] == 2)
        def _():
            out[0, :kv_rows] = nesterov(scale, kg[mine], km[mine])
            out[0, kv_rows : 2 * kv_rows] = nesterov(scale, mirror[0], mirror[1])
            out[1, :kv_rows] = nesterov(scale, kv_sib[0, 0], kv_sib[0, 1])
            out[1, kv_rows : 2 * kv_rows] = nesterov(scale, kv_sib[1, 0], kv_sib[1, 1])


def form_call(kernel, name, table, chip_steps, me, operands, outs):
    kinds, index = visits(table, [2 * step for step in chip_steps])
    vmem = pl.BlockSpec(memory_space=pltpu.VMEM)
    smem = pl.BlockSpec(memory_space=pltpu.SMEM)
    return pl.pallas_call(
        kernel,
        in_specs=[smem] * 3 + [vmem] * len(operands),
        out_specs=[vmem] * len(outs),
        out_shape=outs,
        compiler_params=pltpu.CompilerParams(vmem_limit_bytes=STREAM_LIMIT),
        name=name,
    )(me, kinds, index, *operands)


def form_far(me, table, steps, squares, gv, mv, sib, count):
    block = jax.ShapeDtypeStruct((2,) + gv.shape[1:], BF16)
    clip = jax.ShapeDtypeStruct((8, 128), F32)
    kernel = functools.partial(form_far_kernel, count, steps[0])
    return form_call(
        kernel, "far", table, steps, me, (squares, gv, mv, sib), [clip] + [block] * len(steps)
    )


def form_near(me, table, steps, clip, gv, mv, sib, kg, km, mirror, kv_sib):
    _, rows, width = gv.shape
    block = jax.ShapeDtypeStruct((2, max(rows, 2 * kg.shape[1]), width), BF16)
    operands = (clip, gv, mv, sib, kg, km, mirror, kv_sib)
    return form_call(
        form_near_kernel, "form", table, steps, me, operands, [block] * len(steps)
    )


def dot(left, right):
    return jnp.dot(left, right, preferred_element_type=F32)


def apply_rows(gain, x, rest, lead, low, high, store):
    width = x.shape[1]
    chunk = 512 if width % 512 == 0 else width
    for start in range(0, width, chunk):
        part = x[low:high, start : start + chunk].astype(F32)
        value = lead[low:high, 0:1] * part + dot(rest[low:high], x[:, start : start + chunk])
        value = (gain * value.astype(BF16).astype(F32)).astype(BF16)
        store(start, chunk, value)


def store_blocks(outs, rows):
    def store(start, chunk, value):
        for index, out in enumerate(outs):
            for core in range(2):
                low = (2 * index + core) * rows
                out[core, :rows, start : start + chunk] = value[low : low + rows]

    return store


def outer(left, right):
    return lax.dot_general(left, right, (((1,), (1,)), ((), ())), preferred_element_type=F32)


def transform(raw):
    size = raw.shape[0]
    row = lax.broadcasted_iota(jnp.int32, (size, size), 0)
    col = lax.broadcasted_iota(jnp.int32, (size, size), 1)
    diagonal = row == col
    norm = jnp.sqrt(jnp.sum(jnp.where(diagonal, raw, 0.0), keepdims=True))
    inverse = 1.0 / (norm + NORM_EPS)
    gram = raw * inverse * inverse
    low = gram.astype(BF16)
    first = (NS_B * low.astype(F32) + NS_C * dot(low, low)).astype(BF16)
    product = dot(first, low)
    gram = (NS_A * NS_A) * gram + (2.0 * NS_A) * product + dot(product.astype(BF16), first)
    low = gram.astype(BF16)
    second = (NS_B * low.astype(F32) + NS_C * dot(low, low)).astype(BF16)
    mixed = NS_A * (first.astype(F32) + second.astype(F32)) + dot(second, first)
    main = NS_A * NS_A + jnp.sum(jnp.where(diagonal, mixed, 0.0), axis=1, keepdims=True)
    return main * inverse, (jnp.where(diagonal, 0.0, mixed) * inverse).astype(BF16)


def place_blocks(blocks, rows, x, start):
    for index, block in enumerate(blocks):
        for core in range(2):
            low = start + (2 * index + core) * rows
            x[low : low + rows] = block[core, :rows]


def near_kernel(me, kinds, *refs):
    blocks, (x, gram) = refs[:-2], refs[-2:]

    @pl.when(kinds[me[0]] == 1)
    def _():
        place_blocks(blocks, x.shape[0] // len(blocks) // 2, x, 0)
        gram[...] = outer(x[...], x[...])


def transform_kernel(gain, kv_rows, me, kinds, near, gram, *refs):
    chips = kinds.shape[0] // 2
    kv_blocks, blocks = refs[: chips // 2], refs[chips // 2 : chips]
    (x, rest, lead), outs = refs[chips : chips + 3], refs[chips + 3 :]
    half, rows = near.shape[0], blocks[0].shape[1]
    kind = kinds[me[0]]

    @pl.when(kind == 1)
    def _():
        x[:half] = near[...]
        place_blocks(blocks, rows, x, half)
        far = x[half:]
        cross = outer(near[...], far)
        raw = jnp.concatenate(
            [
                jnp.concatenate([gram[...], cross], axis=1),
                jnp.concatenate([cross.T, outer(far, far)], axis=1),
            ],
            axis=0,
        )
        main, other = transform(raw)
        lead[...] = jnp.broadcast_to(main, lead.shape)
        rest[...] = other
        apply_rows(gain, x, rest, lead, half, 2 * half, store_blocks(outs, rows))

    @pl.when(kind == 2)
    def _():
        size = 4 * kv_rows * len(kv_blocks)
        place_blocks(kv_blocks, 2 * kv_rows, x, 0)
        main, other = transform(outer(x[:size], x[:size]))
        lead[:size] = jnp.broadcast_to(main, (size, lead.shape[1]))
        rest[:size, :size] = other


def apply_kernel(gain, kv_rows, me, kinds, x, rest, lead, *outs):
    kind = kinds[me[0]]

    @pl.when(kind == 1)
    def _():
        rows = x.shape[0] // len(outs) // 4
        apply_rows(gain, x, rest, lead, 0, x.shape[0] // 2, store_blocks(outs, rows))

    @pl.when(kind == 2)
    def _():
        size = 4 * kv_rows * len(outs)
        kv = [ref.at[:size] for ref in (x, rest, lead)]
        kv[1] = rest.at[:size, :size]
        apply_rows(gain, *kv, 0, size, store_blocks(outs, 2 * kv_rows))


def near_gram(me, kinds, blocks, rows):
    width = blocks[0].shape[2]
    half = 2 * len(blocks) * rows
    vmem = pl.BlockSpec(memory_space=pltpu.VMEM)
    smem = pl.BlockSpec(memory_space=pltpu.SMEM)
    return pl.pallas_call(
        near_kernel,
        in_specs=[smem, smem] + [vmem] * len(blocks),
        out_specs=[vmem, vmem],
        out_shape=[
            jax.ShapeDtypeStruct((half, width), BF16),
            jax.ShapeDtypeStruct((half, half), F32),
        ],
        compiler_params=pltpu.CompilerParams(vmem_limit_bytes=STREAM_LIMIT),
        cost_estimate=pl.CostEstimate(
            flops=2 * half * half * width, bytes_accessed=4 * half * width, transcendentals=0
        ),
        name="near",
    )(me, kinds, *blocks)


def orthogonal_update(me, kinds, near, gram, kv_blocks, blocks, kv_rows):
    _, rows, width = blocks[0].shape
    half = near.shape[0]
    size = 2 * half
    gain = UPDATE_GAIN * math.sqrt(width)
    vmem = pl.BlockSpec(memory_space=pltpu.VMEM)
    smem = pl.BlockSpec(memory_space=pltpu.SMEM)
    like = lambda arrays: [jax.ShapeDtypeStruct(array.shape, BF16) for array in arrays]
    params = pltpu.CompilerParams(vmem_limit_bytes=VMEM_LIMIT)
    x, rest, lead, *far = pl.pallas_call(
        functools.partial(transform_kernel, gain, kv_rows),
        in_specs=[smem, smem] + [vmem] * (2 + 2 * len(blocks)),
        out_specs=[vmem] * (3 + len(blocks)),
        out_shape=[
            jax.ShapeDtypeStruct((size, width), BF16),
            jax.ShapeDtypeStruct((size, size), BF16),
            jax.ShapeDtypeStruct((size, 128), F32),
            *like(blocks),
        ],
        compiler_params=params,
        name="transform",
    )(me, kinds, near, gram, *kv_blocks, *blocks)
    near = pl.pallas_call(
        functools.partial(apply_kernel, gain, kv_rows),
        in_specs=[smem, smem] + [vmem] * 3,
        out_specs=[vmem] * len(blocks),
        out_shape=like(kv_blocks),
        compiler_params=params,
        name="apply",
    )(me, kinds, x, rest, lead)
    return list(near), far


def gather_kernel(rows, kv_rows, me, kinds, *refs):
    if kv_rows:
        blocks, (out, kv, kv_mirror) = refs[:-3], refs[-3:]
    else:
        blocks, out = refs[:-1], refs[-1]
    for index, block in enumerate(blocks):
        out[index] = block[1, :rows]
        if kv_rows:

            @pl.when(kinds[me[0] * len(blocks) + index] == 2)
            def _():
                for core in range(2):
                    kv[core] = block[core, :kv_rows]
                    kv_mirror[core] = block[core, kv_rows : 2 * kv_rows]


def gather_sibling(me, table, steps, blocks, rows, kv_rows):
    width = blocks[0].shape[2]
    kinds, _ = visits(table, [2 * step for step in steps])
    vmem = pl.BlockSpec(memory_space=pltpu.VMEM)
    smem = pl.BlockSpec(memory_space=pltpu.SMEM)
    kv = [jax.ShapeDtypeStruct((2, kv_rows, width), BF16)] * 2 if kv_rows else []
    return pl.pallas_call(
        functools.partial(gather_kernel, rows, kv_rows),
        in_specs=[smem, smem] + [vmem] * len(blocks),
        out_specs=[vmem] * (1 + len(kv)),
        out_shape=[jax.ShapeDtypeStruct((len(blocks), rows, width), BF16)] + kv,
        compiler_params=pltpu.CompilerParams(vmem_limit_bytes=STREAM_LIMIT),
        name="gather",
    )(me, kinds, *blocks)


def kv_kernel(devices, me, kv, back, kv_sibling, back_sibling, kw, ko, kb, ku):
    mine = (me[0] >= devices // 2).astype(jnp.int32)

    def apply(index, update):
        value = kw[index] * (1.0 - RATE * DECAY) - RATE * update.astype(F32)
        ko[index] = value
        kb[index] = value.astype(BF16)
        ku[index] = update

    @pl.when(me[0] % 2 == 1)
    def _():
        apply(mine, kv[0])
        apply(1 - mine, back[0])

    @pl.when(me[0] % 2 == 0)
    def _():
        apply(mine, kv_sibling[...])
        apply(1 - mine, back_sibling[...])


def finish_kv(me, devices, sources, kw):
    vmem = pl.BlockSpec(memory_space=pltpu.VMEM)
    return pl.pallas_call(
        functools.partial(kv_kernel, devices),
        in_specs=[pl.BlockSpec(memory_space=pltpu.SMEM)] + [vmem] * 5,
        out_specs=[vmem] * 3,
        out_shape=[jax.ShapeDtypeStruct(kw.shape, kind) for kind in (F32, BF16, BF16)],
        compiler_params=pltpu.CompilerParams(vmem_limit_bytes=STREAM_LIMIT),
        name="kv",
    )(me, *sources, kw)


def finish_kernel(plan, me, kinds, held, *refs):
    own, has_sibling, has_earlier, steps, idle = plan
    owns, refs = refs[:own], list(refs[own:])
    sibling = refs.pop(0) if has_sibling else None
    ew = refs.pop(0)
    earlier, (new_ref, low_ref, update_ref) = refs[:-3], refs[-3:]
    now = pl.program_id(0)

    if has_earlier and idle:
        first = me[0] * steps
        busy = sum((kinds[first + step] == 1).astype(jnp.int32) for step in range(steps))

        @pl.when(jnp.logical_and(now == 0, busy == 0))
        def _():
            for before, after in zip(earlier, refs[-3:]):
                pltpu.sync_copy(before.at[pl.ds(held[first], 1)], after)

    def apply(update):
        value = ew[0] * (1.0 - RATE * DECAY) - RATE * update.astype(F32)
        new_ref[0] = value
        low_ref[0] = value.astype(BF16)
        update_ref[0] = update

    valid = kinds[me[0] * steps + now] == 1
    for step, block in enumerate(owns):

        @pl.when(jnp.logical_and(now == step, valid))
        def _():
            apply(block[0, : ew.shape[1]])

    if has_sibling:

        @pl.when(jnp.logical_and(now >= own, valid))
        def _():
            apply(sibling[0])


def finish(me, table, ew, owns, own_steps, sibling, sibling_steps, earlier):
    _, rows, width = ew.shape
    steps = [2 * step for step in own_steps] + [2 * step + 1 for step in sibling_steps]
    kinds, held = visits(table, steps)
    idle = not (visit_tables(table, steps)[0] == 1).any(axis=1).all()
    size, own = len(steps), len(owns)
    block = (1, rows, width)
    spec = pl.BlockSpec(block, lambda i, me, k, h: (h[me[0] * size + i], 0, 0))
    operands = [me, kinds, held, *owns]
    in_specs = [
        pl.BlockSpec((1,) + array.shape[1:], lambda i, *_: (0, 0, 0)) for array in owns
    ]
    if sibling is not None:
        last = sibling.shape[0] - 1
        in_specs.append(pl.BlockSpec(block, lambda i, *_: (jnp.clip(i - own, 0, last), 0, 0)))
        operands.append(sibling)
    in_specs.append(spec)
    operands.append(ew)
    aliases = {}
    if earlier is not None:
        aliases = {len(operands) + index: index for index in range(3)}
        in_specs += [pl.BlockSpec(memory_space=pl.ANY)] * 3
        operands += list(earlier)
    return pl.pallas_call(
        functools.partial(
            finish_kernel, (own, sibling is not None, earlier is not None, size, idle)
        ),
        grid_spec=pltpu.PrefetchScalarGridSpec(
            num_scalar_prefetch=3,
            grid=(size,),
            in_specs=in_specs,
            out_specs=[spec] * 3,
        ),
        out_shape=[jax.ShapeDtypeStruct(ew.shape, kind) for kind in (F32, BF16, BF16)],
        input_output_aliases=aliases,
        compiler_params=pltpu.CompilerParams(vmem_limit_bytes=STREAM_LIMIT),
        name="finish",
    )(*operands)


def permute(array, pairs):
    return lax.ppermute(array, "fsdp", pairs)


def together(*arrays):
    return lax.optimization_barrier(arrays)


def block_pairs(table, step, to_owners):
    devices = table.shape[1]
    kinds = (1, 2) if 2 * step < devices // 2 else (1,)
    pairs = [(d ^ (2 * step), d) for d in range(devices) if table[0, d] in kinds]
    return pairs if to_owners else [(there, here) for here, there in pairs]


def cross(blocks, table, steps, to_owners):
    moved = []
    depth = max(len(blocks) // 2, 2)
    for place, (step, block) in enumerate(zip(steps, blocks)):
        if place >= depth:
            block, moved[place - depth] = together(block, moved[place - depth])
        moved.append(permute(block, block_pairs(table, step, to_owners)))
    return moved


def shards(expert_grad, expert_momentum, expert_master, kv_grad, kv_momentum, kv_master):
    devices = lax.axis_size("fsdp")
    chips, half = devices // 2, devices // 4
    me = lax.axis_index("fsdp").reshape(1)
    shape = expert_grad.shape
    rows, width = shape[2], shape[3]
    kv_rows = kv_grad.shape[1]
    flat = lambda array: array.reshape(-1, rows, width)
    eg, em, ew = flat(expert_grad), flat(expert_momentum), flat(expert_master)
    table = owner_table(eg.shape[0], kv_grad.shape[0], devices)
    count = CLIP_RATIO * math.sqrt(devices * (expert_grad.size + kv_grad.size))
    cores = [(device, device ^ 1) for device in range(devices)]
    mirrors = [(device, device ^ chips) for device in range(devices)]
    near_steps, far_steps = list(range(half)), list(range(half, chips))

    total, gv, mv = load(eg, em)
    partial, staged, keep, away = stage(me, table, total, gv, mv, kv_grad, kv_momentum)
    mirror = permute(away, mirrors)
    squares = lax.all_to_all(partial, "fsdp", 0, 0, tiled=True)
    squares, sibling, mirror = together(squares, permute(staged, cores), mirror)

    clip, *far = form_far(me, table, far_steps, squares, gv, mv, sibling, count)
    clip, far[0], keep = together(clip, far[0], keep)
    kv_sibling = permute(jnp.stack([keep, mirror]), [pair for pair in cores if pair[1] % 2])
    near = form_near(
        me, table, near_steps, clip, gv, mv, sibling, kv_grad, kv_momentum, mirror, kv_sibling
    )
    near = list(near)
    far = cross(far, table, far_steps, True)
    for step in near_steps[1:]:
        near[step] = permute(near[step], block_pairs(table, step, True))
    kinds = jnp.asarray(table[0])

    factor = clip[0, 0]
    expert_moment_out = MOMENTUM * expert_momentum + factor * expert_grad
    kv_moment_out = MOMENTUM * kv_momentum + factor * kv_grad
    near[0], expert_moment_out, kv_moment_out = together(
        near[0], expert_moment_out, kv_moment_out
    )
    near_rows, near_product = near_gram(me, kinds, near, rows)
    near, far = orthogonal_update(me, kinds, near_rows, near_product, near, far, kv_rows)

    far = cross(far, table, far_steps, False)
    for step in near_steps[1:]:
        near[step] = permute(near[step], block_pairs(table, step, False))
    near_sibling, kv, kv_mirror = gather_sibling(me, table, near_steps, near, rows, kv_rows)
    near_sibling = permute(near_sibling, cores)
    odd_mirrors = [pair for pair in mirrors if pair[0] % 2]
    down = [pair for pair in cores if pair[0] % 2]
    kv_back = permute(kv_mirror, odd_mirrors)
    done = finish(me, table, ew, near, near_steps, None, [], None)
    far[0], *done = together(far[0], *done)
    kv_sources = (kv, kv_back, permute(kv[1], down), permute(kv_back[1], down))
    far_sibling = permute(gather_sibling(me, table, far_steps, far, rows, 0)[0], cores)
    done = finish(me, table, ew, far, far_steps, near_sibling, near_steps, done)
    eo, eb, eu = finish(me, table, ew, [], [], far_sibling, far_steps, done)
    ko, kb, ku = finish_kv(me, devices, kv_sources, kv_master)
    return (
        eo.reshape(shape),
        expert_moment_out,
        eb.reshape(shape),
        eu.reshape(shape),
        ko,
        kv_moment_out,
        kb,
        ku,
    )


def solution(mesh):
    expert = P("groups", None, "fsdp", None)
    kv = P("groups", "fsdp", None)
    return jax.shard_map(
        shards,
        mesh=mesh,
        in_specs=(expert, expert, expert, kv, kv, kv),
        out_specs=(expert, expert, expert, expert, kv, kv, kv, kv),
        check_vma=False,
    )
```

```python
import functools
import math

import jax
import jax.numpy as jnp
import numpy as np
from jax import lax
from jax.experimental import pallas as pl
from jax.experimental.pallas import tpu as pltpu
from jax.sharding import PartitionSpec as P

NS_A = 3.4445
NS_B = -4.775
NS_C = 2.0315
MOMENTUM = 0.95
RATE = 0.02
DECAY = 0.1
NORM_EPS = 1e-07
CLIP_EPS = 1e-06
CLIP_RATIO = 0.5
UPDATE_GAIN = 0.2

F32 = jnp.float32
BF16 = jnp.bfloat16
VMEM_LIMIT = 40 * 1024 * 1024
LOAD_LIMIT = 42 * 1024 * 1024
STREAM_LIMIT = 16 * 1024 * 1024


def owner_table(experts, kvs, devices):
    table = np.zeros((2, devices), np.int32)
    chips = devices // 2
    first = min(experts, chips)
    for index in range(first):
        table[:, 2 * (index * chips // first)] = (1, index)
    by_parity = sorted(range(chips), key=lambda chip: bin(chip).count("1") % 2)
    for index in range(first, experts):
        table[:, 2 * by_parity[index - first] + 1] = (1, index)
    for index in range(kvs):
        low = index * devices // kvs
        free = [d for d in range(low, low + devices // kvs) if d % 2 and not table[0, d]]
        table[:, free[0]] = (2, index)
    return table


def visit_tables(table, steps):
    devices = table.shape[1]
    kinds = np.zeros((devices, len(steps)), np.int32)
    held = np.zeros((devices, len(steps)), np.int32)
    for me in range(devices):
        owners = [me ^ step for step in steps]
        experts = [table[1, owner] for owner in owners if table[0, owner] == 1]
        last = experts[0] if experts else 0
        for place, owner in enumerate(owners):
            kinds[me, place] = table[0, owner]
            last = table[1, owner] if table[0, owner] == 1 else last
            held[me, place] = last
    return kinds, held


def visits(table, steps):
    return tuple(jnp.asarray(part.reshape(-1)) for part in visit_tables(table, steps))


def fold(block, rows):
    parts = block.reshape(-1, rows, block.shape[-1])
    return jnp.sum(parts * parts, axis=0)


def load_kernel(eg, em, total, gv, mv, sems):
    chunks = sems.shape[1]
    size = gv.shape[0] // chunks
    copies = [
        [
            pltpu.make_async_copy(
                source.at[pl.ds(chunk * size, size)],
                target.at[pl.ds(chunk * size, size)],
                sems.at[place, chunk],
            )
            for chunk in range(chunks)
        ]
        for place, (source, target) in enumerate(((eg, gv), (em, mv)))
    ]
    for copy in copies[0] + copies[1]:
        copy.start()
    total[...] = jnp.zeros_like(total)
    for chunk in range(chunks):
        copies[0][chunk].wait()
        total[...] += fold(gv[chunk * size : (chunk + 1) * size], total.shape[0])
    for copy in copies[1]:
        copy.wait()


def load(eg, em):
    vmem = pl.BlockSpec(memory_space=pltpu.VMEM)
    hbm = pl.BlockSpec(memory_space=pltpu.HBM)
    chunks = eg.shape[0] // 3
    total = jax.ShapeDtypeStruct((math.gcd(8, 3 * eg.shape[1]), eg.shape[2]), F32)
    return pl.pallas_call(
        load_kernel,
        in_specs=[hbm] * 2,
        out_specs=[vmem] * 3,
        out_shape=[total] + [jax.ShapeDtypeStruct(eg.shape, F32)] * 2,
        scratch_shapes=[pltpu.SemaphoreType.DMA((2, chunks))],
        compiler_params=pltpu.CompilerParams(vmem_limit_bytes=LOAD_LIMIT),
        name="load",
    )(eg, em)


def stage_kernel(devices, me, held, total, gv, mv, kg, km, partial, staged, keep, away):
    squares = jnp.sum(total[...]) + jnp.sum(fold(kg[...], math.gcd(8, kg.shape[1])))
    partial[...] = jnp.full(partial.shape, squares, F32)
    mine = (me[0] >= devices // 2).astype(jnp.int32)
    for out, index in ((keep, mine), (away, 1 - mine)):
        out[0] = kg[index].astype(BF16)
        out[1] = km[index].astype(BF16)
    chips = staged.shape[1]
    for step in range(chips):
        expert = held[me[0] * chips + step]
        staged[0, step] = gv[expert].astype(BF16)
        staged[1, step] = mv[expert].astype(BF16)


def stage(me, table, total, gv, mv, kg, km):
    _, rows, width = gv.shape
    devices = table.shape[1]
    chips = devices // 2
    _, held = visits(table, [2 * step + 1 for step in range(chips)])
    vmem = pl.BlockSpec(memory_space=pltpu.VMEM)
    smem = pl.BlockSpec(memory_space=pltpu.SMEM)
    kv = jax.ShapeDtypeStruct((2,) + kg.shape[1:], BF16)
    return pl.pallas_call(
        functools.partial(stage_kernel, devices),
        in_specs=[smem] * 2 + [vmem] * 5,
        out_specs=[vmem] * 4,
        out_shape=[
            jax.ShapeDtypeStruct((devices, 8, 128), F32),
            jax.ShapeDtypeStruct((2, chips, rows, width), BF16),
            kv,
            kv,
        ],
        compiler_params=pltpu.CompilerParams(vmem_limit_bytes=STREAM_LIMIT),
        name="stage",
    )(me, held, total, gv, mv, kg, km)


def nesterov(scale, grad, moment):
    clipped = scale * grad.astype(F32)
    return (clipped + MOMENTUM * (MOMENTUM * moment.astype(F32) + clipped)).astype(BF16)


def form_far_kernel(count, start, me, kinds, index, squares, gv, mv, sib, clip, *outs):
    total = jnp.sum(squares[...], axis=0)
    factor = jnp.minimum(1.0, count / (jnp.sqrt(total) + CLIP_EPS))
    clip[...] = factor
    scale = factor[0:1, 0:1]
    for step, out in enumerate(outs):
        place = me[0] * len(outs) + step

        @pl.when(kinds[place] == 1)
        def _():
            out[0] = nesterov(scale, gv[index[place]], mv[index[place]])
            out[1] = nesterov(scale, sib[0, start + step], sib[1, start + step])


def form_near_kernel(
    me, kinds, index, clip, gv, mv, sib, kg, km, mirror, kv_sib, *outs
):
    scale = clip[0:1, 0:1]
    rows, kv_rows = gv.shape[1], kg.shape[1]
    mine = (me[0] >= kinds.shape[0] // len(outs) // 2).astype(jnp.int32)
    for step, out in enumerate(outs):
        place = me[0] * len(outs) + step

        @pl.when(kinds[place] == 1)
        def _():
            out[0, :rows] = nesterov(scale, gv[index[place]], mv[index[place]])
            out[1, :rows] = nesterov(scale, sib[0, step], sib[1, step])

        @pl.when(kinds[place] == 2)
        def _():
            out[0, :kv_rows] = nesterov(scale, kg[mine], km[mine])
            out[0, kv_rows : 2 * kv_rows] = nesterov(scale, mirror[0], mirror[1])
            out[1, :kv_rows] = nesterov(scale, kv_sib[0, 0], kv_sib[0, 1])
            out[1, kv_rows : 2 * kv_rows] = nesterov(scale, kv_sib[1, 0], kv_sib[1, 1])


def form_call(kernel, name, table, chip_steps, me, operands, outs):
    kinds, index = visits(table, [2 * step for step in chip_steps])
    vmem = pl.BlockSpec(memory_space=pltpu.VMEM)
    smem = pl.BlockSpec(memory_space=pltpu.SMEM)
    return pl.pallas_call(
        kernel,
        in_specs=[smem] * 3 + [vmem] * len(operands),
        out_specs=[vmem] * len(outs),
        out_shape=outs,
        compiler_params=pltpu.CompilerParams(vmem_limit_bytes=STREAM_LIMIT),
        name=name,
    )(me, kinds, index, *operands)


def form_far(me, table, steps, squares, gv, mv, sib, count):
    block = jax.ShapeDtypeStruct((2,) + gv.shape[1:], BF16)
    clip = jax.ShapeDtypeStruct((8, 128), F32)
    kernel = functools.partial(form_far_kernel, count, steps[0])
    return form_call(
        kernel, "far", table, steps, me, (squares, gv, mv, sib), [clip] + [block] * len(steps)
    )


def form_near(me, table, steps, clip, gv, mv, sib, kg, km, mirror, kv_sib):
    _, rows, width = gv.shape
    block = jax.ShapeDtypeStruct((2, max(rows, 2 * kg.shape[1]), width), BF16)
    operands = (clip, gv, mv, sib, kg, km, mirror, kv_sib)
    return form_call(
        form_near_kernel, "form", table, steps, me, operands, [block] * len(steps)
    )


def dot(left, right):
    return jnp.dot(left, right, preferred_element_type=F32)


def apply_rows(gain, x, rest, lead, low, high, store):
    width = x.shape[1]
    chunk = 512 if width % 512 == 0 else width
    for start in range(0, width, chunk):
        part = x[low:high, start : start + chunk].astype(F32)
        value = lead[low:high, 0:1] * part + dot(rest[low:high], x[:, start : start + chunk])
        value = (gain * value.astype(BF16).astype(F32)).astype(BF16)
        store(start, chunk, value)


def store_blocks(outs, rows):
    def store(start, chunk, value):
        for index, out in enumerate(outs):
            for core in range(2):
                low = (2 * index + core) * rows
                out[core, :rows, start : start + chunk] = value[low : low + rows]

    return store


def outer(left, right):
    return lax.dot_general(left, right, (((1,), (1,)), ((), ())), preferred_element_type=F32)


def transform(raw):
    size = raw.shape[0]
    row = lax.broadcasted_iota(jnp.int32, (size, size), 0)
    col = lax.broadcasted_iota(jnp.int32, (size, size), 1)
    diagonal = row == col
    norm = jnp.sqrt(jnp.sum(jnp.where(diagonal, raw, 0.0), keepdims=True))
    inverse = 1.0 / (norm + NORM_EPS)
    gram = raw * inverse * inverse
    low = gram.astype(BF16)
    first = (NS_B * low.astype(F32) + NS_C * dot(low, low)).astype(BF16)
    product = dot(first, low)
    gram = (NS_A * NS_A) * gram + (2.0 * NS_A) * product + dot(product.astype(BF16), first)
    low = gram.astype(BF16)
    second = (NS_B * low.astype(F32) + NS_C * dot(low, low)).astype(BF16)
    mixed = NS_A * (first.astype(F32) + second.astype(F32)) + dot(second, first)
    main = NS_A * NS_A + jnp.sum(jnp.where(diagonal, mixed, 0.0), axis=1, keepdims=True)
    return main * inverse, (jnp.where(diagonal, 0.0, mixed) * inverse).astype(BF16)


def place_blocks(blocks, rows, x, start):
    for index, block in enumerate(blocks):
        for core in range(2):
            low = start + (2 * index + core) * rows
            x[low : low + rows] = block[core, :rows]


def near_kernel(me, kinds, *refs):
    blocks, (x, gram) = refs[:-2], refs[-2:]

    @pl.when(kinds[me[0]] == 1)
    def _():
        place_blocks(blocks, x.shape[0] // len(blocks) // 2, x, 0)
        gram[...] = outer(x[...], x[...])


def transform_kernel(gain, kv_rows, me, kinds, near, gram, *refs):
    chips = kinds.shape[0] // 2
    kv_blocks, blocks = refs[: chips // 2], refs[chips // 2 : chips]
    (x, rest, lead), outs = refs[chips : chips + 3], refs[chips + 3 :]
    half, rows = near.shape[0], blocks[0].shape[1]
    kind = kinds[me[0]]

    @pl.when(kind == 1)
    def _():
        x[:half] = near[...]
        place_blocks(blocks, rows, x, half)
        far = x[half:]
        cross = outer(near[...], far)
        raw = jnp.concatenate(
            [
                jnp.concatenate([gram[...], cross], axis=1),
                jnp.concatenate([cross.T, outer(far, far)], axis=1),
            ],
            axis=0,
        )
        main, other = transform(raw)
        lead[...] = jnp.broadcast_to(main, lead.shape)
        rest[...] = other
        apply_rows(gain, x, rest, lead, half, 2 * half, store_blocks(outs, rows))

    @pl.when(kind == 2)
    def _():
        size = 4 * kv_rows * len(kv_blocks)
        place_blocks(kv_blocks, 2 * kv_rows, x, 0)
        main, other = transform(outer(x[:size], x[:size]))
        lead[:size] = jnp.broadcast_to(main, (size, lead.shape[1]))
        rest[:size, :size] = other


def apply_kernel(gain, kv_rows, me, kinds, x, rest, lead, *outs):
    kind = kinds[me[0]]

    @pl.when(kind == 1)
    def _():
        rows = x.shape[0] // len(outs) // 4
        apply_rows(gain, x, rest, lead, 0, x.shape[0] // 2, store_blocks(outs, rows))

    @pl.when(kind == 2)
    def _():
        size = 4 * kv_rows * len(outs)
        kv = [ref.at[:size] for ref in (x, rest, lead)]
        kv[1] = rest.at[:size, :size]
        apply_rows(gain, *kv, 0, size, store_blocks(outs, 2 * kv_rows))


def near_gram(me, kinds, blocks, rows):
    width = blocks[0].shape[2]
    half = 2 * len(blocks) * rows
    vmem = pl.BlockSpec(memory_space=pltpu.VMEM)
    smem = pl.BlockSpec(memory_space=pltpu.SMEM)
    return pl.pallas_call(
        near_kernel,
        in_specs=[smem, smem] + [vmem] * len(blocks),
        out_specs=[vmem, vmem],
        out_shape=[
            jax.ShapeDtypeStruct((half, width), BF16),
            jax.ShapeDtypeStruct((half, half), F32),
        ],
        compiler_params=pltpu.CompilerParams(vmem_limit_bytes=STREAM_LIMIT),
        cost_estimate=pl.CostEstimate(
            flops=2 * half * half * width, bytes_accessed=4 * half * width, transcendentals=0
        ),
        name="near",
    )(me, kinds, *blocks)


def orthogonal_update(me, kinds, near, gram, kv_blocks, blocks, kv_rows):
    _, rows, width = blocks[0].shape
    half = near.shape[0]
    size = 2 * half
    gain = UPDATE_GAIN * math.sqrt(width)
    vmem = pl.BlockSpec(memory_space=pltpu.VMEM)
    smem = pl.BlockSpec(memory_space=pltpu.SMEM)
    like = lambda arrays: [jax.ShapeDtypeStruct(array.shape, BF16) for array in arrays]
    params = pltpu.CompilerParams(vmem_limit_bytes=VMEM_LIMIT)
    x, rest, lead, *far = pl.pallas_call(
        functools.partial(transform_kernel, gain, kv_rows),
        in_specs=[smem, smem] + [vmem] * (2 + 2 * len(blocks)),
        out_specs=[vmem] * (3 + len(blocks)),
        out_shape=[
            jax.ShapeDtypeStruct((size, width), BF16),
            jax.ShapeDtypeStruct((size, size), BF16),
            jax.ShapeDtypeStruct((size, 128), F32),
            *like(blocks),
        ],
        compiler_params=params,
        name="transform",
    )(me, kinds, near, gram, *kv_blocks, *blocks)
    near = pl.pallas_call(
        functools.partial(apply_kernel, gain, kv_rows),
        in_specs=[smem, smem] + [vmem] * 3,
        out_specs=[vmem] * len(blocks),
        out_shape=like(kv_blocks),
        compiler_params=params,
        name="apply",
    )(me, kinds, x, rest, lead)
    return list(near), far


def gather_kernel(rows, kv_rows, me, kinds, *refs):
    if kv_rows:
        blocks, (out, kv, across) = refs[:-3], refs[-3:]
    else:
        blocks, out = refs[:-1], refs[-1]
    for index, block in enumerate(blocks):
        out[index] = block[1, :rows]
        if kv_rows:

            @pl.when(kinds[me[0] * len(blocks) + index] == 2)
            def _():
                out[len(blocks), :kv_rows] = block[1, :kv_rows]
                kv[...] = block[0, :kv_rows]
                for core in range(2):
                    across[core] = block[core, kv_rows : 2 * kv_rows]


def gather_sibling(me, table, steps, blocks, rows, kv_rows):
    width = blocks[0].shape[2]
    kinds, _ = visits(table, [2 * step for step in steps])
    vmem = pl.BlockSpec(memory_space=pltpu.VMEM)
    smem = pl.BlockSpec(memory_space=pltpu.SMEM)
    shapes = [(kv_rows, width), (2, kv_rows, width)] if kv_rows else []
    kv = [jax.ShapeDtypeStruct(shape, BF16) for shape in shapes]
    size = len(blocks) + (1 if kv_rows else 0)
    return pl.pallas_call(
        functools.partial(gather_kernel, rows, kv_rows),
        in_specs=[smem, smem] + [vmem] * len(blocks),
        out_specs=[vmem] * (1 + len(kv)),
        out_shape=[jax.ShapeDtypeStruct((size, rows, width), BF16)] + kv,
        compiler_params=pltpu.CompilerParams(vmem_limit_bytes=STREAM_LIMIT),
        name="gather",
    )(me, kinds, *blocks)


def kv_kernel(devices, me, kv, across, sibling, across_sibling, kw, ko, kb, ku):
    rows = kw.shape[1]
    mine = (me[0] >= devices // 2).astype(jnp.int32)

    def apply(index, update):
        value = kw[index] * (1.0 - RATE * DECAY) - RATE * update.astype(F32)
        ko[index] = value
        kb[index] = value.astype(BF16)
        ku[index] = update

    @pl.when(me[0] % 2 == 1)
    def _():
        apply(mine, kv[...])
        apply(1 - mine, across[0])

    @pl.when(me[0] % 2 == 0)
    def _():
        apply(mine, sibling[sibling.shape[0] - 1, :rows])
        apply(1 - mine, across_sibling[...])


def finish_kv(me, devices, sources, kw):
    vmem = pl.BlockSpec(memory_space=pltpu.VMEM)
    return pl.pallas_call(
        functools.partial(kv_kernel, devices),
        in_specs=[pl.BlockSpec(memory_space=pltpu.SMEM)] + [vmem] * 5,
        out_specs=[vmem] * 3,
        out_shape=[jax.ShapeDtypeStruct(kw.shape, kind) for kind in (F32, BF16, BF16)],
        compiler_params=pltpu.CompilerParams(vmem_limit_bytes=STREAM_LIMIT),
        name="kv",
    )(me, *sources, kw)


def finish_kernel(plan, me, kinds, held, *refs):
    own, has_sibling, has_earlier, steps, idle = plan
    owns, refs = refs[:own], list(refs[own:])
    sibling = refs.pop(0) if has_sibling else None
    ew = refs.pop(0)
    earlier, (new_ref, low_ref, update_ref) = refs[:-3], refs[-3:]
    now = pl.program_id(0)

    if has_earlier and idle:
        first = me[0] * steps
        busy = sum((kinds[first + step] == 1).astype(jnp.int32) for step in range(steps))

        @pl.when(jnp.logical_and(now == 0, busy == 0))
        def _():
            for before, after in zip(earlier, refs[-3:]):
                pltpu.sync_copy(before.at[pl.ds(held[first], 1)], after)

    def apply(update):
        value = ew[0] * (1.0 - RATE * DECAY) - RATE * update.astype(F32)
        new_ref[0] = value
        low_ref[0] = value.astype(BF16)
        update_ref[0] = update

    valid = kinds[me[0] * steps + now] == 1
    for step, block in enumerate(owns):

        @pl.when(jnp.logical_and(now == step, valid))
        def _():
            apply(block[0, : ew.shape[1]])

    if has_sibling:

        @pl.when(jnp.logical_and(now >= own, valid))
        def _():
            apply(sibling[0])


def finish(me, table, ew, owns, own_steps, sibling, sibling_steps, earlier):
    _, rows, width = ew.shape
    steps = [2 * step for step in own_steps] + [2 * step + 1 for step in sibling_steps]
    kinds, held = visits(table, steps)
    idle = not (visit_tables(table, steps)[0] == 1).any(axis=1).all()
    size, own = len(steps), len(owns)
    block = (1, rows, width)
    spec = pl.BlockSpec(block, lambda i, me, k, h: (h[me[0] * size + i], 0, 0))
    operands = [me, kinds, held, *owns]
    in_specs = [
        pl.BlockSpec((1,) + array.shape[1:], lambda i, *_: (0, 0, 0)) for array in owns
    ]
    if sibling is not None:
        last = sibling.shape[0] - 1
        in_specs.append(pl.BlockSpec(block, lambda i, *_: (jnp.clip(i - own, 0, last), 0, 0)))
        operands.append(sibling)
    in_specs.append(spec)
    operands.append(ew)
    aliases = {}
    if earlier is not None:
        aliases = {len(operands) + index: index for index in range(3)}
        in_specs += [pl.BlockSpec(memory_space=pl.ANY)] * 3
        operands += list(earlier)
    return pl.pallas_call(
        functools.partial(
            finish_kernel, (own, sibling is not None, earlier is not None, size, idle)
        ),
        grid_spec=pltpu.PrefetchScalarGridSpec(
            num_scalar_prefetch=3,
            grid=(size,),
            in_specs=in_specs,
            out_specs=[spec] * 3,
        ),
        out_shape=[jax.ShapeDtypeStruct(ew.shape, kind) for kind in (F32, BF16, BF16)],
        input_output_aliases=aliases,
        compiler_params=pltpu.CompilerParams(vmem_limit_bytes=STREAM_LIMIT),
        name="finish",
    )(*operands)


def permute(array, pairs):
    return lax.ppermute(array, "fsdp", pairs)


def together(*arrays):
    return lax.optimization_barrier(arrays)


def block_pairs(table, step, to_owners):
    devices = table.shape[1]
    kinds = (1, 2) if 2 * step < devices // 2 else (1,)
    pairs = [(d ^ (2 * step), d) for d in range(devices) if table[0, d] in kinds]
    return pairs if to_owners else [(there, here) for here, there in pairs]


def cross(blocks, table, steps, to_owners):
    moved = []
    depth = max(len(blocks) // 2, 2)
    for place, (step, block) in enumerate(zip(steps, blocks)):
        if place >= depth:
            block, moved[place - depth] = together(block, moved[place - depth])
        moved.append(permute(block, block_pairs(table, step, to_owners)))
    return moved


def shards(expert_grad, expert_momentum, expert_master, kv_grad, kv_momentum, kv_master):
    devices = lax.axis_size("fsdp")
    chips, half = devices // 2, devices // 4
    me = lax.axis_index("fsdp").reshape(1)
    shape = expert_grad.shape
    rows, width = shape[2], shape[3]
    kv_rows = kv_grad.shape[1]
    flat = lambda array: array.reshape(-1, rows, width)
    eg, em, ew = flat(expert_grad), flat(expert_momentum), flat(expert_master)
    table = owner_table(eg.shape[0], kv_grad.shape[0], devices)
    count = CLIP_RATIO * math.sqrt(devices * (expert_grad.size + kv_grad.size))
    cores = [(device, device ^ 1) for device in range(devices)]
    mirrors = [(device, device ^ chips) for device in range(devices)]
    near_steps, far_steps = list(range(half)), list(range(half, chips))

    total, gv, mv = load(eg, em)
    partial, staged, keep, away = stage(me, table, total, gv, mv, kv_grad, kv_momentum)
    mirror = permute(away, mirrors)
    squares = lax.all_to_all(partial, "fsdp", 0, 0, tiled=True)
    squares, sibling, mirror = together(squares, permute(staged, cores), mirror)

    clip, *far = form_far(me, table, far_steps, squares, gv, mv, sibling, count)
    clip, far[0], keep = together(clip, far[0], keep)
    kv_sibling = permute(jnp.stack([keep, mirror]), [pair for pair in cores if pair[1] % 2])
    near = form_near(
        me, table, near_steps, clip, gv, mv, sibling, kv_grad, kv_momentum, mirror, kv_sibling
    )
    near = list(near)
    far = cross(far, table, far_steps, True)
    for step in near_steps[1:]:
        near[step] = permute(near[step], block_pairs(table, step, True))
    kinds = jnp.asarray(table[0])

    factor = clip[0, 0]
    expert_moment_out = MOMENTUM * expert_momentum + factor * expert_grad
    kv_moment_out = MOMENTUM * kv_momentum + factor * kv_grad
    near[0], expert_moment_out, kv_moment_out = together(
        near[0], expert_moment_out, kv_moment_out
    )
    near_rows, near_product = near_gram(me, kinds, near, rows)
    near, far = orthogonal_update(me, kinds, near_rows, near_product, near, far, kv_rows)

    far = cross(far, table, far_steps, False)
    for step in near_steps[1:]:
        near[step] = permute(near[step], block_pairs(table, step, False))
    near_sibling, kv, across = gather_sibling(me, table, near_steps, near, rows, kv_rows)
    near_sibling = permute(near_sibling, cores)
    across = permute(across, [pair for pair in mirrors if pair[0] % 2])
    done = finish(me, table, ew, near, near_steps, None, [], None)
    far[0], *done = together(far[0], *done)
    across_sibling = permute(across[1], [pair for pair in cores if pair[0] % 2])
    far_sibling = permute(gather_sibling(me, table, far_steps, far, rows, 0)[0], cores)
    done = finish(me, table, ew, far, far_steps, near_sibling, near_steps, done)
    across_sibling, *done = together(across_sibling, *done)
    ko, kb, ku = finish_kv(
        me, devices, (kv, across, near_sibling, across_sibling), kv_master
    )
    eo, eb, eu = finish(me, table, ew, [], [], far_sibling, far_steps, done)
    return (
        eo.reshape(shape),
        expert_moment_out,
        eb.reshape(shape),
        eu.reshape(shape),
        ko,
        kv_moment_out,
        kb,
        ku,
    )


def solution(mesh):
    expert = P("groups", None, "fsdp", None)
    kv = P("groups", "fsdp", None)
    return jax.shard_map(
        shards,
        mesh=mesh,
        in_specs=(expert, expert, expert, kv, kv, kv),
        out_specs=(expert, expert, expert, expert, kv, kv, kv, kv),
        check_vma=False,
    )
```

```python
import functools
import math

import jax
import jax.numpy as jnp
import numpy as np
from jax import lax
from jax.experimental import pallas as pl
from jax.experimental.pallas import tpu as pltpu
from jax.sharding import PartitionSpec as P

NS_A = 3.4445
NS_B = -4.775
NS_C = 2.0315
MOMENTUM = 0.95
RATE = 0.02
DECAY = 0.1
NORM_EPS = 1e-07
CLIP_EPS = 1e-06
CLIP_RATIO = 0.5
UPDATE_GAIN = 0.2

F32 = jnp.float32
BF16 = jnp.bfloat16
VMEM_LIMIT = 40 * 1024 * 1024
LOAD_LIMIT = 42 * 1024 * 1024
STREAM_LIMIT = 16 * 1024 * 1024


def owner_table(experts, kvs, devices):
    table = np.zeros((2, devices), np.int32)
    chips = devices // 2
    first = min(experts, chips)
    for index in range(first):
        table[:, 2 * (index * chips // first)] = (1, index)
    by_parity = sorted(range(chips), key=lambda chip: bin(chip).count("1") % 2)
    for index in range(first, experts):
        table[:, 2 * by_parity[index - first] + 1] = (1, index)
    for index in range(kvs):
        low = index * devices // kvs
        free = [d for d in range(low, low + devices // kvs) if d % 2 and not table[0, d]]
        table[:, free[0]] = (2, index)
    return table


def visit_tables(table, steps):
    devices = table.shape[1]
    kinds = np.zeros((devices, len(steps)), np.int32)
    held = np.zeros((devices, len(steps)), np.int32)
    for me in range(devices):
        owners = [me ^ step for step in steps]
        experts = [table[1, owner] for owner in owners if table[0, owner] == 1]
        last = experts[0] if experts else 0
        for place, owner in enumerate(owners):
            kinds[me, place] = table[0, owner]
            last = table[1, owner] if table[0, owner] == 1 else last
            held[me, place] = last
    return kinds, held


def visits(table, steps):
    return tuple(jnp.asarray(part.reshape(-1)) for part in visit_tables(table, steps))


def fold(block, rows):
    parts = block.reshape(-1, rows, block.shape[-1])
    return jnp.sum(parts * parts, axis=0)


def load_kernel(eg, em, total, gv, mv, sems):
    chunks = sems.shape[1]
    size = gv.shape[0] // chunks
    copies = [
        [
            pltpu.make_async_copy(
                source.at[pl.ds(chunk * size, size)],
                target.at[pl.ds(chunk * size, size)],
                sems.at[place, chunk],
            )
            for chunk in range(chunks)
        ]
        for place, (source, target) in enumerate(((eg, gv), (em, mv)))
    ]
    for copy in copies[0] + copies[1]:
        copy.start()
    total[...] = jnp.zeros_like(total)
    for chunk in range(chunks):
        copies[0][chunk].wait()
        total[...] += fold(gv[chunk * size : (chunk + 1) * size], total.shape[0])
    for copy in copies[1]:
        copy.wait()


def load(eg, em):
    vmem = pl.BlockSpec(memory_space=pltpu.VMEM)
    hbm = pl.BlockSpec(memory_space=pltpu.HBM)
    chunks = eg.shape[0] // 3
    total = jax.ShapeDtypeStruct((math.gcd(8, 3 * eg.shape[1]), eg.shape[2]), F32)
    return pl.pallas_call(
        load_kernel,
        in_specs=[hbm] * 2,
        out_specs=[vmem] * 3,
        out_shape=[total] + [jax.ShapeDtypeStruct(eg.shape, F32)] * 2,
        scratch_shapes=[pltpu.SemaphoreType.DMA((2, chunks))],
        compiler_params=pltpu.CompilerParams(vmem_limit_bytes=LOAD_LIMIT),
        name="load",
    )(eg, em)


def stage_kernel(devices, me, held, total, gv, mv, kg, km, partial, staged, keep, away):
    squares = jnp.sum(total[...]) + jnp.sum(fold(kg[...], math.gcd(8, kg.shape[1])))
    partial[...] = jnp.full(partial.shape, squares, F32)
    mine = (me[0] >= devices // 2).astype(jnp.int32)
    for out, index in ((keep, mine), (away, 1 - mine)):
        out[0] = kg[index].astype(BF16)
        out[1] = km[index].astype(BF16)
    chips = staged.shape[1]
    for step in range(chips):
        expert = held[me[0] * chips + step]
        staged[0, step] = gv[expert].astype(BF16)
        staged[1, step] = mv[expert].astype(BF16)


def stage(me, table, total, gv, mv, kg, km):
    _, rows, width = gv.shape
    devices = table.shape[1]
    chips = devices // 2
    _, held = visits(table, [2 * step + 1 for step in range(chips)])
    vmem = pl.BlockSpec(memory_space=pltpu.VMEM)
    smem = pl.BlockSpec(memory_space=pltpu.SMEM)
    kv = jax.ShapeDtypeStruct((2,) + kg.shape[1:], BF16)
    return pl.pallas_call(
        functools.partial(stage_kernel, devices),
        in_specs=[smem] * 2 + [vmem] * 5,
        out_specs=[vmem] * 4,
        out_shape=[
            jax.ShapeDtypeStruct((devices, 8, 128), F32),
            jax.ShapeDtypeStruct((2, chips, rows, width), BF16),
            kv,
            kv,
        ],
        compiler_params=pltpu.CompilerParams(vmem_limit_bytes=STREAM_LIMIT),
        name="stage",
    )(me, held, total, gv, mv, kg, km)


def nesterov(scale, grad, moment):
    clipped = scale * grad.astype(F32)
    return (clipped + MOMENTUM * (MOMENTUM * moment.astype(F32) + clipped)).astype(BF16)


def form_far_kernel(count, start, me, kinds, index, squares, gv, mv, sib, clip, *outs):
    total = jnp.sum(squares[...], axis=0)
    factor = jnp.minimum(1.0, count / (jnp.sqrt(total) + CLIP_EPS))
    clip[...] = factor
    scale = factor[0:1, 0:1]
    for step, out in enumerate(outs):
        place = me[0] * len(outs) + step

        @pl.when(kinds[place] == 1)
        def _():
            out[0] = nesterov(scale, gv[index[place]], mv[index[place]])
            out[1] = nesterov(scale, sib[0, start + step], sib[1, start + step])


def form_near_kernel(me, kinds, index, clip, gv, mv, sib, kg, km, mirror, kv_sib, *outs):
    scale = clip[0:1, 0:1]
    steps, kv_rows = len(outs) // 2, kg.shape[1]
    mine = (me[0] >= kinds.shape[0] // steps // 2).astype(jnp.int32)
    for step, (out, kv) in enumerate(zip(outs[:steps], outs[steps:])):
        place = me[0] * steps + step

        @pl.when(kinds[place] == 1)
        def _():
            out[0] = nesterov(scale, gv[index[place]], mv[index[place]])
            out[1] = nesterov(scale, sib[0, step], sib[1, step])

        @pl.when(kinds[place] == 2)
        def _():
            kv[0, :kv_rows] = nesterov(scale, kg[mine], km[mine])
            kv[0, kv_rows:] = nesterov(scale, mirror[0], mirror[1])
            kv[1, :kv_rows] = nesterov(scale, kv_sib[0, 0], kv_sib[0, 1])
            kv[1, kv_rows:] = nesterov(scale, kv_sib[1, 0], kv_sib[1, 1])


def form_call(kernel, name, table, chip_steps, me, operands, outs):
    kinds, index = visits(table, [2 * step for step in chip_steps])
    vmem = pl.BlockSpec(memory_space=pltpu.VMEM)
    smem = pl.BlockSpec(memory_space=pltpu.SMEM)
    return pl.pallas_call(
        kernel,
        in_specs=[smem] * 3 + [vmem] * len(operands),
        out_specs=[vmem] * len(outs),
        out_shape=outs,
        compiler_params=pltpu.CompilerParams(vmem_limit_bytes=STREAM_LIMIT),
        name=name,
    )(me, kinds, index, *operands)


def form_far(me, table, steps, squares, gv, mv, sib, count):
    block = jax.ShapeDtypeStruct((2,) + gv.shape[1:], BF16)
    clip = jax.ShapeDtypeStruct((8, 128), F32)
    kernel = functools.partial(form_far_kernel, count, steps[0])
    return form_call(
        kernel, "far", table, steps, me, (squares, gv, mv, sib), [clip] + [block] * len(steps)
    )


def form_near(me, table, steps, clip, gv, mv, sib, kg, km, mirror, kv_sib):
    _, rows, width = gv.shape
    shapes = [(2, rows, width)] * len(steps) + [(2, 2 * kg.shape[1], width)] * len(steps)
    outs = [jax.ShapeDtypeStruct(shape, BF16) for shape in shapes]
    operands = (clip, gv, mv, sib, kg, km, mirror, kv_sib)
    blocks = form_call(form_near_kernel, "form", table, steps, me, operands, outs)
    return list(blocks[: len(steps)]), list(blocks[len(steps) :])


def dot(left, right):
    return jnp.dot(left, right, preferred_element_type=F32)


def apply_rows(gain, x, rest, lead, low, high, store):
    width = x.shape[1]
    chunk = 512 if width % 512 == 0 else width
    for start in range(0, width, chunk):
        part = x[low:high, start : start + chunk].astype(F32)
        value = lead[low:high, 0:1] * part + dot(rest[low:high], x[:, start : start + chunk])
        value = (gain * value.astype(BF16).astype(F32)).astype(BF16)
        store(start, chunk, value)


def store_blocks(outs, rows):
    def store(start, chunk, value):
        for index, out in enumerate(outs):
            for core in range(2):
                low = (2 * index + core) * rows
                out[core, :rows, start : start + chunk] = value[low : low + rows]

    return store


def outer(left, right):
    return lax.dot_general(left, right, (((1,), (1,)), ((), ())), preferred_element_type=F32)


def transform(raw):
    size = raw.shape[0]
    row = lax.broadcasted_iota(jnp.int32, (size, size), 0)
    col = lax.broadcasted_iota(jnp.int32, (size, size), 1)
    diagonal = row == col
    norm = jnp.sqrt(jnp.sum(jnp.where(diagonal, raw, 0.0), keepdims=True))
    inverse = 1.0 / (norm + NORM_EPS)
    gram = raw * inverse * inverse
    low = gram.astype(BF16)
    first = (NS_B * low.astype(F32) + NS_C * dot(low, low)).astype(BF16)
    product = dot(first, low)
    gram = (NS_A * NS_A) * gram + (2.0 * NS_A) * product + dot(product.astype(BF16), first)
    low = gram.astype(BF16)
    second = (NS_B * low.astype(F32) + NS_C * dot(low, low)).astype(BF16)
    mixed = NS_A * (first.astype(F32) + second.astype(F32)) + dot(second, first)
    main = NS_A * NS_A + jnp.sum(jnp.where(diagonal, mixed, 0.0), axis=1, keepdims=True)
    return main * inverse, (jnp.where(diagonal, 0.0, mixed) * inverse).astype(BF16)


def place_blocks(blocks, rows, x, start):
    for index, block in enumerate(blocks):
        for core in range(2):
            low = start + (2 * index + core) * rows
            x[low : low + rows] = block[core, :rows]


def near_kernel(me, kinds, *refs):
    blocks, (x, gram) = refs[:-2], refs[-2:]

    @pl.when(kinds[me[0]] == 1)
    def _():
        place_blocks(blocks, x.shape[0] // len(blocks) // 2, x, 0)
        gram[...] = outer(x[...], x[...])


def transform_kernel(gain, kv_rows, me, kinds, near, gram, *refs):
    chips = kinds.shape[0] // 2
    kv_blocks, blocks = refs[: chips // 2], refs[chips // 2 : chips]
    (x, rest, lead), outs = refs[chips : chips + 3], refs[chips + 3 :]
    half, rows = near.shape[0], blocks[0].shape[1]
    kind = kinds[me[0]]

    @pl.when(kind == 1)
    def _():
        x[:half] = near[...]
        place_blocks(blocks, rows, x, half)
        far = x[half:]
        cross = outer(near[...], far)
        raw = jnp.concatenate(
            [
                jnp.concatenate([gram[...], cross], axis=1),
                jnp.concatenate([cross.T, outer(far, far)], axis=1),
            ],
            axis=0,
        )
        main, other = transform(raw)
        lead[...] = jnp.broadcast_to(main, lead.shape)
        rest[...] = other
        high = half + 2 * rows * len(outs)
        apply_rows(gain, x, rest, lead, half, high, store_blocks(outs, rows))

    @pl.when(kind == 2)
    def _():
        size = 4 * kv_rows * len(kv_blocks)
        place_blocks(kv_blocks, 2 * kv_rows, x, 0)
        main, other = transform(outer(x[:size], x[:size]))
        lead[:size] = jnp.broadcast_to(main, (size, lead.shape[1]))
        rest[:size, :size] = other


def apply_kernel(gain, rows, kv_rows, me, kinds, x, rest, lead, *outs):
    steps = kinds.shape[0] // 4
    near, far = outs[:steps], outs[steps:]
    kind = kinds[me[0]]

    @pl.when(kind == 1)
    def _():
        apply_rows(gain, x, rest, lead, 0, x.shape[0] // 2, store_blocks(near, rows))
        low = x.shape[0] - 2 * rows * len(far)
        apply_rows(gain, x, rest, lead, low, x.shape[0], store_blocks(far, rows))

    @pl.when(kind == 2)
    def _():
        size = 4 * kv_rows * steps
        part = x.at[:size], rest.at[:size, :size], lead.at[:size]
        apply_rows(gain, *part, 0, size, store_blocks(near, 2 * kv_rows))


def near_gram(me, kinds, blocks, rows):
    width = blocks[0].shape[2]
    half = 2 * len(blocks) * rows
    vmem = pl.BlockSpec(memory_space=pltpu.VMEM)
    smem = pl.BlockSpec(memory_space=pltpu.SMEM)
    return pl.pallas_call(
        near_kernel,
        in_specs=[smem, smem] + [vmem] * len(blocks),
        out_specs=[vmem, vmem],
        out_shape=[
            jax.ShapeDtypeStruct((half, width), BF16),
            jax.ShapeDtypeStruct((half, half), F32),
        ],
        compiler_params=pltpu.CompilerParams(vmem_limit_bytes=STREAM_LIMIT),
        cost_estimate=pl.CostEstimate(
            flops=2 * half * half * width, bytes_accessed=4 * half * width, transcendentals=0
        ),
        name="near",
    )(me, kinds, *blocks)


def orthogonal_update(me, kinds, near, gram, kv_blocks, blocks, kv_rows):
    _, rows, width = blocks[0].shape
    half = near.shape[0]
    size = 2 * half
    gain = UPDATE_GAIN * math.sqrt(width)
    vmem = pl.BlockSpec(memory_space=pltpu.VMEM)
    smem = pl.BlockSpec(memory_space=pltpu.SMEM)
    like = lambda arrays: [jax.ShapeDtypeStruct(array.shape, BF16) for array in arrays]
    params = pltpu.CompilerParams(vmem_limit_bytes=VMEM_LIMIT)
    early = max(len(blocks) // 2, 1)
    x, rest, lead, *far = pl.pallas_call(
        functools.partial(transform_kernel, gain, kv_rows),
        in_specs=[smem, smem] + [vmem] * (2 + 2 * len(blocks)),
        out_specs=[vmem] * (3 + early),
        out_shape=[
            jax.ShapeDtypeStruct((size, width), BF16),
            jax.ShapeDtypeStruct((size, size), BF16),
            jax.ShapeDtypeStruct((size, 128), F32),
            *like(blocks[:early]),
        ],
        compiler_params=params,
        name="transform",
    )(me, kinds, near, gram, *kv_blocks, *blocks)
    slot = (2, max(rows, 2 * kv_rows), width)
    outs = [jax.ShapeDtypeStruct(slot, BF16)] * len(blocks) + like(blocks[early:])
    outs = pl.pallas_call(
        functools.partial(apply_kernel, gain, rows, kv_rows),
        in_specs=[smem, smem] + [vmem] * 3,
        out_specs=[vmem] * len(outs),
        out_shape=outs,
        compiler_params=params,
        name="apply",
    )(me, kinds, x, rest, lead)
    steps = len(blocks)
    return list(outs[:steps]), far + list(outs[steps:])


def gather_kernel(rows, kv_rows, me, kinds, *refs):
    if kv_rows:
        blocks, (out, kv, across) = refs[:-3], refs[-3:]
    else:
        blocks, out = refs[:-1], refs[-1]
    for index, block in enumerate(blocks):
        out[index] = block[1, :rows]
        if kv_rows:

            @pl.when(kinds[me[0] * len(blocks) + index] == 2)
            def _():
                out[len(blocks), :kv_rows] = block[1, :kv_rows]
                kv[...] = block[0, :kv_rows]
                for core in range(2):
                    across[core] = block[core, kv_rows : 2 * kv_rows]


def gather_sibling(me, table, steps, blocks, rows, kv_rows):
    width = blocks[0].shape[2]
    kinds, _ = visits(table, [2 * step for step in steps])
    vmem = pl.BlockSpec(memory_space=pltpu.VMEM)
    smem = pl.BlockSpec(memory_space=pltpu.SMEM)
    shapes = [(kv_rows, width), (2, kv_rows, width)] if kv_rows else []
    kv = [jax.ShapeDtypeStruct(shape, BF16) for shape in shapes]
    size = len(blocks) + (1 if kv_rows else 0)
    return pl.pallas_call(
        functools.partial(gather_kernel, rows, kv_rows),
        in_specs=[smem, smem] + [vmem] * len(blocks),
        out_specs=[vmem] * (1 + len(kv)),
        out_shape=[jax.ShapeDtypeStruct((size, rows, width), BF16)] + kv,
        compiler_params=pltpu.CompilerParams(vmem_limit_bytes=STREAM_LIMIT),
        name="gather",
    )(me, kinds, *blocks)


def kv_kernel(devices, me, kv, across, sibling, across_sibling, kw, ko, kb, ku):
    rows = kw.shape[1]
    mine = (me[0] >= devices // 2).astype(jnp.int32)

    def apply(index, update):
        value = kw[index] * (1.0 - RATE * DECAY) - RATE * update.astype(F32)
        ko[index] = value
        kb[index] = value.astype(BF16)
        ku[index] = update

    @pl.when(me[0] % 2 == 1)
    def _():
        apply(mine, kv[...])
        apply(1 - mine, across[0])

    @pl.when(me[0] % 2 == 0)
    def _():
        apply(mine, sibling[sibling.shape[0] - 1, :rows])
        apply(1 - mine, across_sibling[...])


def finish_kv(me, devices, sources, kw):
    vmem = pl.BlockSpec(memory_space=pltpu.VMEM)
    return pl.pallas_call(
        functools.partial(kv_kernel, devices),
        in_specs=[pl.BlockSpec(memory_space=pltpu.SMEM)] + [vmem] * 5,
        out_specs=[vmem] * 3,
        out_shape=[jax.ShapeDtypeStruct(kw.shape, kind) for kind in (F32, BF16, BF16)],
        compiler_params=pltpu.CompilerParams(vmem_limit_bytes=STREAM_LIMIT),
        name="kv",
    )(me, *sources, kw)


def finish_kernel(plan, me, kinds, held, *refs):
    own, has_sibling, has_earlier, steps, idle = plan
    owns, refs = refs[:own], list(refs[own:])
    sibling = refs.pop(0) if has_sibling else None
    ew = refs.pop(0)
    earlier, (new_ref, low_ref, update_ref) = refs[:-3], refs[-3:]
    now = pl.program_id(0)

    if has_earlier and idle:
        first = me[0] * steps
        busy = sum((kinds[first + step] == 1).astype(jnp.int32) for step in range(steps))

        @pl.when(jnp.logical_and(now == 0, busy == 0))
        def _():
            for before, after in zip(earlier, refs[-3:]):
                pltpu.sync_copy(before.at[pl.ds(held[first], 1)], after)

    def apply(update):
        value = ew[0] * (1.0 - RATE * DECAY) - RATE * update.astype(F32)
        new_ref[0] = value
        low_ref[0] = value.astype(BF16)
        update_ref[0] = update

    valid = kinds[me[0] * steps + now] == 1
    for step, block in enumerate(owns):

        @pl.when(jnp.logical_and(now == step, valid))
        def _():
            apply(block[0, : ew.shape[1]])

    if has_sibling:

        @pl.when(jnp.logical_and(now >= own, valid))
        def _():
            apply(sibling[0])


def finish(me, table, ew, owns, own_steps, sibling, sibling_steps, earlier):
    _, rows, width = ew.shape
    steps = [2 * step for step in own_steps] + [2 * step + 1 for step in sibling_steps]
    kinds, held = visits(table, steps)
    idle = not (visit_tables(table, steps)[0] == 1).any(axis=1).all()
    size, own = len(steps), len(owns)
    block = (1, rows, width)
    spec = pl.BlockSpec(block, lambda i, me, k, h: (h[me[0] * size + i], 0, 0))
    operands = [me, kinds, held, *owns]
    in_specs = [
        pl.BlockSpec((1,) + array.shape[1:], lambda i, *_: (0, 0, 0)) for array in owns
    ]
    if sibling is not None:
        last = sibling.shape[0] - 1
        in_specs.append(pl.BlockSpec(block, lambda i, *_: (jnp.clip(i - own, 0, last), 0, 0)))
        operands.append(sibling)
    in_specs.append(spec)
    operands.append(ew)
    aliases = {}
    if earlier is not None:
        aliases = {len(operands) + index: index for index in range(3)}
        in_specs += [pl.BlockSpec(memory_space=pl.ANY)] * 3
        operands += list(earlier)
    return pl.pallas_call(
        functools.partial(
            finish_kernel, (own, sibling is not None, earlier is not None, size, idle)
        ),
        grid_spec=pltpu.PrefetchScalarGridSpec(
            num_scalar_prefetch=3,
            grid=(size,),
            in_specs=in_specs,
            out_specs=[spec] * 3,
        ),
        out_shape=[jax.ShapeDtypeStruct(ew.shape, kind) for kind in (F32, BF16, BF16)],
        input_output_aliases=aliases,
        compiler_params=pltpu.CompilerParams(vmem_limit_bytes=STREAM_LIMIT),
        name="finish",
    )(*operands)


def permute(array, pairs):
    return lax.ppermute(array, "fsdp", pairs)


def together(*arrays):
    return lax.optimization_barrier(arrays)


def block_pairs(table, step, to_owners, kinds=(1,)):
    devices = table.shape[1]
    pairs = [(d ^ (2 * step), d) for d in range(devices) if table[0, d] in kinds]
    return pairs if to_owners else [(there, here) for here, there in pairs]


def cross(blocks, table, steps, to_owners):
    moved = []
    depth = max(len(blocks) // 2, 2)
    for place, (step, block) in enumerate(zip(steps, blocks)):
        if place >= depth:
            block, moved[place - depth] = together(block, moved[place - depth])
        moved.append(permute(block, block_pairs(table, step, to_owners)))
    return moved


def shards(expert_grad, expert_momentum, expert_master, kv_grad, kv_momentum, kv_master):
    devices = lax.axis_size("fsdp")
    chips, half = devices // 2, devices // 4
    me = lax.axis_index("fsdp").reshape(1)
    shape = expert_grad.shape
    rows, width = shape[2], shape[3]
    kv_rows = kv_grad.shape[1]
    flat = lambda array: array.reshape(-1, rows, width)
    eg, em, ew = flat(expert_grad), flat(expert_momentum), flat(expert_master)
    table = owner_table(eg.shape[0], kv_grad.shape[0], devices)
    count = CLIP_RATIO * math.sqrt(devices * (expert_grad.size + kv_grad.size))
    cores = [(device, device ^ 1) for device in range(devices)]
    mirrors = [(device, device ^ chips) for device in range(devices)]
    near_steps, far_steps = list(range(half)), list(range(half, chips))

    total, gv, mv = load(eg, em)
    partial, staged, keep, away = stage(me, table, total, gv, mv, kv_grad, kv_momentum)
    mirror = permute(away, mirrors)
    squares = lax.all_to_all(partial, "fsdp", 0, 0, tiled=True)
    squares, sibling, mirror = together(squares, permute(staged, cores), mirror)

    clip, *far = form_far(me, table, far_steps, squares, gv, mv, sibling, count)
    clip, far[0], keep = together(clip, far[0], keep)
    kv_sibling = permute(jnp.stack([keep, mirror]), [pair for pair in cores if pair[1] % 2])
    near, kv = form_near(
        me, table, near_steps, clip, gv, mv, sibling, kv_grad, kv_momentum, mirror, kv_sibling
    )
    far = cross(far, table, far_steps, True)
    for step in near_steps[1:]:
        near[step] = permute(near[step], block_pairs(table, step, True))
        kv[step] = permute(kv[step], block_pairs(table, step, True, (2,)))
    kinds = jnp.asarray(table[0])

    factor = clip[0, 0]
    expert_moment_out = MOMENTUM * expert_momentum + factor * expert_grad
    kv_moment_out = MOMENTUM * kv_momentum + factor * kv_grad
    near[0], expert_moment_out, kv_moment_out = together(
        near[0], expert_moment_out, kv_moment_out
    )
    near_rows, near_product = near_gram(me, kinds, near, rows)
    near, far = orthogonal_update(me, kinds, near_rows, near_product, kv, far, kv_rows)

    far = cross(far, table, far_steps, False)
    for step in near_steps[1:]:
        near[step] = permute(near[step], block_pairs(table, step, False, (1, 2)))
    near_sibling, kv, across = gather_sibling(me, table, near_steps, near, rows, kv_rows)
    near_sibling = permute(near_sibling, cores)
    across = permute(across, [pair for pair in mirrors if pair[0] % 2])
    done = finish(me, table, ew, near, near_steps, None, [], None)
    far[0], *done = together(far[0], *done)
    across_sibling = permute(across[1], [pair for pair in cores if pair[0] % 2])
    far_sibling = permute(gather_sibling(me, table, far_steps, far, rows, 0)[0], cores)
    done = finish(me, table, ew, far, far_steps, near_sibling, near_steps, done)
    across_sibling, *done = together(across_sibling, *done)
    ko, kb, ku = finish_kv(
        me, devices, (kv, across, near_sibling, across_sibling), kv_master
    )
    eo, eb, eu = finish(me, table, ew, [], [], far_sibling, far_steps, done)
    return (
        eo.reshape(shape),
        expert_moment_out,
        eb.reshape(shape),
        eu.reshape(shape),
        ko,
        kv_moment_out,
        kb,
        ku,
    )


def solution(mesh):
    expert = P("groups", None, "fsdp", None)
    kv = P("groups", "fsdp", None)
    return jax.shard_map(
        shards,
        mesh=mesh,
        in_specs=(expert, expert, expert, kv, kv, kv),
        out_specs=(expert, expert, expert, expert, kv, kv, kv, kv),
        check_vma=False,
    )
```

```python
import functools
import math

import jax
import jax.numpy as jnp
import numpy as np
from jax import lax
from jax.experimental import pallas as pl
from jax.experimental.pallas import tpu as pltpu
from jax.sharding import PartitionSpec as P

NS_A = 3.4445
NS_B = -4.775
NS_C = 2.0315
MOMENTUM = 0.95
RATE = 0.02
DECAY = 0.1
NORM_EPS = 1e-07
CLIP_EPS = 1e-06
CLIP_RATIO = 0.5
UPDATE_GAIN = 0.2

F32 = jnp.float32
BF16 = jnp.bfloat16
VMEM_LIMIT = 40 * 1024 * 1024
LOAD_LIMIT = 42 * 1024 * 1024
STREAM_LIMIT = 16 * 1024 * 1024


def owner_table(experts, kvs, devices):
    table = np.zeros((2, devices), np.int32)
    chips = devices // 2
    first = min(experts, chips)
    for index in range(first):
        table[:, 2 * (index * chips // first)] = (1, index)
    by_parity = sorted(range(chips), key=lambda chip: bin(chip).count("1") % 2)
    for index in range(first, experts):
        table[:, 2 * by_parity[index - first] + 1] = (1, index)
    for index in range(kvs):
        low = index * devices // kvs
        free = [d for d in range(low, low + devices // kvs) if d % 2 and not table[0, d]]
        table[:, free[0]] = (2, index)
    return table


def visit_tables(table, steps):
    devices = table.shape[1]
    kinds = np.zeros((devices, len(steps)), np.int32)
    held = np.zeros((devices, len(steps)), np.int32)
    for me in range(devices):
        owners = [me ^ step for step in steps]
        experts = [table[1, owner] for owner in owners if table[0, owner] == 1]
        last = experts[0] if experts else 0
        for place, owner in enumerate(owners):
            kinds[me, place] = table[0, owner]
            last = table[1, owner] if table[0, owner] == 1 else last
            held[me, place] = last
    return kinds, held


def visits(table, steps):
    return tuple(jnp.asarray(part.reshape(-1)) for part in visit_tables(table, steps))


def fold(block, rows):
    parts = block.reshape(-1, rows, block.shape[-1])
    return jnp.sum(parts * parts, axis=0)


def load_kernel(eg, em, total, gv, mv, sems):
    chunks = sems.shape[1]
    size = gv.shape[0] // chunks
    copies = [
        [
            pltpu.make_async_copy(
                source.at[pl.ds(chunk * size, size)],
                target.at[pl.ds(chunk * size, size)],
                sems.at[place, chunk],
            )
            for chunk in range(chunks)
        ]
        for place, (source, target) in enumerate(((eg, gv), (em, mv)))
    ]
    for copy in copies[0] + copies[1]:
        copy.start()
    total[...] = jnp.zeros_like(total)
    for chunk in range(chunks):
        copies[0][chunk].wait()
        total[...] += fold(gv[chunk * size : (chunk + 1) * size], total.shape[0])
    for copy in copies[1]:
        copy.wait()


def load(eg, em):
    vmem = pl.BlockSpec(memory_space=pltpu.VMEM)
    hbm = pl.BlockSpec(memory_space=pltpu.HBM)
    chunks = eg.shape[0] // 3
    total = jax.ShapeDtypeStruct((math.gcd(8, 3 * eg.shape[1]), eg.shape[2]), F32)
    return pl.pallas_call(
        load_kernel,
        in_specs=[hbm] * 2,
        out_specs=[vmem] * 3,
        out_shape=[total] + [jax.ShapeDtypeStruct(eg.shape, F32)] * 2,
        scratch_shapes=[pltpu.SemaphoreType.DMA((2, chunks))],
        compiler_params=pltpu.CompilerParams(vmem_limit_bytes=LOAD_LIMIT),
        name="load",
    )(eg, em)


def stage_kernel(devices, me, kinds, held, total, gv, mv, kg, km, partial, staged, away):
    squares = jnp.sum(total[...]) + jnp.sum(fold(kg[...], math.gcd(8, kg.shape[1])))
    partial[...] = jnp.full(partial.shape, squares, F32)
    mine = (me[0] >= devices // 2).astype(jnp.int32)
    away[0] = kg[1 - mine].astype(BF16)
    away[1] = km[1 - mine].astype(BF16)
    chips = staged.shape[1]
    for step in range(chips):
        expert = held[me[0] * chips + step]
        staged[0, step] = gv[expert].astype(BF16)
        staged[1, step] = mv[expert].astype(BF16)

        @pl.when(kinds[me[0] * chips + step] == 2)
        def _():
            staged[0, step, : kg.shape[1]] = kg[mine].astype(BF16)
            staged[1, step, : kg.shape[1]] = km[mine].astype(BF16)


def stage(me, table, total, gv, mv, kg, km):
    _, rows, width = gv.shape
    devices = table.shape[1]
    chips = devices // 2
    kinds, held = visits(table, [2 * step + 1 for step in range(chips)])
    vmem = pl.BlockSpec(memory_space=pltpu.VMEM)
    smem = pl.BlockSpec(memory_space=pltpu.SMEM)
    return pl.pallas_call(
        functools.partial(stage_kernel, devices),
        in_specs=[smem] * 3 + [vmem] * 5,
        out_specs=[vmem] * 3,
        out_shape=[
            jax.ShapeDtypeStruct((devices, 8, 128), F32),
            jax.ShapeDtypeStruct((2, chips, rows, width), BF16),
            jax.ShapeDtypeStruct((2,) + kg.shape[1:], BF16),
        ],
        compiler_params=pltpu.CompilerParams(vmem_limit_bytes=STREAM_LIMIT),
        name="stage",
    )(me, kinds, held, total, gv, mv, kg, km)


def nesterov(scale, grad, moment):
    clipped = scale * grad.astype(F32)
    return (clipped + MOMENTUM * (MOMENTUM * moment.astype(F32) + clipped)).astype(BF16)


def form_far_kernel(count, start, me, kinds, index, squares, gv, mv, sib, clip, *outs):
    total = jnp.sum(squares[...], axis=0)
    factor = jnp.minimum(1.0, count / (jnp.sqrt(total) + CLIP_EPS))
    scale = factor[0:1, 0:1]
    clip[...] = scale
    for step, out in enumerate(outs):
        place = me[0] * len(outs) + step

        @pl.when(kinds[place] == 1)
        def _():
            out[0] = nesterov(scale, gv[index[place]], mv[index[place]])
            out[1] = nesterov(scale, sib[0, start + step], sib[1, start + step])


def form_near_kernel(me, kinds, index, clip, gv, mv, sib, kg, km, mirror, mirror_sib, *outs):
    scale = clip[...]
    steps, kv_rows = len(outs) // 2, kg.shape[1]
    mine = (me[0] >= kinds.shape[0] // steps // 2).astype(jnp.int32)
    for step, (out, kv) in enumerate(zip(outs[:steps], outs[steps:])):
        place = me[0] * steps + step

        @pl.when(kinds[place] == 1)
        def _():
            out[0] = nesterov(scale, gv[index[place]], mv[index[place]])
            out[1] = nesterov(scale, sib[0, step], sib[1, step])

        @pl.when(kinds[place] == 2)
        def _():
            kv[0, :kv_rows] = nesterov(scale, kg[mine], km[mine])
            kv[0, kv_rows:] = nesterov(scale, mirror[0], mirror[1])
            kv[1, :kv_rows] = nesterov(scale, sib[0, step, :kv_rows], sib[1, step, :kv_rows])
            kv[1, kv_rows:] = nesterov(scale, mirror_sib[0], mirror_sib[1])


def form_call(kernel, name, table, chip_steps, me, operands, outs):
    kinds, index = visits(table, [2 * step for step in chip_steps])
    vmem = pl.BlockSpec(memory_space=pltpu.VMEM)
    smem = pl.BlockSpec(memory_space=pltpu.SMEM)
    return pl.pallas_call(
        kernel,
        in_specs=[smem] * 3 + [vmem] * len(operands),
        out_specs=[vmem] * len(outs),
        out_shape=outs,
        compiler_params=pltpu.CompilerParams(vmem_limit_bytes=STREAM_LIMIT),
        name=name,
    )(me, kinds, index, *operands)


def form_far(me, table, steps, squares, gv, mv, sib, count):
    block = jax.ShapeDtypeStruct((2,) + gv.shape[1:], BF16)
    clip = jax.ShapeDtypeStruct((1, 1), F32)
    kernel = functools.partial(form_far_kernel, count, steps[0])
    return form_call(
        kernel, "far", table, steps, me, (squares, gv, mv, sib), [clip] + [block] * len(steps)
    )


def form_near(me, table, steps, clip, gv, mv, sib, kg, km, mirror, mirror_sib):
    _, rows, width = gv.shape
    shapes = [(2, rows, width)] * len(steps) + [(2, 2 * kg.shape[1], width)] * len(steps)
    outs = [jax.ShapeDtypeStruct(shape, BF16) for shape in shapes]
    operands = (clip, gv, mv, sib, kg, km, mirror, mirror_sib)
    blocks = form_call(form_near_kernel, "form", table, steps, me, operands, outs)
    return list(blocks[: len(steps)]), list(blocks[len(steps) :])


def dot(left, right):
    return jnp.dot(left, right, preferred_element_type=F32)


def apply_rows(gain, x, rest, lead, low, high, store):
    width = x.shape[1]
    chunk = 512 if width % 512 == 0 else width
    for start in range(0, width, chunk):
        part = x[low:high, start : start + chunk].astype(F32)
        value = lead[low:high, 0:1] * part + dot(rest[low:high], x[:, start : start + chunk])
        value = (gain * value.astype(BF16).astype(F32)).astype(BF16)
        store(start, chunk, value)


def store_blocks(outs, rows):
    def store(start, chunk, value):
        for index, out in enumerate(outs):
            for core in range(2):
                low = (2 * index + core) * rows
                out[core, :rows, start : start + chunk] = value[low : low + rows]

    return store


def outer(left, right):
    return lax.dot_general(left, right, (((1,), (1,)), ((), ())), preferred_element_type=F32)


def transform(raw):
    size = raw.shape[0]
    row = lax.broadcasted_iota(jnp.int32, (size, size), 0)
    col = lax.broadcasted_iota(jnp.int32, (size, size), 1)
    diagonal = row == col
    norm = jnp.sqrt(jnp.sum(jnp.where(diagonal, raw, 0.0), keepdims=True))
    inverse = 1.0 / (norm + NORM_EPS)
    gram = raw * inverse * inverse
    low = gram.astype(BF16)
    first = (NS_B * low.astype(F32) + NS_C * dot(low, low)).astype(BF16)
    product = dot(first, low)
    gram = (NS_A * NS_A) * gram + (2.0 * NS_A) * product + dot(product.astype(BF16), first)
    low = gram.astype(BF16)
    second = (NS_B * low.astype(F32) + NS_C * dot(low, low)).astype(BF16)
    mixed = NS_A * (first.astype(F32) + second.astype(F32)) + dot(second, first)
    main = NS_A * NS_A + jnp.sum(jnp.where(diagonal, mixed, 0.0), axis=1, keepdims=True)
    return main * inverse, (jnp.where(diagonal, 0.0, mixed) * inverse).astype(BF16)


def place_blocks(blocks, rows, x, start):
    for index, block in enumerate(blocks):
        for core in range(2):
            low = start + (2 * index + core) * rows
            x[low : low + rows] = block[core, :rows]


def near_kernel(me, kinds, *refs):
    blocks, (x, gram) = refs[:-2], refs[-2:]

    @pl.when(kinds[me[0]] == 1)
    def _():
        place_blocks(blocks, x.shape[0] // len(blocks) // 2, x, 0)
        gram[...] = outer(x[...], x[...])


def transform_kernel(gain, kv_rows, me, kinds, near, gram, *refs):
    chips = kinds.shape[0] // 2
    kv_blocks, blocks = refs[: chips // 2], refs[chips // 2 : chips]
    (x, rest, lead), outs = refs[chips : chips + 3], refs[chips + 3 :]
    half, rows = near.shape[0], blocks[0].shape[1]
    kind = kinds[me[0]]

    @pl.when(kind == 1)
    def _():
        x[:half] = near[...]
        place_blocks(blocks, rows, x, half)
        far = x[half:]
        cross = outer(near[...], far)
        raw = jnp.concatenate(
            [
                jnp.concatenate([gram[...], cross], axis=1),
                jnp.concatenate([cross.T, outer(far, far)], axis=1),
            ],
            axis=0,
        )
        main, other = transform(raw)
        lead[...] = jnp.broadcast_to(main, lead.shape)
        rest[...] = other
        high = half + 2 * rows * len(outs)
        apply_rows(gain, x, rest, lead, half, high, store_blocks(outs, rows))

    @pl.when(kind == 2)
    def _():
        size = 4 * kv_rows * len(kv_blocks)
        place_blocks(kv_blocks, 2 * kv_rows, x, 0)
        main, other = transform(outer(x[:size], x[:size]))
        lead[:size] = jnp.broadcast_to(main, (size, lead.shape[1]))
        rest[:size, :size] = other


def apply_kernel(gain, rows, kv_rows, me, kinds, x, rest, lead, *outs):
    steps = kinds.shape[0] // 4
    near, far = outs[:steps], outs[steps:]
    kind = kinds[me[0]]

    @pl.when(kind == 1)
    def _():
        apply_rows(gain, x, rest, lead, 0, x.shape[0] // 2, store_blocks(near, rows))
        low = x.shape[0] - 2 * rows * len(far)
        apply_rows(gain, x, rest, lead, low, x.shape[0], store_blocks(far, rows))

    @pl.when(kind == 2)
    def _():
        size = 4 * kv_rows * steps
        part = x.at[:size], rest.at[:size, :size], lead.at[:size]
        apply_rows(gain, *part, 0, size, store_blocks(near, 2 * kv_rows))


def near_gram(me, kinds, blocks, rows):
    width = blocks[0].shape[2]
    half = 2 * len(blocks) * rows
    vmem = pl.BlockSpec(memory_space=pltpu.VMEM)
    smem = pl.BlockSpec(memory_space=pltpu.SMEM)
    return pl.pallas_call(
        near_kernel,
        in_specs=[smem, smem] + [vmem] * len(blocks),
        out_specs=[vmem, vmem],
        out_shape=[
            jax.ShapeDtypeStruct((half, width), BF16),
            jax.ShapeDtypeStruct((half, half), F32),
        ],
        compiler_params=pltpu.CompilerParams(vmem_limit_bytes=STREAM_LIMIT),
        cost_estimate=pl.CostEstimate(
            flops=2 * half * half * width, bytes_accessed=4 * half * width, transcendentals=0
        ),
        name="near",
    )(me, kinds, *blocks)


def orthogonal_update(me, kinds, near, gram, kv_blocks, blocks, kv_rows):
    _, rows, width = blocks[0].shape
    half = near.shape[0]
    size = 2 * half
    gain = UPDATE_GAIN * math.sqrt(width)
    vmem = pl.BlockSpec(memory_space=pltpu.VMEM)
    smem = pl.BlockSpec(memory_space=pltpu.SMEM)
    like = lambda arrays: [jax.ShapeDtypeStruct(array.shape, BF16) for array in arrays]
    params = pltpu.CompilerParams(vmem_limit_bytes=VMEM_LIMIT)
    early = max(len(blocks) // 2, 1)
    x, rest, lead, *far = pl.pallas_call(
        functools.partial(transform_kernel, gain, kv_rows),
        in_specs=[smem, smem] + [vmem] * (2 + 2 * len(blocks)),
        out_specs=[vmem] * (3 + early),
        out_shape=[
            jax.ShapeDtypeStruct((size, width), BF16),
            jax.ShapeDtypeStruct((size, size), BF16),
            jax.ShapeDtypeStruct((size, 128), F32),
            *like(blocks[:early]),
        ],
        compiler_params=params,
        name="transform",
    )(me, kinds, near, gram, *kv_blocks, *blocks)
    slot = (2, max(rows, 2 * kv_rows), width)
    outs = [jax.ShapeDtypeStruct(slot, BF16)] * len(blocks) + like(blocks[early:])
    outs = pl.pallas_call(
        functools.partial(apply_kernel, gain, rows, kv_rows),
        in_specs=[smem, smem] + [vmem] * 3,
        out_specs=[vmem] * len(outs),
        out_shape=outs,
        compiler_params=params,
        name="apply",
    )(me, kinds, x, rest, lead)
    steps = len(blocks)
    return list(outs[:steps]), far + list(outs[steps:])


def gather_kernel(rows, kv_rows, me, kinds, *refs):
    if kv_rows:
        blocks, (out, kv, across) = refs[:-3], refs[-3:]
    else:
        blocks, out = refs[:-1], refs[-1]
    for index, block in enumerate(blocks):
        out[index] = block[1, :rows]
        if kv_rows:

            @pl.when(kinds[me[0] * len(blocks) + index] == 2)
            def _():
                out[len(blocks), :kv_rows] = block[1, :kv_rows]
                kv[...] = block[0, :kv_rows]
                for core in range(2):
                    across[core] = block[core, kv_rows : 2 * kv_rows]


def gather_sibling(me, table, steps, blocks, rows, kv_rows):
    width = blocks[0].shape[2]
    kinds, _ = visits(table, [2 * step for step in steps])
    vmem = pl.BlockSpec(memory_space=pltpu.VMEM)
    smem = pl.BlockSpec(memory_space=pltpu.SMEM)
    shapes = [(kv_rows, width), (2, kv_rows, width)] if kv_rows else []
    kv = [jax.ShapeDtypeStruct(shape, BF16) for shape in shapes]
    size = len(blocks) + (1 if kv_rows else 0)
    return pl.pallas_call(
        functools.partial(gather_kernel, rows, kv_rows),
        in_specs=[smem, smem] + [vmem] * len(blocks),
        out_specs=[vmem] * (1 + len(kv)),
        out_shape=[jax.ShapeDtypeStruct((size, rows, width), BF16)] + kv,
        compiler_params=pltpu.CompilerParams(vmem_limit_bytes=STREAM_LIMIT),
        name="gather",
    )(me, kinds, *blocks)


def kv_kernel(devices, me, kv, across, sibling, across_sibling, kw, ko, kb, ku):
    rows = kw.shape[1]
    mine = (me[0] >= devices // 2).astype(jnp.int32)

    def apply(index, update):
        value = kw[index] * (1.0 - RATE * DECAY) - RATE * update.astype(F32)
        ko[index] = value
        kb[index] = value.astype(BF16)
        ku[index] = update

    @pl.when(me[0] % 2 == 1)
    def _():
        apply(mine, kv[...])
        apply(1 - mine, across[0])

    @pl.when(me[0] % 2 == 0)
    def _():
        apply(mine, sibling[sibling.shape[0] - 1, :rows])
        apply(1 - mine, across_sibling[...])


def finish_kv(me, devices, sources, kw):
    vmem = pl.BlockSpec(memory_space=pltpu.VMEM)
    return pl.pallas_call(
        functools.partial(kv_kernel, devices),
        in_specs=[pl.BlockSpec(memory_space=pltpu.SMEM)] + [vmem] * 5,
        out_specs=[vmem] * 3,
        out_shape=[jax.ShapeDtypeStruct(kw.shape, kind) for kind in (F32, BF16, BF16)],
        compiler_params=pltpu.CompilerParams(vmem_limit_bytes=STREAM_LIMIT),
        name="kv",
    )(me, *sources, kw)


def finish_kernel(plan, me, kinds, held, *refs):
    own, has_sibling, has_earlier, steps, idle = plan
    owns, refs = refs[:own], list(refs[own:])
    sibling = refs.pop(0) if has_sibling else None
    ew = refs.pop(0)
    earlier, (new_ref, low_ref, update_ref) = refs[:-3], refs[-3:]
    now = pl.program_id(0)

    if has_earlier and idle:
        first = me[0] * steps
        busy = sum((kinds[first + step] == 1).astype(jnp.int32) for step in range(steps))

        @pl.when(jnp.logical_and(now == 0, busy == 0))
        def _():
            for before, after in zip(earlier, refs[-3:]):
                pltpu.sync_copy(before.at[pl.ds(held[first], 1)], after)

    def apply(update):
        value = ew[0] * (1.0 - RATE * DECAY) - RATE * update.astype(F32)
        new_ref[0] = value
        low_ref[0] = value.astype(BF16)
        update_ref[0] = update

    valid = kinds[me[0] * steps + now] == 1
    for step, block in enumerate(owns):

        @pl.when(jnp.logical_and(now == step, valid))
        def _():
            apply(block[0, : ew.shape[1]])

    if has_sibling:

        @pl.when(jnp.logical_and(now >= own, valid))
        def _():
            apply(sibling[0])


def finish(me, table, ew, owns, own_steps, sibling, sibling_steps, earlier):
    _, rows, width = ew.shape
    steps = [2 * step for step in own_steps] + [2 * step + 1 for step in sibling_steps]
    kinds, held = visits(table, steps)
    idle = not (visit_tables(table, steps)[0] == 1).any(axis=1).all()
    size, own = len(steps), len(owns)
    block = (1, rows, width)
    spec = pl.BlockSpec(block, lambda i, me, k, h: (h[me[0] * size + i], 0, 0))
    operands = [me, kinds, held, *owns]
    in_specs = [
        pl.BlockSpec((1,) + array.shape[1:], lambda i, *_: (0, 0, 0)) for array in owns
    ]
    if sibling is not None:
        last = sibling.shape[0] - 1
        in_specs.append(pl.BlockSpec(block, lambda i, *_: (jnp.clip(i - own, 0, last), 0, 0)))
        operands.append(sibling)
    in_specs.append(spec)
    operands.append(ew)
    aliases = {}
    if earlier is not None:
        aliases = {len(operands) + index: index for index in range(3)}
        in_specs += [pl.BlockSpec(memory_space=pl.ANY)] * 3
        operands += list(earlier)
    return pl.pallas_call(
        functools.partial(
            finish_kernel, (own, sibling is not None, earlier is not None, size, idle)
        ),
        grid_spec=pltpu.PrefetchScalarGridSpec(
            num_scalar_prefetch=3,
            grid=(size,),
            in_specs=in_specs,
            out_specs=[spec] * 3,
        ),
        out_shape=[jax.ShapeDtypeStruct(ew.shape, kind) for kind in (F32, BF16, BF16)],
        input_output_aliases=aliases,
        compiler_params=pltpu.CompilerParams(vmem_limit_bytes=STREAM_LIMIT),
        name="finish",
    )(*operands)


def permute(array, pairs):
    return lax.ppermute(array, "fsdp", pairs)


def together(*arrays):
    return lax.optimization_barrier(arrays)


def block_pairs(table, step, to_owners, kinds=(1,)):
    devices = table.shape[1]
    pairs = [(d ^ (2 * step), d) for d in range(devices) if table[0, d] in kinds]
    return pairs if to_owners else [(there, here) for here, there in pairs]


def cross(blocks, table, steps, to_owners):
    moved = []
    depth = max(len(blocks) // 2, 2)
    for place, (step, block) in enumerate(zip(steps, blocks)):
        if place >= depth:
            block, moved[place - depth] = together(block, moved[place - depth])
        moved.append(permute(block, block_pairs(table, step, to_owners)))
    return moved


def shards(expert_grad, expert_momentum, expert_master, kv_grad, kv_momentum, kv_master):
    devices = lax.axis_size("fsdp")
    chips, half = devices // 2, devices // 4
    me = lax.axis_index("fsdp").reshape(1)
    shape = expert_grad.shape
    rows, width = shape[2], shape[3]
    kv_rows = kv_grad.shape[1]
    flat = lambda array: array.reshape(-1, rows, width)
    eg, em, ew = flat(expert_grad), flat(expert_momentum), flat(expert_master)
    table = owner_table(eg.shape[0], kv_grad.shape[0], devices)
    count = CLIP_RATIO * math.sqrt(devices * (expert_grad.size + kv_grad.size))
    cores = [(device, device ^ 1) for device in range(devices)]
    mirrors = [(device, device ^ chips) for device in range(devices)]
    near_steps, far_steps = list(range(half)), list(range(half, chips))

    total, gv, mv = load(eg, em)
    partial, staged, away = stage(me, table, total, gv, mv, kv_grad, kv_momentum)
    mirror = permute(away, [pair for pair in mirrors if pair[0] % 2])
    mirror_sib = permute(away, [(here, there ^ 1) for here, there in mirrors if here % 2 == 0])
    squares = lax.all_to_all(partial, "fsdp", 0, 0, tiled=True)
    squares, sibling, mirror, mirror_sib = together(
        squares, permute(staged, cores), mirror, mirror_sib
    )

    clip, *far = form_far(me, table, far_steps, squares, gv, mv, sibling, count)
    clip, far[0] = together(clip, far[0])
    near, kv = form_near(
        me, table, near_steps, clip, gv, mv, sibling, kv_grad, kv_momentum, mirror, mirror_sib
    )
    far = cross(far, table, far_steps, True)
    for step in near_steps[1:]:
        near[step] = permute(near[step], block_pairs(table, step, True))
        kv[step], near[step] = together(kv[step], near[step])
        kv[step] = permute(kv[step], block_pairs(table, step, True, (2,)))
    kinds = jnp.asarray(table[0])

    factor = clip[0, 0]
    expert_moment_out = MOMENTUM * expert_momentum + factor * expert_grad
    kv_moment_out = MOMENTUM * kv_momentum + factor * kv_grad
    near[0], expert_moment_out, kv_moment_out = together(
        near[0], expert_moment_out, kv_moment_out
    )
    near_rows, near_product = near_gram(me, kinds, near, rows)
    near, far = orthogonal_update(me, kinds, near_rows, near_product, kv, far, kv_rows)

    far = cross(far, table, far_steps, False)
    for step in near_steps[1:]:
        near[step] = permute(near[step], block_pairs(table, step, False, (1, 2)))
    near_sibling, kv, across = gather_sibling(me, table, near_steps, near, rows, kv_rows)
    near_sibling = permute(near_sibling, cores)
    across = permute(across, [pair for pair in mirrors if pair[0] % 2])
    done = finish(me, table, ew, near, near_steps, None, [], None)
    far[0], *done = together(far[0], *done)
    across_sibling = permute(across[1], [pair for pair in cores if pair[0] % 2])
    far_sibling = permute(gather_sibling(me, table, far_steps, far, rows, 0)[0], cores)
    done = finish(me, table, ew, far, far_steps, near_sibling, near_steps, done)
    across_sibling, *done = together(across_sibling, *done)
    ko, kb, ku = finish_kv(
        me, devices, (kv, across, near_sibling, across_sibling), kv_master
    )
    eo, eb, eu = finish(me, table, ew, [], [], far_sibling, far_steps, done)
    return (
        eo.reshape(shape),
        expert_moment_out,
        eb.reshape(shape),
        eu.reshape(shape),
        ko,
        kv_moment_out,
        kb,
        ku,
    )


def solution(mesh):
    expert = P("groups", None, "fsdp", None)
    kv = P("groups", "fsdp", None)
    return jax.shard_map(
        shards,
        mesh=mesh,
        in_specs=(expert, expert, expert, kv, kv, kv),
        out_specs=(expert, expert, expert, expert, kv, kv, kv, kv),
        check_vma=False,
    )
```

```python
import functools
import math

import jax
import jax.numpy as jnp
import numpy as np
from jax import lax
from jax.experimental import pallas as pl
from jax.experimental.pallas import tpu as pltpu
from jax.sharding import PartitionSpec as P

NS_A = 3.4445
NS_B = -4.775
NS_C = 2.0315
MOMENTUM = 0.95
RATE = 0.02
DECAY = 0.1
NORM_EPS = 1e-07
CLIP_EPS = 1e-06
CLIP_RATIO = 0.5
UPDATE_GAIN = 0.2

F32 = jnp.float32
BF16 = jnp.bfloat16
VMEM_LIMIT = 40 * 1024 * 1024
LOAD_LIMIT = 42 * 1024 * 1024
STREAM_LIMIT = 16 * 1024 * 1024


def owner_table(experts, kvs, devices):
    table = np.zeros((2, devices), np.int32)
    chips = devices // 2
    first = min(experts, chips)
    for index in range(first):
        table[:, 2 * (index * chips // first)] = (1, index)
    by_parity = sorted(range(chips), key=lambda chip: bin(chip).count("1") % 2)
    for index in range(first, experts):
        table[:, 2 * by_parity[index - first] + 1] = (1, index)
    for index in range(kvs):
        low = index * devices // kvs
        free = [d for d in range(low, low + devices // kvs) if d % 2 and not table[0, d]]
        table[:, free[0]] = (2, index)
    return table


def visit_tables(table, steps):
    devices = table.shape[1]
    kinds = np.zeros((devices, len(steps)), np.int32)
    held = np.zeros((devices, len(steps)), np.int32)
    for me in range(devices):
        owners = [me ^ step for step in steps]
        experts = [table[1, owner] for owner in owners if table[0, owner] == 1]
        last = experts[0] if experts else 0
        for place, owner in enumerate(owners):
            kinds[me, place] = table[0, owner]
            last = table[1, owner] if table[0, owner] == 1 else last
            held[me, place] = last
    return kinds, held


def visits(table, steps):
    return tuple(jnp.asarray(part.reshape(-1)) for part in visit_tables(table, steps))


def fold(block, rows):
    parts = block.reshape(-1, rows, block.shape[-1])
    return jnp.sum(parts * parts, axis=0)


def load_kernel(eg, em, total, gv, mv, sems):
    chunks = sems.shape[1]
    size = gv.shape[0] // chunks
    copies = [
        [
            pltpu.make_async_copy(
                source.at[pl.ds(chunk * size, size)],
                target.at[pl.ds(chunk * size, size)],
                sems.at[place, chunk],
            )
            for chunk in range(chunks)
        ]
        for place, (source, target) in enumerate(((eg, gv), (em, mv)))
    ]
    for copy in copies[0] + copies[1]:
        copy.start()
    total[...] = jnp.zeros_like(total)
    for chunk in range(chunks):
        copies[0][chunk].wait()
        total[...] += fold(gv[chunk * size : (chunk + 1) * size], total.shape[0])
    for copy in copies[1]:
        copy.wait()


def load(eg, em):
    vmem = pl.BlockSpec(memory_space=pltpu.VMEM)
    hbm = pl.BlockSpec(memory_space=pltpu.HBM)
    chunks = eg.shape[0] // 3
    total = jax.ShapeDtypeStruct((math.gcd(8, 3 * eg.shape[1]), eg.shape[2]), F32)
    return pl.pallas_call(
        load_kernel,
        in_specs=[hbm] * 2,
        out_specs=[vmem] * 3,
        out_shape=[total] + [jax.ShapeDtypeStruct(eg.shape, F32)] * 2,
        scratch_shapes=[pltpu.SemaphoreType.DMA((2, chunks))],
        compiler_params=pltpu.CompilerParams(vmem_limit_bytes=LOAD_LIMIT),
        name="load",
    )(eg, em)


def stage_kernel(devices, me, held, total, gv, mv, kg, km, partial, staged, keep, away):
    squares = jnp.sum(total[...]) + jnp.sum(fold(kg[...], math.gcd(8, kg.shape[1])))
    partial[...] = jnp.full(partial.shape, squares, F32)
    mine = (me[0] >= devices // 2).astype(jnp.int32)
    for out, index in ((keep, mine), (away, 1 - mine)):
        out[0] = kg[index].astype(BF16)
        out[1] = km[index].astype(BF16)
    chips = staged.shape[1]
    for step in range(chips):
        expert = held[me[0] * chips + step]
        staged[0, step] = gv[expert].astype(BF16)
        staged[1, step] = mv[expert].astype(BF16)


def stage(me, table, total, gv, mv, kg, km):
    _, rows, width = gv.shape
    devices = table.shape[1]
    chips = devices // 2
    _, held = visits(table, [2 * step + 1 for step in range(chips)])
    vmem = pl.BlockSpec(memory_space=pltpu.VMEM)
    smem = pl.BlockSpec(memory_space=pltpu.SMEM)
    kv = jax.ShapeDtypeStruct((2,) + kg.shape[1:], BF16)
    return pl.pallas_call(
        functools.partial(stage_kernel, devices),
        in_specs=[smem] * 2 + [vmem] * 5,
        out_specs=[vmem] * 4,
        out_shape=[
            jax.ShapeDtypeStruct((devices, 8, 128), F32),
            jax.ShapeDtypeStruct((2, chips, rows, width), BF16),
            kv,
            kv,
        ],
        compiler_params=pltpu.CompilerParams(vmem_limit_bytes=STREAM_LIMIT),
        name="stage",
    )(me, held, total, gv, mv, kg, km)


def nesterov(scale, grad, moment):
    clipped = scale * grad.astype(F32)
    return (clipped + MOMENTUM * (MOMENTUM * moment.astype(F32) + clipped)).astype(BF16)


def form_far_kernel(count, start, me, kinds, index, squares, gv, mv, sib, clip, *outs):
    total = jnp.sum(squares[...], axis=0)
    factor = jnp.minimum(1.0, count / (jnp.sqrt(total) + CLIP_EPS))
    clip[...] = factor
    scale = factor[0:1, 0:1]
    for step, out in enumerate(outs):
        place = me[0] * len(outs) + step

        @pl.when(kinds[place] == 1)
        def _():
            out[0] = nesterov(scale, gv[index[place]], mv[index[place]])
            out[1] = nesterov(scale, sib[0, start + step], sib[1, start + step])


def form_near_kernel(me, kinds, index, clip, gv, mv, sib, kg, km, mirror, kv_sib, *outs):
    scale = clip[0:1, 0:1]
    steps, kv_rows = len(outs) // 2, kg.shape[1]
    mine = (me[0] >= kinds.shape[0] // steps // 2).astype(jnp.int32)
    for step, (out, kv) in enumerate(zip(outs[:steps], outs[steps:])):
        place = me[0] * steps + step

        @pl.when(kinds[place] == 1)
        def _():
            out[0] = nesterov(scale, gv[index[place]], mv[index[place]])
            out[1] = nesterov(scale, sib[0, step], sib[1, step])

        @pl.when(kinds[place] == 2)
        def _():
            kv[0, :kv_rows] = nesterov(scale, kg[mine], km[mine])
            kv[0, kv_rows:] = nesterov(scale, mirror[0], mirror[1])
            kv[1, :kv_rows] = nesterov(scale, kv_sib[0, 0], kv_sib[0, 1])
            kv[1, kv_rows:] = nesterov(scale, kv_sib[1, 0], kv_sib[1, 1])


def form_call(kernel, name, table, chip_steps, me, operands, outs):
    kinds, index = visits(table, [2 * step for step in chip_steps])
    vmem = pl.BlockSpec(memory_space=pltpu.VMEM)
    smem = pl.BlockSpec(memory_space=pltpu.SMEM)
    return pl.pallas_call(
        kernel,
        in_specs=[smem] * 3 + [vmem] * len(operands),
        out_specs=[vmem] * len(outs),
        out_shape=outs,
        compiler_params=pltpu.CompilerParams(vmem_limit_bytes=STREAM_LIMIT),
        name=name,
    )(me, kinds, index, *operands)


def form_far(me, table, steps, squares, gv, mv, sib, count):
    block = jax.ShapeDtypeStruct((2,) + gv.shape[1:], BF16)
    clip = jax.ShapeDtypeStruct((8, 128), F32)
    kernel = functools.partial(form_far_kernel, count, steps[0])
    return form_call(
        kernel, "far", table, steps, me, (squares, gv, mv, sib), [clip] + [block] * len(steps)
    )


def form_near(me, table, steps, clip, gv, mv, sib, kg, km, mirror, kv_sib):
    _, rows, width = gv.shape
    shapes = [(2, rows, width)] * len(steps) + [(2, 2 * kg.shape[1], width)] * len(steps)
    outs = [jax.ShapeDtypeStruct(shape, BF16) for shape in shapes]
    operands = (clip, gv, mv, sib, kg, km, mirror, kv_sib)
    blocks = form_call(form_near_kernel, "form", table, steps, me, operands, outs)
    return list(blocks[: len(steps)]), list(blocks[len(steps) :])


def dot(left, right):
    return jnp.dot(left, right, preferred_element_type=F32)


def apply_rows(gain, x, rest, lead, low, high, store):
    width = x.shape[1]
    chunk = 512 if width % 512 == 0 else width
    for start in range(0, width, chunk):
        part = x[low:high, start : start + chunk].astype(F32)
        value = lead[low:high, 0:1] * part + dot(rest[low:high], x[:, start : start + chunk])
        value = (gain * value.astype(BF16).astype(F32)).astype(BF16)
        store(start, chunk, value)


def store_blocks(outs, rows):
    def store(start, chunk, value):
        for index, out in enumerate(outs):
            for core in range(2):
                low = (2 * index + core) * rows
                out[core, :rows, start : start + chunk] = value[low : low + rows]

    return store


def outer(left, right):
    return lax.dot_general(left, right, (((1,), (1,)), ((), ())), preferred_element_type=F32)


def transform(raw):
    size = raw.shape[0]
    row = lax.broadcasted_iota(jnp.int32, (size, size), 0)
    col = lax.broadcasted_iota(jnp.int32, (size, size), 1)
    diagonal = row == col
    norm = jnp.sqrt(jnp.sum(jnp.where(diagonal, raw, 0.0), keepdims=True))
    inverse = 1.0 / (norm + NORM_EPS)
    gram = raw * inverse * inverse
    low = gram.astype(BF16)
    first = (NS_B * low.astype(F32) + NS_C * dot(low, low)).astype(BF16)
    product = dot(first, low)
    gram = (NS_A * NS_A) * gram + (2.0 * NS_A) * product + dot(product.astype(BF16), first)
    low = gram.astype(BF16)
    second = (NS_B * low.astype(F32) + NS_C * dot(low, low)).astype(BF16)
    mixed = NS_A * (first.astype(F32) + second.astype(F32)) + dot(second, first)
    main = NS_A * NS_A + jnp.sum(jnp.where(diagonal, mixed, 0.0), axis=1, keepdims=True)
    return main * inverse, (jnp.where(diagonal, 0.0, mixed) * inverse).astype(BF16)


def place_blocks(blocks, rows, x, start):
    for index, block in enumerate(blocks):
        for core in range(2):
            low = start + (2 * index + core) * rows
            x[low : low + rows] = block[core, :rows]


def near_kernel(me, kinds, *refs):
    blocks, (x, gram) = refs[:-2], refs[-2:]

    @pl.when(kinds[me[0]] == 1)
    def _():
        place_blocks(blocks, x.shape[0] // len(blocks) // 2, x, 0)
        gram[...] = outer(x[...], x[...])


def transform_kernel(gain, kv_rows, me, kinds, near, gram, *refs):
    chips = kinds.shape[0] // 2
    kv_blocks, blocks = refs[: chips // 2], refs[chips // 2 : chips]
    (x, rest, lead), outs = refs[chips : chips + 3], refs[chips + 3 :]
    half, rows = near.shape[0], blocks[0].shape[1]
    kind = kinds[me[0]]

    @pl.when(kind == 1)
    def _():
        x[:half] = near[...]
        place_blocks(blocks, rows, x, half)
        far = x[half:]
        cross = outer(near[...], far)
        raw = jnp.concatenate(
            [
                jnp.concatenate([gram[...], cross], axis=1),
                jnp.concatenate([cross.T, outer(far, far)], axis=1),
            ],
            axis=0,
        )
        main, other = transform(raw)
        lead[...] = jnp.broadcast_to(main, lead.shape)
        rest[...] = other
        high = half + 2 * rows * len(outs)
        apply_rows(gain, x, rest, lead, half, high, store_blocks(outs, rows))

    @pl.when(kind == 2)
    def _():
        size = 4 * kv_rows * len(kv_blocks)
        place_blocks(kv_blocks, 2 * kv_rows, x, 0)
        main, other = transform(outer(x[:size], x[:size]))
        lead[:size] = jnp.broadcast_to(main, (size, lead.shape[1]))
        rest[:size, :size] = other


def apply_kernel(gain, rows, kv_rows, me, kinds, x, rest, lead, *outs):
    steps = kinds.shape[0] // 4
    near, far = outs[:steps], outs[steps:]
    kind = kinds[me[0]]

    @pl.when(kind == 1)
    def _():
        apply_rows(gain, x, rest, lead, 0, x.shape[0] // 2, store_blocks(near, rows))
        low = x.shape[0] - 2 * rows * len(far)
        apply_rows(gain, x, rest, lead, low, x.shape[0], store_blocks(far, rows))

    @pl.when(kind == 2)
    def _():
        size = 4 * kv_rows * steps
        part = x.at[:size], rest.at[:size, :size], lead.at[:size]
        apply_rows(gain, *part, 0, size, store_blocks(near, 2 * kv_rows))


def near_gram(me, kinds, blocks, rows):
    width = blocks[0].shape[2]
    half = 2 * len(blocks) * rows
    vmem = pl.BlockSpec(memory_space=pltpu.VMEM)
    smem = pl.BlockSpec(memory_space=pltpu.SMEM)
    return pl.pallas_call(
        near_kernel,
        in_specs=[smem, smem] + [vmem] * len(blocks),
        out_specs=[vmem, vmem],
        out_shape=[
            jax.ShapeDtypeStruct((half, width), BF16),
            jax.ShapeDtypeStruct((half, half), F32),
        ],
        compiler_params=pltpu.CompilerParams(vmem_limit_bytes=STREAM_LIMIT),
        cost_estimate=pl.CostEstimate(
            flops=2 * half * half * width, bytes_accessed=4 * half * width, transcendentals=0
        ),
        name="near",
    )(me, kinds, *blocks)


def orthogonal_update(me, kinds, near, gram, kv_blocks, blocks, kv_rows):
    _, rows, width = blocks[0].shape
    half = near.shape[0]
    size = 2 * half
    gain = UPDATE_GAIN * math.sqrt(width)
    vmem = pl.BlockSpec(memory_space=pltpu.VMEM)
    smem = pl.BlockSpec(memory_space=pltpu.SMEM)
    like = lambda arrays: [jax.ShapeDtypeStruct(array.shape, BF16) for array in arrays]
    params = pltpu.CompilerParams(vmem_limit_bytes=VMEM_LIMIT)
    early = max(len(blocks) // 2, 1)
    x, rest, lead, *far = pl.pallas_call(
        functools.partial(transform_kernel, gain, kv_rows),
        in_specs=[smem, smem] + [vmem] * (2 + 2 * len(blocks)),
        out_specs=[vmem] * (3 + early),
        out_shape=[
            jax.ShapeDtypeStruct((size, width), BF16),
            jax.ShapeDtypeStruct((size, size), BF16),
            jax.ShapeDtypeStruct((size, 128), F32),
            *like(blocks[:early]),
        ],
        compiler_params=params,
        name="transform",
    )(me, kinds, near, gram, *kv_blocks, *blocks)
    slot = (2, max(rows, 2 * kv_rows), width)
    outs = [jax.ShapeDtypeStruct(slot, BF16)] * len(blocks) + like(blocks[early:])
    outs = pl.pallas_call(
        functools.partial(apply_kernel, gain, rows, kv_rows),
        in_specs=[smem, smem] + [vmem] * 3,
        out_specs=[vmem] * len(outs),
        out_shape=outs,
        compiler_params=params,
        name="apply",
    )(me, kinds, x, rest, lead)
    steps = len(blocks)
    return list(outs[:steps]), far + list(outs[steps:])


def gather_kernel(rows, kv_rows, me, kinds, *refs):
    if kv_rows:
        blocks, (out, kv, across) = refs[:-3], refs[-3:]
    else:
        blocks, out = refs[:-1], refs[-1]
    for index, block in enumerate(blocks):
        out[index] = block[1, :rows]
        if kv_rows:

            @pl.when(kinds[me[0] * len(blocks) + index] == 2)
            def _():
                out[len(blocks), :kv_rows] = block[1, :kv_rows]
                kv[...] = block[0, :kv_rows]
                for core in range(2):
                    across[core] = block[core, kv_rows : 2 * kv_rows]


def gather_sibling(me, table, steps, blocks, rows, kv_rows):
    width = blocks[0].shape[2]
    kinds, _ = visits(table, [2 * step for step in steps])
    vmem = pl.BlockSpec(memory_space=pltpu.VMEM)
    smem = pl.BlockSpec(memory_space=pltpu.SMEM)
    shapes = [(kv_rows, width), (2, kv_rows, width)] if kv_rows else []
    kv = [jax.ShapeDtypeStruct(shape, BF16) for shape in shapes]
    size = len(blocks) + (1 if kv_rows else 0)
    return pl.pallas_call(
        functools.partial(gather_kernel, rows, kv_rows),
        in_specs=[smem, smem] + [vmem] * len(blocks),
        out_specs=[vmem] * (1 + len(kv)),
        out_shape=[jax.ShapeDtypeStruct((size, rows, width), BF16)] + kv,
        compiler_params=pltpu.CompilerParams(vmem_limit_bytes=STREAM_LIMIT),
        name="gather",
    )(me, kinds, *blocks)


def kv_kernel(devices, me, kv, across, sibling, across_sibling, kw, ko, kb, ku):
    rows = kw.shape[1]
    mine = (me[0] >= devices // 2).astype(jnp.int32)

    def apply(index, update):
        value = kw[index] * (1.0 - RATE * DECAY) - RATE * update.astype(F32)
        ko[index] = value
        kb[index] = value.astype(BF16)
        ku[index] = update

    @pl.when(me[0] % 2 == 1)
    def _():
        apply(mine, kv[...])
        apply(1 - mine, across[0])

    @pl.when(me[0] % 2 == 0)
    def _():
        apply(mine, sibling[sibling.shape[0] - 1, :rows])
        apply(1 - mine, across_sibling[...])


def finish_kv(me, devices, sources, kw):
    vmem = pl.BlockSpec(memory_space=pltpu.VMEM)
    return pl.pallas_call(
        functools.partial(kv_kernel, devices),
        in_specs=[pl.BlockSpec(memory_space=pltpu.SMEM)] + [vmem] * 5,
        out_specs=[vmem] * 3,
        out_shape=[jax.ShapeDtypeStruct(kw.shape, kind) for kind in (F32, BF16, BF16)],
        compiler_params=pltpu.CompilerParams(vmem_limit_bytes=STREAM_LIMIT),
        name="kv",
    )(me, *sources, kw)


def finish_kernel(plan, me, kinds, held, *refs):
    own, has_sibling, has_earlier, steps, idle = plan
    owns, refs = refs[:own], list(refs[own:])
    sibling = refs.pop(0) if has_sibling else None
    ew = refs.pop(0)
    earlier, (new_ref, low_ref, update_ref) = refs[:-3], refs[-3:]
    now = pl.program_id(0)

    if has_earlier and idle:
        first = me[0] * steps
        busy = sum((kinds[first + step] == 1).astype(jnp.int32) for step in range(steps))

        @pl.when(jnp.logical_and(now == 0, busy == 0))
        def _():
            for before, after in zip(earlier, refs[-3:]):
                pltpu.sync_copy(before.at[pl.ds(held[first], 1)], after)

    def apply(update):
        value = ew[0] * (1.0 - RATE * DECAY) - RATE * update.astype(F32)
        new_ref[0] = value
        low_ref[0] = value.astype(BF16)
        update_ref[0] = update

    valid = kinds[me[0] * steps + now] == 1
    for step, block in enumerate(owns):

        @pl.when(jnp.logical_and(now == step, valid))
        def _():
            apply(block[0, : ew.shape[1]])

    if has_sibling:

        @pl.when(jnp.logical_and(now >= own, valid))
        def _():
            apply(sibling[0])


def finish(me, table, ew, owns, own_steps, sibling, sibling_steps, earlier):
    _, rows, width = ew.shape
    steps = [2 * step for step in own_steps] + [2 * step + 1 for step in sibling_steps]
    kinds, held = visits(table, steps)
    idle = not (visit_tables(table, steps)[0] == 1).any(axis=1).all()
    size, own = len(steps), len(owns)
    block = (1, rows, width)
    spec = pl.BlockSpec(block, lambda i, me, k, h: (h[me[0] * size + i], 0, 0))
    operands = [me, kinds, held, *owns]
    in_specs = [
        pl.BlockSpec((1,) + array.shape[1:], lambda i, *_: (0, 0, 0)) for array in owns
    ]
    if sibling is not None:
        last = sibling.shape[0] - 1
        in_specs.append(pl.BlockSpec(block, lambda i, *_: (jnp.clip(i - own, 0, last), 0, 0)))
        operands.append(sibling)
    in_specs.append(spec)
    operands.append(ew)
    aliases = {}
    if earlier is not None:
        aliases = {len(operands) + index: index for index in range(3)}
        in_specs += [pl.BlockSpec(memory_space=pl.ANY)] * 3
        operands += list(earlier)
    return pl.pallas_call(
        functools.partial(
            finish_kernel, (own, sibling is not None, earlier is not None, size, idle)
        ),
        grid_spec=pltpu.PrefetchScalarGridSpec(
            num_scalar_prefetch=3,
            grid=(size,),
            in_specs=in_specs,
            out_specs=[spec] * 3,
        ),
        out_shape=[jax.ShapeDtypeStruct(ew.shape, kind) for kind in (F32, BF16, BF16)],
        input_output_aliases=aliases,
        compiler_params=pltpu.CompilerParams(vmem_limit_bytes=STREAM_LIMIT),
        name="finish",
    )(*operands)


def permute(array, pairs):
    return lax.ppermute(array, "fsdp", pairs)


def together(*arrays):
    return lax.optimization_barrier(arrays)


def block_pairs(table, step, to_owners, kinds=(1,)):
    devices = table.shape[1]
    pairs = [(d ^ (2 * step), d) for d in range(devices) if table[0, d] in kinds]
    return pairs if to_owners else [(there, here) for here, there in pairs]


def cross(blocks, table, steps, to_owners):
    moved = []
    depth = max(len(blocks) // 2, 2)
    for place, (step, block) in enumerate(zip(steps, blocks)):
        if place >= depth:
            block, moved[place - depth] = together(block, moved[place - depth])
        moved.append(permute(block, block_pairs(table, step, to_owners)))
    return moved


def shards(expert_grad, expert_momentum, expert_master, kv_grad, kv_momentum, kv_master):
    devices = lax.axis_size("fsdp")
    chips, half = devices // 2, devices // 4
    me = lax.axis_index("fsdp").reshape(1)
    shape = expert_grad.shape
    rows, width = shape[2], shape[3]
    kv_rows = kv_grad.shape[1]
    flat = lambda array: array.reshape(-1, rows, width)
    eg, em, ew = flat(expert_grad), flat(expert_momentum), flat(expert_master)
    table = owner_table(eg.shape[0], kv_grad.shape[0], devices)
    count = CLIP_RATIO * math.sqrt(devices * (expert_grad.size + kv_grad.size))
    cores = [(device, device ^ 1) for device in range(devices)]
    mirrors = [(device, device ^ chips) for device in range(devices)]
    near_steps, far_steps = list(range(half)), list(range(half, chips))

    total, gv, mv = load(eg, em)
    partial, staged, keep, away = stage(me, table, total, gv, mv, kv_grad, kv_momentum)
    mirror = permute(away, mirrors)
    squares = lax.all_to_all(partial, "fsdp", 0, 0, tiled=True)
    squares, sibling, mirror = together(squares, permute(staged, cores), mirror)

    clip, *far = form_far(me, table, far_steps, squares, gv, mv, sibling, count)
    clip, far[0], keep = together(clip, far[0], keep)
    kv_sibling = permute(jnp.stack([keep, mirror]), [pair for pair in cores if pair[1] % 2])
    near, kv = form_near(
        me, table, near_steps, clip, gv, mv, sibling, kv_grad, kv_momentum, mirror, kv_sibling
    )
    far = cross(far, table, far_steps, True)
    for step in near_steps[1:]:
        near[step] = permute(near[step], block_pairs(table, step, True))
        kv[step], near[step] = together(kv[step], near[step])
        kv[step] = permute(kv[step], block_pairs(table, step, True, (2,)))
    kinds = jnp.asarray(table[0])

    factor = clip[0, 0]
    expert_moment_out = MOMENTUM * expert_momentum + factor * expert_grad
    kv_moment_out = MOMENTUM * kv_momentum + factor * kv_grad
    near[0], expert_moment_out, kv_moment_out = together(
        near[0], expert_moment_out, kv_moment_out
    )
    near_rows, near_product = near_gram(me, kinds, near, rows)
    near, far = orthogonal_update(me, kinds, near_rows, near_product, kv, far, kv_rows)

    far = cross(far, table, far_steps, False)
    for step in near_steps[1:]:
        near[step] = permute(near[step], block_pairs(table, step, False, (1, 2)))
    near_sibling, kv, across = gather_sibling(me, table, near_steps, near, rows, kv_rows)
    near_sibling = permute(near_sibling, cores)
    across = permute(across, [pair for pair in mirrors if pair[0] % 2])
    done = finish(me, table, ew, near, near_steps, None, [], None)
    far[0], *done = together(far[0], *done)
    across_sibling = permute(across[1], [pair for pair in cores if pair[0] % 2])
    far_sibling = permute(gather_sibling(me, table, far_steps, far, rows, 0)[0], cores)
    done = finish(me, table, ew, far, far_steps, near_sibling, near_steps, done)
    across_sibling, *done = together(across_sibling, *done)
    ko, kb, ku = finish_kv(
        me, devices, (kv, across, near_sibling, across_sibling), kv_master
    )
    eo, eb, eu = finish(me, table, ew, [], [], far_sibling, far_steps, done)
    return (
        eo.reshape(shape),
        expert_moment_out,
        eb.reshape(shape),
        eu.reshape(shape),
        ko,
        kv_moment_out,
        kb,
        ku,
    )


def solution(mesh):
    expert = P("groups", None, "fsdp", None)
    kv = P("groups", "fsdp", None)
    return jax.shard_map(
        shards,
        mesh=mesh,
        in_specs=(expert, expert, expert, kv, kv, kv),
        out_specs=(expert, expert, expert, expert, kv, kv, kv, kv),
        check_vma=False,
    )
```
